256 devices in a mesh: grp: 32 (over x, y, z_lo), mem: 8 (over z_hi, core).
Axes of the slice: x: 4, y: 4, z: 8 (z_hi: 4, z_lo: 2; z = z_hi * 2 + z_lo), core: 2. Of those that a mesh axis runs over, the one named last changes fastest.
Arguments:
- embeddings: float32 [98304, 256], P(('grp', 'mem')), may hold values from -30 to 30
- positive: int32 [98304], P(('grp', 'mem')), may hold values from 0 to 98303, as said below
- pairing: int32 [2, 32], replicated, may hold values from 0 to 31, as said below
Outputs:
- loss: float32 [98304], P(('grp', 'mem'))
- grad_embed: float32 [98304, 256], P(('grp', 'mem'))
The draws below stay inside these ranges and needn't reach their ends.
Inputs may be any that keep to these rules, and one draw needn't show every extreme that they name: positive[i] lies in the same block of 3072 views as i, differs from i, and positive[positive[i]] = i. Each row is a pairing of the 32 blocks into partners (pairing[r, pairing[r, b]] = b, never b itself); no two blocks are partners in two rounds.
All inputs are finite; a program needn't handle non-finite values.
Results may differ from the reference program's by a relative error of at most 0.0003.
Values sent between devices are 32-bit elements; how exact they have to be, the bound alone decides.
No kernel may reach another device: no remote copies, remote signals or barrier semaphores. Data moves between devices by JAX's collectives and lax.ppermute only.
A program may use at most 128 MiB of HBM per device.

```python
import jax
import jax.numpy as jnp
from jax import lax

W = 256
ROUNDS = 2
GROUPS = 32
BLOCK = 3072
VIEWS = 98304


def pair_views(key):
    keys = jax.random.split(key, GROUPS)
    perms = jax.vmap(lambda one_key: jax.random.permutation(one_key, BLOCK))(keys).astype(jnp.int32)
    firsts = perms[:, 0::2]
    seconds = perms[:, 1::2]
    lines = jnp.arange(GROUPS, dtype=jnp.int32)[:, None]
    local = jnp.zeros((GROUPS, BLOCK), jnp.int32)
    local = local.at[lines, firsts].set(seconds)
    local = local.at[lines, seconds].set(firsts)
    return (local + lines * BLOCK).reshape(VIEWS)


def draw_positive(key, part):
    shared = pair_views(key)
    return shared


def draw_embeddings(key, part):
    partner = pair_views(key)
    key = jax.random.fold_in(key, 2)
    keys = jax.random.split(key, 4)
    leader = jnp.minimum(jnp.arange(VIEWS, dtype=jnp.int32), partner)
    labels = jax.random.randint(keys[0], (VIEWS,), 0, 64)[leader]
    centres = jax.random.normal(keys[1], (64, W), jnp.float32)
    images = jax.random.normal(keys[2], (VIEWS, W), jnp.float32)[leader]
    noise = jax.random.normal(keys[3], (VIEWS, W), jnp.float32)
    values = 0.7 * centres[labels] + 0.5 * images + 0.6 * noise
    return jnp.clip(values, -30.0, 30.0)


def draw_pairing(key, part):
    key = jax.random.fold_in(key, 3)
    relabel = jax.random.permutation(key, GROUPS).astype(jnp.int32)
    count = GROUPS
    turns = jnp.arange(ROUNDS, dtype=jnp.int32)[:, None]
    places = jnp.arange(count // 2, dtype=jnp.int32)[None, :]
    first = (turns + places) % (count - 1)
    second = (turns - places) % (count - 1)
    second = jnp.where(places == 0, count - 1, second)
    lines = jnp.broadcast_to(turns, first.shape)
    table = jnp.zeros((ROUNDS, count), jnp.int32)
    table = table.at[lines, relabel[first]].set(relabel[second])
    table = table.at[lines, relabel[second]].set(relabel[first])
    return table


def setup_inputs(seed: int = 0) -> dict:
    seeds = jax.random.split(jax.random.key(seed), 4)
    return {
        "embeddings": draw_embeddings(jax.random.fold_in(seeds[3], 71), 0),
        "positive": draw_positive(jax.random.fold_in(seeds[3], 71), 0),
        "pairing": draw_pairing(jax.random.fold_in(seeds[3], 71), 0),
    }


logit_divisor = 0.1
epsilon = 1e-06

def unit_rows(values):
    radius = jnp.sqrt(lax.optimization_barrier(jnp.sum(values * values, axis=-1, keepdims=True)) + epsilon)
    return (values / radius, radius)

def expos(row_data, col_data):
    cosine_logits = jnp.dot(row_data, col_data.T, precision=lax.Precision.HIGHEST, preferred_element_type=jnp.float32)
    return jnp.exp(cosine_logits / logit_divisor)

def reference(embeddings, positive, pairing):
    sphere_embedding_matrix, radius = unit_rows(embeddings)
    blocks = sphere_embedding_matrix.reshape(GROUPS, BLOCK, W)
    ident = jnp.arange(BLOCK, dtype=jnp.int32)
    diagonal = ident[:, None] == ident[None, :]

    def denoms(group):
        row_data = blocks[group]
        total = lax.optimization_barrier(jnp.sum(jnp.where(diagonal, 0.0, expos(row_data, row_data)), axis=1))
        for which_round in range(ROUNDS):
            total = total + lax.optimization_barrier(jnp.sum(expos(row_data, blocks[pairing[which_round, group]]), axis=1))
        return total
    dens = lax.map(denoms, jnp.arange(GROUPS, dtype=jnp.int32))

    def grads(group):
        row_data = blocks[group]
        inverse = 1.0 / dens[group]
        weight = jnp.where(diagonal, 0.0, expos(row_data, row_data)) * (inverse[:, None] + inverse[None, :])
        running_aggregate = jnp.dot(weight, row_data, precision=lax.Precision.HIGHEST, preferred_element_type=jnp.float32)
        for which_round in range(ROUNDS):
            other = pairing[which_round, group]
            weight = expos(row_data, blocks[other]) * (inverse[:, None] + (1.0 / dens[other])[None, :])
            running_aggregate = running_aggregate + jnp.dot(weight, blocks[other], precision=lax.Precision.HIGHEST, preferred_element_type=jnp.float32)
        return running_aggregate
    running_aggregate = lax.map(grads, jnp.arange(GROUPS, dtype=jnp.int32)).reshape(VIEWS, W)
    rival_entries = sphere_embedding_matrix[positive]
    matched_logit = lax.optimization_barrier(jnp.sum(sphere_embedding_matrix * rival_entries, axis=-1)) / logit_divisor
    loss = jnp.log(dens.reshape(VIEWS)) - matched_logit
    sphere_derivative = (running_aggregate - 2.0 * rival_entries) / logit_divisor
    grad_embed = (sphere_derivative - sphere_embedding_matrix * lax.optimization_barrier(jnp.sum(sphere_embedding_matrix * sphere_derivative, axis=-1, keepdims=True))) / radius
    return (loss, grad_embed)
```

```python
import functools

import jax
import jax.numpy as jnp
from jax import lax
from jax.experimental import pallas as pl
from jax.experimental.pallas import tpu as pltpu
from jax.sharding import PartitionSpec as P

LOGIT_DIVISOR = 0.1
EPSILON = 1e-06
SLICE = 384
WIDTH = 256
SELF = 2
VMEM = 16 * 1024 * 1024
VMEM_LARGE = 40 * 1024 * 1024
HBM = pl.BlockSpec(memory_space=pltpu.HBM)
SMEM = pl.BlockSpec(memory_space=pltpu.SMEM)


def split(values):
    hi = values.astype(jnp.bfloat16)
    lo = (values - hi.astype(jnp.float32)).astype(jnp.bfloat16)
    return hi, lo


def rows_of(tiles):
    pairs = tiles.reshape(tiles.shape[0] // 2, 2, 8, 128)
    rows = tiles.shape[0] * 4
    return jnp.concatenate([pairs[:, 0].reshape(rows, 128), pairs[:, 1].reshape(rows, 128)], axis=1)


def radius_of(values):
    return jnp.sqrt(jnp.sum(values * values, axis=-1, keepdims=True) + EPSILON)


def as_column(line):
    return jnp.broadcast_to(line, (128, line.shape[1])).T


def in_hbm(value):
    return pltpu.with_memory_space_constraint(value, pltpu.HBM)


def params(limit=VMEM):
    return pltpu.CompilerParams(vmem_limit_bytes=limit)


def tile_kernel(emb_ref, tile_ref):
    rows = emb_ref.shape[0]
    for half in range(2):
        tile_ref[:, half] = emb_ref[:, half * 128 : half * 128 + 128].reshape(rows // 8, 8, 128)


def as_tiles(embeddings):
    rows, _ = embeddings.shape
    return pl.pallas_call(
        tile_kernel,
        out_shape=jax.ShapeDtypeStruct((rows // 8, 2, 8, 128), jnp.float32),
        compiler_params=params(),
        name="as_tiles",
    )(embeddings)


def forward_kernel(first, order, pieces, *refs):
    rows, refs = refs[:pieces], list(refs[pieces:])
    if first:
        sib, got, got_sib = refs[:3]
        refs = refs[3:]
    else:
        c_in = refs.pop(0)
    pos_ref, e_out, refs = refs[0], refs[1], refs[2:]
    if first:
        c_out = refs.pop(0)
    line_refs, (left_ref, e_buf, c_buf, tot_ref, e_sem, c_sem) = refs[:-6], refs[-6:]
    slices, _, count = e_buf.shape
    height, wide = slices * SLICE, 2 * SLICE

    copies, col_copies = [], []
    for base in range(0, count, wide):
        view, sem = (pl.ds(base, wide),), c_sem.at[base // wide]
        if first:
            col_copies.append(pltpu.make_async_copy(c_buf.at[view], c_out.at[view], sem))
        else:
            col_copies.append(pltpu.make_async_copy(c_in.at[view], c_buf.at[view], sem))
            col_copies[-1].start()
    at = 0
    for ref in rows:
        values = ref[...]
        hi, lo = split(values * (1.0 / (radius_of(values) * LOGIT_DIVISOR)))
        left_ref[at : at + hi.shape[0]] = jnp.concatenate([hi, lo, hi], axis=1)
        at += hi.shape[0]

    for base in range(0, count, wide):
        if first:
            half = got.shape[1] // 2
            tiles = got.shape[0] * half // 8
            for which, ref in enumerate((rows[0], sib) if base == 0 else (got, got_sib)):
                if base == 0:
                    piece = ref[...]
                else:
                    begin = (base // wide - 1) * half
                    piece = rows_of(ref[:, begin : begin + half].reshape(tiles, 8, 128))
                hi, lo = split(piece * (1.0 / radius_of(piece)))
                c_buf[base + which * SLICE : base + which * SLICE + SLICE] = jnp.concatenate([hi, lo], axis=1)
            col_copies[base // wide].start()
        else:
            col_copies[base // wide].wait()
        col = c_buf[base : base + wide]
        hi, lo = col[:, :WIDTH], col[:, WIDTH:]
        scores = lax.dot_general(
            left_ref[...],
            jnp.concatenate([hi, hi, lo], axis=1),
            (((1,), (1,)), ((), ())),
            preferred_element_type=jnp.float32,
        )
        total = jnp.zeros((height, 128), jnp.float32) if base == 0 else tot_ref[0]
        if base == 0:
            match = jnp.zeros((height, 128), jnp.float32)
            row_ids = lax.broadcasted_iota(jnp.int32, (height, 128), 0) + order * SLICE
            lane_ids = lax.broadcasted_iota(jnp.int32, (height, 128), 1)
        for k in range(0, wide, 128):
            score = scores[:, k : k + 128]
            e = jnp.exp(score)
            if base == 0:
                match = match + jnp.where(row_ids == pos_ref[:, k : k + 128], score, 0.0)
                if order == SELF and k < SLICE:
                    e = jnp.where(row_ids - SELF * SLICE == lane_ids + k, 0.0, e)
            total = total + e
            e_buf[:, :, base + k : base + k + 128] = e.reshape(slices, SLICE, 128)
        tot_ref[0] = total
        if base == 0:
            tot_ref[1] = match
        view = (slice(None), slice(None), pl.ds(base, wide))
        copies.append(pltpu.make_async_copy(e_buf.at[view], e_out.at[view], e_sem.at[base // wide]))
        copies[-1].start()

    for kind in range(2):
        line = jnp.sum(tot_ref[kind].T, axis=0, keepdims=True)
        for which, ref in enumerate(line_refs):
            ref[kind : kind + 1] = line[:, which * SLICE : which * SLICE + SLICE]
    for copy in copies + (col_copies if first else []):
        copy.wait()


def forward(order, slices, rows, cols, pos):
    height, count = slices * SLICE, 6 * SLICE
    first = len(cols) > 1
    split_shape = pltpu.HBM((count, 2 * WIDTH), jnp.bfloat16)
    line_shape = jax.ShapeDtypeStruct((2, SLICE), jnp.float32)
    return pl.pallas_call(
        functools.partial(forward_kernel, first, order, len(rows)),
        in_specs=[pl.BlockSpec()] * len(rows)
        + ([pl.BlockSpec()] * len(cols) if first else [HBM])
        + [pl.BlockSpec()],
        out_specs=[HBM] * (1 + first) + [pl.BlockSpec()] * slices,
        out_shape=[pltpu.HBM((slices, SLICE, count), jnp.float32)]
        + [split_shape] * first
        + [line_shape] * slices,
        scratch_shapes=[
            pltpu.VMEM((height, 3 * WIDTH), jnp.bfloat16),
            pltpu.VMEM((slices, SLICE, count), jnp.float32),
            pltpu.VMEM((count, 2 * WIDTH), jnp.bfloat16),
            pltpu.VMEM((2, height, 128), jnp.float32),
            pltpu.SemaphoreType.DMA((3,)),
            pltpu.SemaphoreType.DMA((3,)),
        ],
        cost_estimate=pl.CostEstimate(
            flops=6 * height * count * WIDTH, bytes_accessed=4 * height * count, transcendentals=height * count
        ),
        compiler_params=params(VMEM_LARGE),
        name="forward_%d" % order,
    )(*rows, *(cols if first else map(in_hbm, cols)), pos)


def sum_kernel(a_ref, b_ref, c_ref, d_ref, out_ref):
    out_ref[...] = (a_ref[...] + b_ref[...]) + (c_ref[...] + d_ref[...])


def sum_lines(*lines):
    return pl.pallas_call(
        sum_kernel,
        out_shape=jax.ShapeDtypeStruct(lines[0].shape, jnp.float32),
        compiler_params=params(),
        name="sum_lines",
    )(*lines)


def spread_kernel(own_ref, sib_ref, out_ref):
    both = jnp.concatenate([own_ref[0:1], sib_ref[0:1]], axis=1)
    out_ref[...] = jnp.broadcast_to(both.reshape(1, 1, 2 * SLICE), out_ref.shape)


def spread(own, sib, groups):
    return pl.pallas_call(
        spread_kernel,
        out_shape=jax.ShapeDtypeStruct((groups, 1, 2 * SLICE), jnp.float32),
        compiler_params=params(),
        name="spread",
    )(own, sib)


def backward_kernel(order, row_refs, partner_ref, *refs):
    rows_den, refs = refs[:row_refs], refs[row_refs:]
    own_ref, sib_ref, everyone_ref, pos_ref, e_in, c_in = refs[:6]
    refs = refs[6:]
    out_refs, (run_ref, e_buf, c_buf, e_sem, c_sem) = refs[:-5], refs[-5:]
    slices = e_buf.shape[0]
    wide = 2 * SLICE
    copies = []
    for k in range(3):
        wanted = pl.ds(k * wide, wide)
        copies.append(
            pltpu.make_async_copy(
                e_in.at[:, :, wanted], e_buf.at[:, :, wanted], e_sem.at[k]
            )
        )
        copies.append(pltpu.make_async_copy(c_in.at[wanted], c_buf.at[wanted], c_sem.at[k]))
    for copy in copies:
        copy.start()

    rows = slices * SLICE
    row_inv = 1.0 / as_column(jnp.concatenate([ref[0:1] for ref in rows_den], axis=1))
    row_ids = lax.broadcasted_iota(jnp.int32, (rows, 128), 0) + order * SLICE
    for k in range(3):
        if k == 0:
            col_inv = 1.0 / jnp.concatenate([own_ref[0:1], sib_ref[0:1]], axis=1)
        else:
            col_inv = 1.0 / everyone_ref[partner_ref[k - 1]]
        copies[2 * k].wait()
        copies[2 * k + 1].wait()
        his, los = [], []
        for at in range(0, wide, 128):
            e = e_buf[:, :, k * wide + at : k * wide + at + 128].reshape(rows, 128)
            weight = e * (row_inv + col_inv[:, at : at + 128])
            if k == 0:
                weight = weight - jnp.where(row_ids == pos_ref[:, at : at + 128], 2.0, 0.0)
            hi, lo = split(weight)
            his.append(hi)
            los.append(lo)
        cols = c_buf[k * wide : k * wide + wide]
        c_hi, c_lo = cols[:, :WIDTH], cols[:, WIDTH:]
        part = jnp.dot(
            jnp.concatenate(his + his + los, axis=1),
            jnp.concatenate([c_hi, c_lo, c_hi], axis=0),
            preferred_element_type=jnp.float32,
        )
        if k == 0:
            run_ref[...] = part
        elif k == 1:
            run_ref[...] += part
        else:
            part = run_ref[...] + part
            size = rows // len(out_refs)
            for which, ref in enumerate(out_refs):
                ref[...] = part[which * size : which * size + size]


def backward(order, pieces, row_dens, e, partners, own, sib, everyone, pos, cols):
    slices = len(row_dens)
    count = 6 * SLICE
    return pl.pallas_call(
        functools.partial(backward_kernel, order, slices),
        in_specs=[SMEM] + [pl.BlockSpec()] * (slices + 4) + [HBM] * 2,
        out_shape=[jax.ShapeDtypeStruct((slices * SLICE // pieces, WIDTH), jnp.float32)] * pieces,
        scratch_shapes=[
            pltpu.VMEM((slices * SLICE, WIDTH), jnp.float32),
            pltpu.VMEM((slices, SLICE, count), jnp.float32),
            pltpu.VMEM((count, 2 * WIDTH), jnp.bfloat16),
            pltpu.SemaphoreType.DMA((3,)),
            pltpu.SemaphoreType.DMA((3,)),
        ],
        cost_estimate=pl.CostEstimate(
            flops=6 * slices * SLICE * count * WIDTH, bytes_accessed=4 * slices * SLICE * count, transcendentals=0
        ),
        compiler_params=params(VMEM_LARGE),
        name="backward_%d" % order,
    )(partners, *row_dens, own, sib, everyone, pos, in_hbm(e), in_hbm(cols))


def add_kernel(a_ref, b_ref, c_ref, d_ref, ab_ref, cd_ref):
    ab_ref[...] = a_ref[...] + b_ref[...]
    cd_ref[...] = c_ref[...] + d_ref[...]


def add_pairs(a, b, c, d):
    out = jax.ShapeDtypeStruct(a.shape, jnp.float32)
    return pl.pallas_call(add_kernel, out_shape=(out, out), compiler_params=params(), name="add_pairs")(
        a, b, c, d
    )


def finish_kernel(emb_ref, run_ref, low0, low1, high0, high1, line_ref, loss_ref, grad_ref):
    values = emb_ref[...]
    radius = radius_of(values)
    unit = values / radius
    low, high = low0[...] + low1[...], high0[...] + high1[...]
    slope = (run_ref[...] + jnp.concatenate([low, high], axis=0)) / LOGIT_DIVISOR
    grad_ref[...] = (slope - unit * jnp.sum(unit * slope, axis=-1, keepdims=True)) / radius
    loss_ref[...] = jnp.log(line_ref[0:1]) - line_ref[1:2]


def finish(embeddings, run, lows, highs, line):
    rows, width = embeddings.shape
    return pl.pallas_call(
        finish_kernel,
        out_shape=(
            jax.ShapeDtypeStruct((1, rows), jnp.float32),
            jax.ShapeDtypeStruct((rows, width), jnp.float32),
        ),
        compiler_params=params(),
        name="finish",
    )(embeddings, run, *lows, *highs, line)


def local(embeddings, positive, pairing):
    rows, width = embeddings.shape
    members = lax.axis_size("mem")
    groups = lax.axis_size("grp")
    block = rows * members
    rounds = pairing.shape[0]
    group = lax.axis_index("grp")
    member = lax.axis_index("mem")
    half = rows // 2

    def shift(value, by):
        return lax.ppermute(value, "mem", [(m, (m + by) % members) for m in range(members)])

    def swap(value):
        return lax.ppermute(value, "mem", [(m, m ^ 1) for m in range(members)])

    per = rows * width // (groups * 128)
    pieces = lax.all_to_all(as_tiles(embeddings).reshape(groups, per, 128), "grp", 0, 0, tiled=True)
    picked = pieces[pairing.T].reshape(groups, rounds * per, 128)
    got = lax.all_to_all(picked, "grp", 0, 0, tiled=True)
    left, right = shift(embeddings, 2), shift(embeddings, -2)
    sib, pos_sib = swap(embeddings), swap(positive)
    got, left, right, sib, pos_sib = lax.optimization_barrier((got, left, right, sib, pos_sib))
    far = (shift(left[:half], 2), shift(right[half:], -2))

    both = jnp.concatenate([positive, pos_sib]) - group * block
    owner = both // rows
    turn = (owner // 2 - member // 2) % (members // 2)
    order = jnp.where(turn == 0, SELF, jnp.where(turn == 3, 0, jnp.where(turn == 1, 1, 3)))
    pos = jnp.where(owner % 2 == member % 2, order * rows + both % rows, -1).reshape(1, 2 * rows)

    e_self, cols, line_self = forward(SELF, 1, (embeddings,), (sib, got, swap(got)), pos)
    e_sides, line_left, line_right = forward(0, 2, (left, right), (cols,), pos)
    e_far, line_far = forward(3, 1, far, (cols,), pos)

    line = sum_lines(line_self, shift(line_left, -2), shift(line_right, 2), shift(line_far, 4))
    line_sib = swap(line)
    everyone = lax.all_to_all(spread(line, line_sib, groups), "grp", 0, 0, tiled=True)
    at_left, at_right, at_far = shift(line, 2), shift(line, -2), shift(line, 4)

    shared = (pairing[:, group], line, line_sib, everyone, pos, cols)
    far_low, far_high = backward(3, 2, (at_far,), e_far, *shared)
    far_low, far_high = shift(far_low, 2), shift(far_high, -2)
    left_low, left_high, right_low, right_high = backward(0, 4, (at_left, at_right), e_sides, *shared)
    high0, low1 = shift(right_high, 2), shift(left_low, -2)
    right_low, left_high = add_pairs(right_low, far_low, left_high, far_high)
    low0, high1 = shift(right_low, 2), shift(left_high, -2)
    (run,) = backward(SELF, 1, (line,), e_self, *shared)
    loss, grad = finish(embeddings, run, (low0, low1), (high0, high1), line)
    return loss.reshape(rows), grad


def solution(mesh):
    placed = (P(("grp", "mem"), None), P(("grp", "mem")), P())
    return jax.shard_map(
        local,
        mesh=mesh,
        in_specs=placed,
        out_specs=(P(("grp", "mem")), P(("grp", "mem"), None)),
        check_vma=False,
    )
```

```python
import functools

import jax
import jax.numpy as jnp
from jax import lax
from jax.experimental import pallas as pl
from jax.experimental.pallas import tpu as pltpu
from jax.sharding import PartitionSpec as P

LOGIT_DIVISOR = 0.1
EPSILON = 1e-06
SLICE = 384
WIDTH = 256
SELF = 2
VMEM = 16 * 1024 * 1024
VMEM_LARGE = 44 * 1024 * 1024
HBM = pl.BlockSpec(memory_space=pltpu.HBM)
SMEM = pl.BlockSpec(memory_space=pltpu.SMEM)


def split(values):
    hi = values.astype(jnp.bfloat16)
    lo = (values - hi.astype(jnp.float32)).astype(jnp.bfloat16)
    return hi, lo


def rows_of(tiles):
    pairs = tiles.reshape(tiles.shape[0] // 2, 2, 8, 128)
    rows = tiles.shape[0] * 4
    return jnp.concatenate([pairs[:, 0].reshape(rows, 128), pairs[:, 1].reshape(rows, 128)], axis=1)


def radius_of(values):
    return jnp.sqrt(jnp.sum(values * values, axis=-1, keepdims=True) + EPSILON)


def as_column(line):
    return jnp.broadcast_to(line, (128, line.shape[1])).T


def in_hbm(value):
    return pltpu.with_memory_space_constraint(value, pltpu.HBM)


def params(limit=VMEM):
    return pltpu.CompilerParams(vmem_limit_bytes=limit)


def tile_kernel(emb_ref, tile_ref):
    rows = emb_ref.shape[0]
    for half in range(2):
        tile_ref[:, half] = emb_ref[:, half * 128 : half * 128 + 128].reshape(rows // 8, 8, 128)


def as_tiles(embeddings):
    rows, _ = embeddings.shape
    return pl.pallas_call(
        tile_kernel,
        out_shape=jax.ShapeDtypeStruct((rows // 8, 2, 8, 128), jnp.float32),
        compiler_params=params(),
        name="as_tiles",
    )(embeddings)


def prepare_kernel(left, right, mine, out_ref):
    at = 0
    for ref in (left, right, mine):
        values = ref[...]
        hi, lo = split(values * (1.0 / (radius_of(values) * LOGIT_DIVISOR)))
        out_ref[at : at + hi.shape[0]] = jnp.concatenate([hi, lo, hi], axis=1)
        at += hi.shape[0]


def prepare(left, right, mine):
    shape = (3 * SLICE, 3 * WIDTH)
    return pl.pallas_call(
        prepare_kernel,
        out_shape=jax.ShapeDtypeStruct(shape, jnp.bfloat16),
        cost_estimate=pl.CostEstimate(flops=20 * 10**9, bytes_accessed=4 * shape[0] * WIDTH, transcendentals=0),
        compiler_params=params(),
        name="prepare",
    )(left, right, mine)


def forward_kernel(
    ready, mine, far0, far1, sib, got, got_sib, pos_ref, e_out, c_out, line_ref,
    left_ref, e_buf, c_buf, tot_ref, e_sem, c_sem, ready_sem,
):
    orders, _, count = e_buf.shape
    wide = 2 * SLICE

    at = ready.shape[0]
    ready_copy = pltpu.make_async_copy(ready, left_ref.at[pl.ds(0, at)], ready_sem)
    ready_copy.start()
    for ref in (far0, far1):
        values = ref[...]
        hi, lo = split(values * (1.0 / (radius_of(values) * LOGIT_DIVISOR)))
        left_ref[at : at + hi.shape[0]] = jnp.concatenate([hi, lo, hi], axis=1)
        at += hi.shape[0]
    half = got.shape[1] // 2
    tiles = got.shape[0] * half // 8

    copies = []
    for base in range(0, count, wide):
        for which, ref in enumerate((mine, sib) if base == 0 else (got, got_sib)):
            if base == 0:
                piece = ref[...]
            else:
                begin = (base // wide - 1) * half
                piece = rows_of(ref[:, begin : begin + half].reshape(tiles, 8, 128))
            hi, lo = split(piece * (1.0 / radius_of(piece)))
            c_buf[base + which * SLICE : base + which * SLICE + SLICE] = jnp.concatenate([hi, lo], axis=1)
        view = (pl.ds(base, wide),)
        copies.append(pltpu.make_async_copy(c_buf.at[view], c_out.at[view], c_sem.at[base // wide]))
        copies[-1].start()
        if base == 0:
            ready_copy.wait()
        for order in range(0, orders, 2):
            band = slice(order * SLICE, (order + 2) * SLICE)
            col = c_buf[base : base + wide]
            hi, lo = col[:, :WIDTH], col[:, WIDTH:]
            scores = lax.dot_general(
                left_ref[band],
                jnp.concatenate([hi, hi, lo], axis=1),
                (((1,), (1,)), ((), ())),
                preferred_element_type=jnp.float32,
            )
            total = jnp.zeros((wide, 128), jnp.float32) if base == 0 else tot_ref[0, band]
            if base == 0:
                match = jnp.zeros((wide, 128), jnp.float32)
                row_ids = lax.broadcasted_iota(jnp.int32, (wide, 128), 0) + order * SLICE
                lane_ids = lax.broadcasted_iota(jnp.int32, (wide, 128), 1)
            for k in range(0, wide, 128):
                score = scores[:, k : k + 128]
                e = jnp.exp(score)
                if base == 0:
                    match = match + jnp.where(row_ids == pos_ref[:, k : k + 128], score, 0.0)
                    if order == SELF and k < SLICE:
                        e = jnp.where(row_ids - SELF * SLICE == lane_ids + k, 0.0, e)
                total = total + e
                e_buf[order : order + 2, :, base + k : base + k + 128] = e.reshape(2, SLICE, 128)
            tot_ref[0, band] = total
            if base == 0:
                tot_ref[1, band] = match
            view = (pl.ds(order, 2), slice(None), pl.ds(base, wide))
            sem = e_sem.at[base // wide * 2 + order // 2]
            copies.append(pltpu.make_async_copy(e_buf.at[view], e_out.at[view], sem))
            copies[-1].start()

    line = jnp.concatenate([jnp.sum(tot_ref[k].T, axis=0, keepdims=True) for k in range(2)], axis=0)
    for member in range(line_ref.shape[0]):
        line_ref[member] = line
    for copy in copies:
        copy.wait()


def forward(operands, members):
    rows, count = 4 * SLICE, 6 * SLICE
    return pl.pallas_call(
        forward_kernel,
        in_specs=[HBM] + [pl.BlockSpec()] * (len(operands) - 1),
        out_specs=[HBM, HBM, pl.BlockSpec()],
        out_shape=(
            pltpu.HBM((4, SLICE, count), jnp.float32),
            pltpu.HBM((count, 2 * WIDTH), jnp.bfloat16),
            jax.ShapeDtypeStruct((members, 2, rows), jnp.float32),
        ),
        scratch_shapes=[
            pltpu.VMEM((rows, 3 * WIDTH), jnp.bfloat16),
            pltpu.VMEM((4, SLICE, count), jnp.float32),
            pltpu.VMEM((count, 2 * WIDTH), jnp.bfloat16),
            pltpu.VMEM((2, rows, 128), jnp.float32),
            pltpu.SemaphoreType.DMA((6,)),
            pltpu.SemaphoreType.DMA((3,)),
            pltpu.SemaphoreType.DMA,
        ],
        cost_estimate=pl.CostEstimate(
            flops=6 * rows * count * WIDTH, bytes_accessed=4 * rows * count, transcendentals=rows * count
        ),
        compiler_params=params(VMEM_LARGE),
        name="forward",
    )(in_hbm(operands[0]), *operands[1:])


def denominator_kernel(member_ref, all_ref, row_ref, own_ref, line_ref, spread_ref):
    member = member_ref[0]
    members = all_ref.shape[0]

    def summed(owner, kind):
        value = 0.0
        for by, order in ((0, SELF), (2, 0), (members - 2, 1), (4, 3)):
            held = all_ref[lax.rem(owner + by, members)]
            value = value + held[kind : kind + 1, order * SLICE : order * SLICE + SLICE]
        return value

    mate = member + 1 - 2 * lax.rem(member, 2)
    own = summed(member, 0)
    line_ref[0:1] = own
    line_ref[1:2] = summed(member, 1)
    both = jnp.concatenate([own, summed(mate, 0)], axis=1)
    own_ref[...] = both
    spread_ref[...] = jnp.broadcast_to(both.reshape(1, 1, 2 * SLICE), spread_ref.shape)
    for order, by in enumerate((members - 2, 2, 0, 4)):
        value = own if by == 0 else summed(lax.rem(member + by, members), 0)
        row_ref[:, order * SLICE : order * SLICE + SLICE] = value


def denominators(member, everything, groups):
    return pl.pallas_call(
        denominator_kernel,
        in_specs=[SMEM, pl.BlockSpec()],
        out_shape=(
            jax.ShapeDtypeStruct((1, 4 * SLICE), jnp.float32),
            jax.ShapeDtypeStruct((1, 2 * SLICE), jnp.float32),
            jax.ShapeDtypeStruct((2, SLICE), jnp.float32),
            jax.ShapeDtypeStruct((groups, 1, 2 * SLICE), jnp.float32),
        ),
        compiler_params=params(),
        name="denominators",
    )(member, everything)


def backward_kernel(
    order, partner_ref, row_ref, own_ref, everyone_ref, pos_ref, e_in, c_in, *refs
):
    out_refs, (run_ref, e_buf, c_buf, e_sem, c_sem) = refs[:-5], refs[-5:]
    slices = e_buf.shape[0]
    wide = 2 * SLICE
    copies = []
    for k in range(3):
        wanted = pl.ds(k * wide, wide)
        copies.append(
            pltpu.make_async_copy(
                e_in.at[pl.ds(order, slices), :, wanted], e_buf.at[:, :, wanted], e_sem.at[k]
            )
        )
        copies.append(pltpu.make_async_copy(c_in.at[wanted], c_buf.at[wanted], c_sem.at[k]))
    for copy in copies:
        copy.start()

    rows = slices * SLICE
    row_inv = 1.0 / as_column(row_ref[:, order * SLICE : order * SLICE + rows])
    row_ids = lax.broadcasted_iota(jnp.int32, (rows, 128), 0) + order * SLICE
    for k in range(3):
        col_inv = 1.0 / (own_ref[...] if k == 0 else everyone_ref[partner_ref[k - 1]])
        copies[2 * k].wait()
        copies[2 * k + 1].wait()
        his, los = [], []
        for at in range(0, wide, 128):
            e = e_buf[:, :, k * wide + at : k * wide + at + 128].reshape(rows, 128)
            weight = e * (row_inv + col_inv[:, at : at + 128])
            if k == 0:
                weight = weight - jnp.where(row_ids == pos_ref[:, at : at + 128], 2.0, 0.0)
            hi, lo = split(weight)
            his.append(hi)
            los.append(lo)
        cols = c_buf[k * wide : k * wide + wide]
        c_hi, c_lo = cols[:, :WIDTH], cols[:, WIDTH:]
        part = jnp.dot(
            jnp.concatenate(his + his + los, axis=1),
            jnp.concatenate([c_hi, c_lo, c_hi], axis=0),
            preferred_element_type=jnp.float32,
        )
        if k == 0:
            run_ref[...] = part
        elif k == 1:
            run_ref[...] += part
        else:
            part = run_ref[...] + part
            size = rows // len(out_refs)
            for which, ref in enumerate(out_refs):
                ref[...] = part[which * size : which * size + size]


def backward(order, slices, pieces, partners, row_den, own_den, everyone, pos, e, cols):
    count = 6 * SLICE
    return pl.pallas_call(
        functools.partial(backward_kernel, order),
        in_specs=[SMEM] + [pl.BlockSpec()] * 4 + [HBM] * 2,
        out_shape=[jax.ShapeDtypeStruct((slices * SLICE // pieces, WIDTH), jnp.float32)] * pieces,
        scratch_shapes=[
            pltpu.VMEM((slices * SLICE, WIDTH), jnp.float32),
            pltpu.VMEM((slices, SLICE, count), jnp.float32),
            pltpu.VMEM((count, 2 * WIDTH), jnp.bfloat16),
            pltpu.SemaphoreType.DMA((3,)),
            pltpu.SemaphoreType.DMA((3,)),
        ],
        cost_estimate=pl.CostEstimate(
            flops=6 * slices * SLICE * count * WIDTH, bytes_accessed=4 * slices * SLICE * count, transcendentals=0
        ),
        compiler_params=params(VMEM_LARGE),
        name="backward_%d" % order,
    )(partners, row_den, own_den, everyone, pos, in_hbm(e), in_hbm(cols))


def add_kernel(a_ref, b_ref, c_ref, d_ref, ab_ref, cd_ref):
    ab_ref[...] = a_ref[...] + b_ref[...]
    cd_ref[...] = c_ref[...] + d_ref[...]


def add_pairs(a, b, c, d):
    out = jax.ShapeDtypeStruct(a.shape, jnp.float32)
    return pl.pallas_call(add_kernel, out_shape=(out, out), compiler_params=params(), name="add_pairs")(
        a, b, c, d
    )


def finish_kernel(emb_ref, run_ref, low0, low1, high0, high1, line_ref, loss_ref, grad_ref):
    values = emb_ref[...]
    radius = radius_of(values)
    unit = values / radius
    low, high = low0[...] + low1[...], high0[...] + high1[...]
    slope = (run_ref[...] + jnp.concatenate([low, high], axis=0)) / LOGIT_DIVISOR
    grad_ref[...] = (slope - unit * jnp.sum(unit * slope, axis=-1, keepdims=True)) / radius
    loss_ref[...] = jnp.log(line_ref[0:1]) - line_ref[1:2]


def finish(embeddings, run, lows, highs, line):
    rows, width = embeddings.shape
    return pl.pallas_call(
        finish_kernel,
        out_shape=(
            jax.ShapeDtypeStruct((1, rows), jnp.float32),
            jax.ShapeDtypeStruct((rows, width), jnp.float32),
        ),
        compiler_params=params(),
        name="finish",
    )(embeddings, run, *lows, *highs, line)


def local(embeddings, positive, pairing):
    rows, width = embeddings.shape
    members = lax.axis_size("mem")
    groups = lax.axis_size("grp")
    block = rows * members
    rounds = pairing.shape[0]
    group = lax.axis_index("grp")
    member = lax.axis_index("mem")
    half = rows // 2

    def shift(value, by):
        return lax.ppermute(value, "mem", [(m, (m + by) % members) for m in range(members)])

    def swap(value):
        return lax.ppermute(value, "mem", [(m, m ^ 1) for m in range(members)])

    left, right = shift(embeddings, 2), shift(embeddings, -2)
    far = (shift(left[:half], 2), shift(right[half:], -2))
    per = rows * width // (groups * 128)
    pieces = lax.all_to_all(as_tiles(embeddings).reshape(groups, per, 128), "grp", 0, 0, tiled=True)
    picked = pieces[pairing.T].reshape(groups, rounds * per, 128)
    got = lax.all_to_all(picked, "grp", 0, 0, tiled=True)
    sib, pos_sib = swap(embeddings), swap(positive)
    ready = prepare(left, right, embeddings)
    got, ready, sib, pos_sib = lax.optimization_barrier((got, ready, sib, pos_sib))

    both = jnp.concatenate([positive, pos_sib]) - group * block
    owner = both // rows
    turn = (owner // 2 - member // 2) % (members // 2)
    order = jnp.where(turn == 0, SELF, jnp.where(turn == 3, 0, jnp.where(turn == 1, 1, 3)))
    pos = jnp.where(owner % 2 == member % 2, order * rows + both % rows, -1).reshape(1, 2 * rows)

    e, cols, line = forward((ready, embeddings, *far, sib, got, swap(got), pos), members)

    everything = lax.all_to_all(line, "mem", 0, 0, tiled=True)
    row_den, own_den, line, spread = denominators(jnp.reshape(member, (1,)), everything, groups)
    everyone = lax.all_to_all(spread, "grp", 0, 0, tiled=True)

    shared = (pairing[:, group], row_den, own_den, everyone, pos, e, cols)
    far_low, far_high = backward(3, 1, 2, *shared)
    far_low, far_high = shift(far_low, 2), shift(far_high, -2)
    left_low, left_high, right_low, right_high = backward(0, 2, 4, *shared)
    high0, low1 = shift(right_high, 2), shift(left_low, -2)
    right_low, left_high = add_pairs(right_low, far_low, left_high, far_high)
    low0, high1 = shift(right_low, 2), shift(left_high, -2)
    (run,) = backward(SELF, 1, 1, *shared)
    loss, grad = finish(embeddings, run, (low0, low1), (high0, high1), line)
    return loss.reshape(rows), grad


def solution(mesh):
    placed = (P(("grp", "mem"), None), P(("grp", "mem")), P())
    return jax.shard_map(
        local,
        mesh=mesh,
        in_specs=placed,
        out_specs=(P(("grp", "mem")), P(("grp", "mem"), None)),
        check_vma=False,
    )
```

```python
import functools

import jax
import jax.numpy as jnp
from jax import lax
from jax.experimental import pallas as pl
from jax.experimental.pallas import tpu as pltpu
from jax.sharding import PartitionSpec as P

LOGIT_DIVISOR = 0.1
EPSILON = 1e-06
SLICE = 384
WIDTH = 256
SELF = 2
VMEM = 16 * 1024 * 1024
VMEM_LARGE = 44 * 1024 * 1024
HBM = pl.BlockSpec(memory_space=pltpu.HBM)
SMEM = pl.BlockSpec(memory_space=pltpu.SMEM)


def split(values):
    hi = values.astype(jnp.bfloat16)
    lo = (values - hi.astype(jnp.float32)).astype(jnp.bfloat16)
    return hi, lo


def rows_of(tiles):
    pairs = tiles.reshape(tiles.shape[0] // 2, 2, 8, 128)
    rows = tiles.shape[0] * 4
    return jnp.concatenate([pairs[:, 0].reshape(rows, 128), pairs[:, 1].reshape(rows, 128)], axis=1)


def radius_of(values):
    return jnp.sqrt(jnp.sum(values * values, axis=-1, keepdims=True) + EPSILON)


def as_column(line):
    return jnp.broadcast_to(line, (128, line.shape[1])).T


def in_hbm(value):
    return pltpu.with_memory_space_constraint(value, pltpu.HBM)


def params(limit=VMEM):
    return pltpu.CompilerParams(vmem_limit_bytes=limit)


def tile_kernel(emb_ref, tile_ref):
    rows = emb_ref.shape[0]
    for half in range(2):
        tile_ref[:, half] = emb_ref[:, half * 128 : half * 128 + 128].reshape(rows // 8, 8, 128)


def as_tiles(embeddings):
    rows, _ = embeddings.shape
    return pl.pallas_call(
        tile_kernel,
        out_shape=jax.ShapeDtypeStruct((rows // 8, 2, 8, 128), jnp.float32),
        compiler_params=params(),
        name="as_tiles",
    )(embeddings)


def pick_kernel(pairing_ref, pieces_ref, out_ref):
    size = pieces_ref.shape[1]
    for which in range(out_ref.shape[1] // size):
        for group in range(out_ref.shape[0]):
            out_ref[group, which * size : which * size + size] = pieces_ref[pairing_ref[which, group]]


def pick(pairing, pieces):
    rounds, groups = pairing.shape
    return pl.pallas_call(
        pick_kernel,
        in_specs=[SMEM, pl.BlockSpec()],
        out_shape=jax.ShapeDtypeStruct((groups, rounds * pieces.shape[1], 128), jnp.float32),
        compiler_params=params(),
        name="pick",
    )(pairing, pieces)


def scaled_rows(refs, out_ref, at=0):
    for ref in refs:
        values = ref[...]
        hi, lo = split(values * (1.0 / (radius_of(values) * LOGIT_DIVISOR)))
        out_ref[at : at + hi.shape[0]] = jnp.concatenate([hi, lo, hi], axis=1)
        at += hi.shape[0]


def unit_parts(values):
    hi, lo = split(values * (1.0 / radius_of(values)))
    return jnp.concatenate([hi, lo], axis=1)


def product(left, cols):
    hi, lo = cols[:, :WIDTH], cols[:, WIDTH:]
    return lax.dot_general(
        left,
        jnp.concatenate([hi, hi, lo], axis=1),
        (((1,), (1,)), ((), ())),
        preferred_element_type=jnp.float32,
    )


def exponentials(scores, first_row, pos_ref, store):
    height = scores.shape[0]
    total = jnp.zeros((height, 128), jnp.float32)
    match = jnp.zeros((height, 128), jnp.float32)
    if first_row is not None:
        row_ids = lax.broadcasted_iota(jnp.int32, (height, 128), 0) + first_row
        lane_ids = lax.broadcasted_iota(jnp.int32, (height, 128), 1)
    for k in range(0, scores.shape[1], 128):
        score = scores[:, k : k + 128]
        e = jnp.exp(score)
        if first_row is not None:
            match = match + jnp.where(row_ids == pos_ref[:, k : k + 128], score, 0.0)
            if first_row <= SELF * SLICE < first_row + height and k < SLICE:
                e = jnp.where(row_ids - SELF * SLICE == lane_ids + k, 0.0, e)
        total = total + e
        store(k, e)
    return total, match


def as_line(total):
    return jnp.sum(total.T, axis=0, keepdims=True)


def own_kernel(
    ready, mine, sib, pos_ref, c_out, e_out, line_ref, left_ref, c_buf, e_buf, ready_sem, c_sem, e_sem
):
    ready_copy = pltpu.make_async_copy(ready, left_ref, ready_sem)
    ready_copy.start()
    c_buf[:SLICE] = unit_parts(mine[...])
    c_buf[SLICE:] = unit_parts(sib[...])
    copies = [pltpu.make_async_copy(c_buf, c_out, c_sem)]
    copies[0].start()
    ready_copy.wait()

    coming = product(left_ref[:SLICE], c_buf[...])
    totals, matches = [], []
    for order in range(3):
        scores = coming
        if order < 2:
            at = (order + 1) * SLICE
            coming = product(left_ref[at : at + SLICE], c_buf[...])

        def store(k, e):
            e_buf[order, :, k : k + 128] = e

        total, match = exponentials(scores, order * SLICE, pos_ref, store)
        totals.append(as_line(total))
        matches.append(as_line(match))
        copies.append(pltpu.make_async_copy(e_buf.at[order], e_out.at[order], e_sem.at[order]))
        copies[-1].start()
    line_ref[0:1] = jnp.concatenate(totals, axis=1)
    line_ref[1:2] = jnp.concatenate(matches, axis=1)
    for copy in copies:
        copy.wait()


def own_scores(ready, mine, sib, pos):
    rows, wide = 3 * SLICE, 2 * SLICE
    shapes = [((wide, 2 * WIDTH), jnp.bfloat16), ((3, SLICE, wide), jnp.float32)]
    return pl.pallas_call(
        own_kernel,
        in_specs=[HBM] + [pl.BlockSpec()] * 3,
        out_specs=[HBM] * 2 + [pl.BlockSpec()],
        out_shape=[pltpu.HBM(*shape) for shape in shapes] + [jax.ShapeDtypeStruct((2, rows), jnp.float32)],
        scratch_shapes=[pltpu.VMEM((rows, 3 * WIDTH), jnp.bfloat16)]
        + [pltpu.VMEM(*shape) for shape in shapes]
        + [pltpu.SemaphoreType.DMA, pltpu.SemaphoreType.DMA, pltpu.SemaphoreType.DMA((3,))],
        cost_estimate=pl.CostEstimate(
            flops=6 * rows * wide * WIDTH, bytes_accessed=4 * rows * wide, transcendentals=rows * wide
        ),
        compiler_params=params(VMEM_LARGE),
        name="own_scores",
    )(in_hbm(ready), mine, sib, pos)


def prepare_kernel(*refs):
    scaled_rows(refs[:-1], refs[-1])


def prepare(name, *pieces):
    rows = sum(piece.shape[0] for piece in pieces)
    return pl.pallas_call(
        prepare_kernel,
        out_shape=jax.ShapeDtypeStruct((rows, 3 * WIDTH), jnp.bfloat16),
        cost_estimate=pl.CostEstimate(flops=20 * 10**9, bytes_accessed=8 * rows * WIDTH, transcendentals=0),
        compiler_params=params(),
        name=name,
    )(*pieces)


def forward_kernel(
    ready, c_own, ready_far, line_in, got, got_sib, pos_ref, e0_out, e1_out, c_out, line_ref,
    left_ref, own_buf, c_buf, e0_buf, e1_buf, tot_ref, in_sem, c_sem, e0_sem, e1_sem,
):
    orders, _, count = e1_buf.shape
    wide = 2 * SLICE
    at = ready.shape[0]
    ready_copy = pltpu.make_async_copy(ready, left_ref.at[pl.ds(0, at)], in_sem.at[0])
    own_copy = pltpu.make_async_copy(c_own, own_buf, in_sem.at[1])
    own_copy.start()
    ready_copy.start()
    left_ref[at:] = ready_far[...]
    half = got.shape[1] // 2
    tiles = got.shape[0] * half // 8

    copies = []

    def columns(base):
        for which, ref in enumerate((got, got_sib)):
            begin = base // wide * half
            piece = rows_of(ref[:, begin : begin + half].reshape(tiles, 8, 128))
            c_buf[base + which * SLICE : base + which * SLICE + SLICE] = unit_parts(piece)
        view = (pl.ds(base, wide),)
        copies.append(pltpu.make_async_copy(c_buf.at[view], c_out.at[view], c_sem.at[base // wide]))
        copies[-1].start()

    def score(band, base):
        rows = left_ref[band * wide : band * wide + wide]
        return product(rows, c_buf[base : base + wide])

    columns(0)
    own_copy.wait()
    ready_copy.wait()
    scores = product(left_ref[at:], own_buf[...])
    coming = score(0, 0)

    def store_own(k, e):
        e0_buf[:, :, k : k + 128] = e.reshape(1, SLICE, 128)

    far_total, far_match = exponentials(scores, at, pos_ref, store_own)
    copies.append(pltpu.make_async_copy(e0_buf, e0_out, e0_sem))
    copies[-1].start()

    items = [(band, base) for base in range(0, count, wide) for band in range(orders // 2)]
    for turn, (band, base) in enumerate(items):
        scores = coming
        if turn + 1 < len(items):
            if items[turn + 1][1] != base:
                columns(items[turn + 1][1])
            coming = score(*items[turn + 1])

        def store(k, e):
            e1_buf[2 * band : 2 * band + 2, :, base + k : base + k + 128] = e.reshape(2, SLICE, 128)

        total, _ = exponentials(scores, None, pos_ref, store)
        if base == 0:
            tot_ref[band * wide : band * wide + wide] = total
        else:
            tot_ref[band * wide : band * wide + wide] += total
        view = (pl.ds(2 * band, 2), slice(None), pl.ds(base, wide))
        copies.append(pltpu.make_async_copy(e1_buf.at[view], e1_out.at[view], e1_sem.at[turn]))
        copies[-1].start()

    far = jnp.concatenate([as_line(far_total), as_line(far_match)], axis=0)
    line = jnp.concatenate([line_in[...], far], axis=1)
    total = as_line(tot_ref[...]) + line[0:1]
    for member in range(line_ref.shape[0]):
        line_ref[member, 0:1] = total
        line_ref[member, 1:2] = line[1:2]
    for copy in copies:
        copy.wait()


def forward(ready, c_own, ready_far, line, got, got_sib, pos, members):
    rows, wide, count = 4 * SLICE, 2 * SLICE, 4 * SLICE
    own_shape, part_shape = ((1, SLICE, wide), jnp.float32), ((4, SLICE, count), jnp.float32)
    col_shape = ((count, 2 * WIDTH), jnp.bfloat16)
    return pl.pallas_call(
        forward_kernel,
        in_specs=[HBM] * 2 + [pl.BlockSpec()] * 5,
        out_specs=[HBM] * 3 + [pl.BlockSpec()],
        out_shape=(
            pltpu.HBM(*own_shape),
            pltpu.HBM(*part_shape),
            pltpu.HBM(*col_shape),
            jax.ShapeDtypeStruct((members, 2, rows), jnp.float32),
        ),
        scratch_shapes=[
            pltpu.VMEM((rows, 3 * WIDTH), jnp.bfloat16),
            pltpu.VMEM((wide, 2 * WIDTH), jnp.bfloat16),
            pltpu.VMEM(*col_shape),
            pltpu.VMEM(*own_shape),
            pltpu.VMEM(*part_shape),
            pltpu.VMEM((rows, 128), jnp.float32),
            pltpu.SemaphoreType.DMA((2,)),
            pltpu.SemaphoreType.DMA((2,)),
            pltpu.SemaphoreType.DMA,
            pltpu.SemaphoreType.DMA((4,)),
        ],
        cost_estimate=pl.CostEstimate(
            flops=6 * rows * count * WIDTH, bytes_accessed=4 * rows * count, transcendentals=rows * count
        ),
        compiler_params=params(VMEM_LARGE),
        name="forward",
    )(in_hbm(ready), in_hbm(c_own), ready_far, line, got, got_sib, pos)


def denominator_kernel(member_ref, all_ref, row_ref, own_ref, line_ref, spread_ref):
    member = member_ref[0]
    members = all_ref.shape[0]

    def summed(owner, kind):
        value = 0.0
        for by, order in ((0, SELF), (2, 0), (members - 2, 1), (4, 3)):
            held = all_ref[lax.rem(owner + by, members)]
            value = value + held[kind : kind + 1, order * SLICE : order * SLICE + SLICE]
        return value

    mate = member + 1 - 2 * lax.rem(member, 2)
    own = summed(member, 0)
    line_ref[0:1] = own
    line_ref[1:2] = summed(member, 1)
    both = jnp.concatenate([own, summed(mate, 0)], axis=1)
    own_ref[...] = both
    spread_ref[...] = jnp.broadcast_to(both.reshape(1, 1, 2 * SLICE), spread_ref.shape)
    for order, by in enumerate((members - 2, 2, 0, 4)):
        value = own if by == 0 else summed(lax.rem(member + by, members), 0)
        row_ref[:, order * SLICE : order * SLICE + SLICE] = value


def denominators(member, everything, groups):
    return pl.pallas_call(
        denominator_kernel,
        in_specs=[SMEM, pl.BlockSpec()],
        out_shape=(
            jax.ShapeDtypeStruct((1, 4 * SLICE), jnp.float32),
            jax.ShapeDtypeStruct((1, 2 * SLICE), jnp.float32),
            jax.ShapeDtypeStruct((2, SLICE), jnp.float32),
            jax.ShapeDtypeStruct((groups, 1, 2 * SLICE), jnp.float32),
        ),
        compiler_params=params(),
        name="denominators",
    )(member, everything)


def backward_kernel(
    bands, partner_ref, row_ref, own_ref, everyone_ref, pos_ref, e0_in, e1_in, c0_in, c1_in, *refs
):
    out_refs, (run_ref, e_buf, c_buf, e_sem, c_sem) = refs[:-5], refs[-5:]
    wide = 2 * SLICE
    steps = e_buf.shape[1] // wide
    copies = []
    for k in range(steps):
        wanted = pl.ds(k * wide, wide)
        group = []
        at = 0
        for which, (order, begin, size) in enumerate(bands):
            rows = pl.ds(begin, size)
            if k == 0:
                src = e0_in.at[order if e0_in.shape[0] > 1 else 0, rows]
            else:
                src = e1_in.at[order, rows, pl.ds((k - 1) * wide, wide)]
            group.append(pltpu.make_async_copy(src, e_buf.at[pl.ds(at, size), wanted], e_sem.at[k, which]))
            at += size
        src = c0_in if k == 0 else c1_in.at[pl.ds((k - 1) * wide, wide)]
        group.append(pltpu.make_async_copy(src, c_buf.at[wanted], c_sem.at[k]))
        copies.append(group)
        for copy in group:
            copy.start()

    columns, places = [], []
    for order, begin, size in bands:
        column = as_column(row_ref[:, order * SLICE : order * SLICE + SLICE])
        columns.append(column[begin : begin + size])
        places.append(lax.broadcasted_iota(jnp.int32, (size, 128), 0) + (order * SLICE + begin))
    row_inv = 1.0 / jnp.concatenate(columns, axis=0)
    row_ids = jnp.concatenate(places, axis=0)
    for k in range(steps):
        col_inv = 1.0 / (own_ref[...] if k == 0 else everyone_ref[partner_ref[k - 1]])
        for copy in copies[k]:
            copy.wait()
        his, los = [], []
        for at in range(0, wide, 128):
            weight = e_buf[:, k * wide + at : k * wide + at + 128] * (row_inv + col_inv[:, at : at + 128])
            if k == 0:
                weight = weight - jnp.where(row_ids == pos_ref[:, at : at + 128], 2.0, 0.0)
            hi, lo = split(weight)
            his.append(hi)
            los.append(lo)
        cols = c_buf[k * wide : k * wide + wide]
        c_hi, c_lo = cols[:, :WIDTH], cols[:, WIDTH:]
        part = jnp.dot(
            jnp.concatenate(his + his + los, axis=1),
            jnp.concatenate([c_hi, c_lo, c_hi], axis=0),
            preferred_element_type=jnp.float32,
        )
        if k == 0:
            run_ref[...] = part
        elif k + 1 < steps:
            run_ref[...] += part
        else:
            part = run_ref[...] + part
            size = part.shape[0] // len(out_refs)
            for which, ref in enumerate(out_refs):
                ref[...] = part[which * size : which * size + size]


def backward(bands, pieces, e0, partners, row_den, own_den, everyone, pos, e1, c0, c1):
    count = 6 * SLICE
    return pl.pallas_call(
        functools.partial(backward_kernel, bands),
        in_specs=[SMEM] + [pl.BlockSpec()] * 4 + [HBM] * 4,
        out_shape=[jax.ShapeDtypeStruct((SLICE // pieces, WIDTH), jnp.float32)] * pieces,
        scratch_shapes=[
            pltpu.VMEM((SLICE, WIDTH), jnp.float32),
            pltpu.VMEM((SLICE, count), jnp.float32),
            pltpu.VMEM((count, 2 * WIDTH), jnp.bfloat16),
            pltpu.SemaphoreType.DMA((3, len(bands))),
            pltpu.SemaphoreType.DMA((3,)),
        ],
        cost_estimate=pl.CostEstimate(
            flops=6 * SLICE * count * WIDTH, bytes_accessed=4 * SLICE * count, transcendentals=0
        ),
        compiler_params=params(VMEM_LARGE),
        name="backward_%d_%d" % bands[0][:2],
    )(partners, row_den, own_den, everyone, pos, *map(in_hbm, (e0, e1, c0, c1)))


def add_kernel(a_ref, b_ref, c_ref, d_ref, ab_ref, cd_ref):
    ab_ref[...] = a_ref[...] + b_ref[...]
    cd_ref[...] = c_ref[...] + d_ref[...]


def add_pairs(a, b, c, d):
    out = jax.ShapeDtypeStruct(a.shape, jnp.float32)
    return pl.pallas_call(add_kernel, out_shape=(out, out), compiler_params=params(), name="add_pairs")(
        a, b, c, d
    )


def finish_kernel(emb_ref, run_ref, low0, low1, high0, high1, line_ref, loss_ref, grad_ref):
    values = emb_ref[...]
    radius = radius_of(values)
    unit = values / radius
    low, high = low0[...] + low1[...], high0[...] + high1[...]
    slope = (run_ref[...] + jnp.concatenate([low, high], axis=0)) / LOGIT_DIVISOR
    grad_ref[...] = (slope - unit * jnp.sum(unit * slope, axis=-1, keepdims=True)) / radius
    loss_ref[...] = (jnp.log(line_ref[0:1]) - line_ref[1:2]).reshape(loss_ref.shape)


def finish(embeddings, run, lows, highs, line):
    rows, width = embeddings.shape
    return pl.pallas_call(
        finish_kernel,
        out_shape=(
            jax.ShapeDtypeStruct((rows,), jnp.float32),
            jax.ShapeDtypeStruct((rows, width), jnp.float32),
        ),
        compiler_params=params(),
        name="finish",
    )(embeddings, run, *lows, *highs, line)


def local(embeddings, positive, pairing):
    rows, width = embeddings.shape
    members = lax.axis_size("mem")
    groups = lax.axis_size("grp")
    block = rows * members
    rounds = pairing.shape[0]
    group = lax.axis_index("grp")
    member = lax.axis_index("mem")
    half = rows // 2

    def shift(value, by):
        return lax.ppermute(value, "mem", [(m, (m + by) % members) for m in range(members)])

    def swap(value):
        return lax.ppermute(value, "mem", [(m, m ^ 1) for m in range(members)])

    left, right = shift(embeddings, 2), shift(embeddings, -2)
    far = (shift(left[:half], 2), shift(right[half:], -2))
    per = rows * width // (groups * 128)
    pieces = lax.all_to_all(as_tiles(embeddings).reshape(groups, per, 128), "grp", 0, 0, tiled=True)
    got = lax.all_to_all(pick(pairing, pieces), "grp", 0, 0, tiled=True)
    sib, pos_sib = swap(embeddings), swap(positive)

    both = jnp.concatenate([positive, pos_sib]) - group * block
    owner = both // rows
    turn = (owner // 2 - member // 2) % (members // 2)
    order = jnp.where(turn == 0, SELF, jnp.where(turn == 3, 0, jnp.where(turn == 1, 1, 3)))
    pos = jnp.where(owner % 2 == member % 2, order * rows + both % rows, -1).reshape(1, 2 * rows)

    ready = prepare("prepare", left, right, embeddings)
    c_own, e_own, line = own_scores(ready, embeddings, sib, pos)
    ready_far = prepare("prepare_far", *far)
    got, line, ready_far = lax.optimization_barrier((got, line, ready_far))
    e_far, e_part, c_part, line = forward(ready, c_own, ready_far, line, got, swap(got), pos, members)

    everything = lax.all_to_all(line, "mem", 0, 0, tiled=True)
    row_den, own_den, line, spread = denominators(jnp.reshape(member, (1,)), everything, groups)
    everyone = lax.all_to_all(spread, "grp", 0, 0, tiled=True)

    shared = (pairing[:, group], row_den, own_den, everyone, pos, e_part, c_own, c_part)
    far_low, far_high = backward(((3, 0, rows),), 2, e_far, *shared)
    far_low, far_high = shift(far_low, 2), shift(far_high, -2)
    left_low, right_high = backward(((0, 0, half), (1, half, half)), 2, e_own, *shared)
    high0, low1 = shift(right_high, 2), shift(left_low, -2)
    left_high, right_low = backward(((0, half, half), (1, 0, half)), 2, e_own, *shared)
    right_low, left_high = add_pairs(right_low, far_low, left_high, far_high)
    low0, high1 = shift(right_low, 2), shift(left_high, -2)
    (run,) = backward(((SELF, 0, rows),), 1, e_own, *shared)
    return finish(embeddings, run, (low0, low1), (high0, high1), line)


def solution(mesh):
    placed = (P(("grp", "mem"), None), P(("grp", "mem")), P())
    return jax.shard_map(
        local,
        mesh=mesh,
        in_specs=placed,
        out_specs=(P(("grp", "mem")), P(("grp", "mem"), None)),
        check_vma=False,
    )
```

```python
import functools

import jax
import jax.numpy as jnp
from jax import lax
from jax.experimental import pallas as pl
from jax.experimental.pallas import tpu as pltpu
from jax.sharding import PartitionSpec as P

LOGIT_DIVISOR = 0.1
EPSILON = 1e-06
SLICE = 384
WIDTH = 256
SELF = 2
VMEM = 16 * 1024 * 1024
VMEM_LARGE = 44 * 1024 * 1024
HBM = pl.BlockSpec(memory_space=pltpu.HBM)
SMEM = pl.BlockSpec(memory_space=pltpu.SMEM)


def split(values):
    hi = values.astype(jnp.bfloat16)
    lo = (values - hi.astype(jnp.float32)).astype(jnp.bfloat16)
    return hi, lo


def rows_of(tiles):
    pairs = tiles.reshape(tiles.shape[0] // 2, 2, 8, 128)
    rows = tiles.shape[0] * 4
    return jnp.concatenate([pairs[:, 0].reshape(rows, 128), pairs[:, 1].reshape(rows, 128)], axis=1)


def radius_of(values):
    return jnp.sqrt(jnp.sum(values * values, axis=-1, keepdims=True) + EPSILON)


def as_column(line):
    return jnp.broadcast_to(line, (128, line.shape[1])).T


def in_hbm(value):
    return pltpu.with_memory_space_constraint(value, pltpu.HBM)


def params(limit=VMEM):
    return pltpu.CompilerParams(vmem_limit_bytes=limit)


def tile_kernel(emb_ref, tile_ref):
    rows = emb_ref.shape[0]
    for half in range(2):
        tile_ref[:, half] = emb_ref[:, half * 128 : half * 128 + 128].reshape(rows // 8, 8, 128)


def as_tiles(embeddings):
    rows, _ = embeddings.shape
    return pl.pallas_call(
        tile_kernel,
        out_shape=jax.ShapeDtypeStruct((rows // 8, 2, 8, 128), jnp.float32),
        compiler_params=params(),
        name="as_tiles",
    )(embeddings)


def pick_kernel(pairing_ref, pieces_ref, out_ref):
    size = pieces_ref.shape[1]
    for which in range(out_ref.shape[1] // size):
        for group in range(out_ref.shape[0]):
            out_ref[group, which * size : which * size + size] = pieces_ref[pairing_ref[which, group]]


def pick(pairing, pieces):
    rounds, groups = pairing.shape
    return pl.pallas_call(
        pick_kernel,
        in_specs=[SMEM, pl.BlockSpec()],
        out_shape=jax.ShapeDtypeStruct((groups, rounds * pieces.shape[1], 128), jnp.float32),
        compiler_params=params(),
        name="pick",
    )(pairing, pieces)


def scaled_rows(refs, out_ref, at=0):
    for ref in refs:
        values = ref[...]
        hi, lo = split(values * (1.0 / (radius_of(values) * LOGIT_DIVISOR)))
        out_ref[at : at + hi.shape[0]] = jnp.concatenate([hi, lo, hi], axis=1)
        at += hi.shape[0]


def unit_parts(values):
    hi, lo = split(values * (1.0 / radius_of(values)))
    return jnp.concatenate([hi, lo], axis=1)


def product(left, cols):
    hi, lo = cols[:, :WIDTH], cols[:, WIDTH:]
    return lax.dot_general(
        left,
        jnp.concatenate([hi, hi, lo], axis=1),
        (((1,), (1,)), ((), ())),
        preferred_element_type=jnp.float32,
    )


def exponentials(scores, first_row, pos_ref, store):
    height = scores.shape[0]
    total = jnp.zeros((height, 128), jnp.float32)
    match = jnp.zeros((height, 128), jnp.float32)
    if first_row is not None:
        row_ids = lax.broadcasted_iota(jnp.int32, (height, 128), 0) + first_row
        lane_ids = lax.broadcasted_iota(jnp.int32, (height, 128), 1)
    for k in range(0, scores.shape[1], 128):
        score = scores[:, k : k + 128]
        e = jnp.exp(score)
        if first_row is not None:
            match = match + jnp.where(row_ids == pos_ref[:, k : k + 128], score, 0.0)
            if first_row <= SELF * SLICE < first_row + height and k < SLICE:
                e = jnp.where(row_ids - SELF * SLICE == lane_ids + k, 0.0, e)
        total = total + e
        store(k, e)
    return total, match


def as_line(total):
    return jnp.sum(total.T, axis=0, keepdims=True)


def own_kernel(
    ready, mine, sib, pos_ref, c_out, e_out, line_ref, left_ref, c_buf, e_buf, ready_sem, c_sem, e_sem
):
    ready_copy = pltpu.make_async_copy(ready, left_ref, ready_sem)
    ready_copy.start()
    c_buf[:SLICE] = unit_parts(mine[...])
    c_buf[SLICE:] = unit_parts(sib[...])
    copies = [pltpu.make_async_copy(c_buf, c_out, c_sem)]
    copies[0].start()
    ready_copy.wait()

    coming = product(left_ref[:SLICE], c_buf[...])
    totals, matches = [], []
    for order in range(3):
        scores = coming
        if order < 2:
            at = (order + 1) * SLICE
            coming = product(left_ref[at : at + SLICE], c_buf[...])

        def store(k, e):
            e_buf[order, :, k : k + 128] = e

        total, match = exponentials(scores, order * SLICE, pos_ref, store)
        totals.append(as_line(total))
        matches.append(as_line(match))
        copies.append(pltpu.make_async_copy(e_buf.at[order], e_out.at[order], e_sem.at[order]))
        copies[-1].start()
    line_ref[0:1] = jnp.concatenate(totals, axis=1)
    line_ref[1:2] = jnp.concatenate(matches, axis=1)
    for copy in copies:
        copy.wait()


def own_scores(ready, mine, sib, pos):
    rows, wide = 3 * SLICE, 2 * SLICE
    shapes = [((wide, 2 * WIDTH), jnp.bfloat16), ((3, SLICE, wide), jnp.float32)]
    return pl.pallas_call(
        own_kernel,
        in_specs=[HBM] + [pl.BlockSpec()] * 3,
        out_specs=[HBM] * 2 + [pl.BlockSpec()],
        out_shape=[pltpu.HBM(*shape) for shape in shapes] + [jax.ShapeDtypeStruct((2, rows), jnp.float32)],
        scratch_shapes=[pltpu.VMEM((rows, 3 * WIDTH), jnp.bfloat16)]
        + [pltpu.VMEM(*shape) for shape in shapes]
        + [pltpu.SemaphoreType.DMA, pltpu.SemaphoreType.DMA, pltpu.SemaphoreType.DMA((3,))],
        cost_estimate=pl.CostEstimate(
            flops=6 * rows * wide * WIDTH, bytes_accessed=4 * rows * wide, transcendentals=rows * wide
        ),
        compiler_params=params(VMEM_LARGE),
        name="own_scores",
    )(in_hbm(ready), mine, sib, pos)


def prepare_kernel(*refs):
    pieces, (out_ref, buf, sem) = refs[:-3], refs[-3:]
    scaled_rows(pieces, buf)
    copy = pltpu.make_async_copy(buf, out_ref, sem)
    copy.start()
    copy.wait()


def prepare(name, *pieces):
    rows = sum(piece.shape[0] for piece in pieces)
    shape = ((rows, 3 * WIDTH), jnp.bfloat16)
    return pl.pallas_call(
        prepare_kernel,
        out_specs=HBM,
        out_shape=pltpu.HBM(*shape),
        scratch_shapes=[pltpu.VMEM(*shape), pltpu.SemaphoreType.DMA],
        cost_estimate=pl.CostEstimate(flops=20 * 10**9, bytes_accessed=8 * rows * WIDTH, transcendentals=0),
        compiler_params=params(),
        name=name,
    )(*pieces)


def forward_kernel(
    ready, c_own, ready_far, line_in, got, got_sib, pos_ref, e0_out, e1_out, c_out, line_ref,
    left_ref, own_buf, c_buf, e0_buf, e1_buf, tot_ref, in_sem, c_sem, e0_sem, e1_sem,
):
    chunks, orders, _, wide = e1_buf.shape
    count = chunks * wide
    at = ready.shape[0]
    ready_copy = pltpu.make_async_copy(ready, left_ref.at[pl.ds(0, at)], in_sem.at[0])
    own_copy = pltpu.make_async_copy(c_own, own_buf, in_sem.at[1])
    far_copy = pltpu.make_async_copy(ready_far, left_ref.at[pl.ds(at, SLICE)], in_sem.at[2])
    for copy in (own_copy, far_copy, ready_copy):
        copy.start()
    half = got.shape[1] // 2
    tiles = got.shape[0] * half // 8

    copies = []

    def columns(base):
        for which, ref in enumerate((got, got_sib)):
            begin = base // wide * half
            piece = rows_of(ref[:, begin : begin + half].reshape(tiles, 8, 128))
            c_buf[base + which * SLICE : base + which * SLICE + SLICE] = unit_parts(piece)
        view = (pl.ds(base, wide),)
        copies.append(pltpu.make_async_copy(c_buf.at[view], c_out.at[view], c_sem.at[base // wide]))
        copies[-1].start()

    def score(band, base):
        rows = left_ref[band * wide : band * wide + wide]
        return product(rows, c_buf[base : base + wide])

    columns(0)
    for copy in (own_copy, far_copy, ready_copy):
        copy.wait()
    scores = product(left_ref[at:], own_buf[...])
    coming = score(0, 0)

    def store_own(k, e):
        e0_buf[:, :, k : k + 128] = e.reshape(1, SLICE, 128)

    far_total, far_match = exponentials(scores, at, pos_ref, store_own)
    copies.append(pltpu.make_async_copy(e0_buf, e0_out, e0_sem))
    copies[-1].start()

    items = [(band, base) for base in range(0, count, wide) for band in range(orders // 2)]
    for turn, (band, base) in enumerate(items):
        scores = coming
        if turn + 1 < len(items):
            if items[turn + 1][1] != base:
                columns(items[turn + 1][1])
            coming = score(*items[turn + 1])

        def store(k, e):
            e1_buf[base // wide, 2 * band : 2 * band + 2, :, k : k + 128] = e.reshape(2, SLICE, 128)

        total, _ = exponentials(scores, None, pos_ref, store)
        if base == 0:
            tot_ref[band * wide : band * wide + wide] = total
        else:
            tot_ref[band * wide : band * wide + wide] += total
        view = (base // wide, pl.ds(2 * band, 2))
        copies.append(pltpu.make_async_copy(e1_buf.at[view], e1_out.at[view], e1_sem.at[turn]))
        copies[-1].start()

    far = jnp.concatenate([as_line(far_total), as_line(far_match)], axis=0)
    line = jnp.concatenate([line_in[...], far], axis=1)
    total = as_line(tot_ref[...]) + line[0:1]
    for member in range(line_ref.shape[0]):
        line_ref[member, 0:1] = total
        line_ref[member, 1:2] = line[1:2]
    for copy in copies:
        copy.wait()


def forward(ready, c_own, ready_far, line, got, got_sib, pos, members):
    rows, wide, count = 4 * SLICE, 2 * SLICE, 4 * SLICE
    own_shape, part_shape = ((1, SLICE, wide), jnp.float32), ((2, 4, SLICE, wide), jnp.float32)
    col_shape = ((count, 2 * WIDTH), jnp.bfloat16)
    return pl.pallas_call(
        forward_kernel,
        in_specs=[HBM] * 3 + [pl.BlockSpec()] * 4,
        out_specs=[HBM] * 3 + [pl.BlockSpec()],
        out_shape=(
            pltpu.HBM(*own_shape),
            pltpu.HBM(*part_shape),
            pltpu.HBM(*col_shape),
            jax.ShapeDtypeStruct((members, 2, rows), jnp.float32),
        ),
        scratch_shapes=[
            pltpu.VMEM((rows, 3 * WIDTH), jnp.bfloat16),
            pltpu.VMEM((wide, 2 * WIDTH), jnp.bfloat16),
            pltpu.VMEM(*col_shape),
            pltpu.VMEM(*own_shape),
            pltpu.VMEM(*part_shape),
            pltpu.VMEM((rows, 128), jnp.float32),
            pltpu.SemaphoreType.DMA((3,)),
            pltpu.SemaphoreType.DMA((2,)),
            pltpu.SemaphoreType.DMA,
            pltpu.SemaphoreType.DMA((4,)),
        ],
        cost_estimate=pl.CostEstimate(
            flops=6 * rows * count * WIDTH, bytes_accessed=4 * rows * count, transcendentals=rows * count
        ),
        compiler_params=params(VMEM_LARGE),
        name="forward",
    )(*map(in_hbm, (ready, c_own, ready_far)), line, got, got_sib, pos)


def denominator_kernel(member_ref, all_ref, row_ref, own_ref, line_ref, spread_ref):
    member = member_ref[0]
    members = all_ref.shape[0]

    def summed(owner, kind):
        value = 0.0
        for by, order in ((0, SELF), (2, 0), (members - 2, 1), (4, 3)):
            held = all_ref[lax.rem(owner + by, members)]
            value = value + held[kind : kind + 1, order * SLICE : order * SLICE + SLICE]
        return value

    mate = member + 1 - 2 * lax.rem(member, 2)
    own = summed(member, 0)
    line_ref[0:1] = own
    line_ref[1:2] = summed(member, 1)
    both = jnp.concatenate([own, summed(mate, 0)], axis=1)
    own_ref[...] = both
    spread_ref[...] = jnp.broadcast_to(both.reshape(1, 1, 2 * SLICE), spread_ref.shape)
    for order, by in enumerate((members - 2, 2, 0, 4)):
        value = own if by == 0 else summed(lax.rem(member + by, members), 0)
        row_ref[:, order * SLICE : order * SLICE + SLICE] = value


def denominators(member, everything, groups):
    return pl.pallas_call(
        denominator_kernel,
        in_specs=[SMEM, pl.BlockSpec()],
        out_shape=(
            jax.ShapeDtypeStruct((1, 4 * SLICE), jnp.float32),
            jax.ShapeDtypeStruct((1, 2 * SLICE), jnp.float32),
            jax.ShapeDtypeStruct((2, SLICE), jnp.float32),
            jax.ShapeDtypeStruct((groups, 1, 2 * SLICE), jnp.float32),
        ),
        compiler_params=params(),
        name="denominators",
    )(member, everything)


def backward_kernel(
    bands, partner_ref, row_ref, own_ref, everyone_ref, pos_ref, e0_in, e1_in, c0_in, c1_in, *refs
):
    out_refs, (run_ref, e_buf, c_buf, e_sem, c_sem) = refs[:-5], refs[-5:]
    wide = 2 * SLICE
    steps = e_buf.shape[0]
    copies = []
    for k in range(steps):
        wanted = pl.ds(k * wide, wide)
        group = []
        at = 0
        for which, (order, begin, size) in enumerate(bands):
            rows = pl.ds(begin, size)
            if k == 0:
                src = e0_in.at[order if e0_in.shape[0] > 1 else 0, rows]
            else:
                src = e1_in.at[k - 1, order, rows]
            group.append(pltpu.make_async_copy(src, e_buf.at[k, pl.ds(at, size)], e_sem.at[k, which]))
            at += size
        src = c0_in if k == 0 else c1_in.at[pl.ds((k - 1) * wide, wide)]
        group.append(pltpu.make_async_copy(src, c_buf.at[wanted], c_sem.at[k]))
        copies.append(group)
        for copy in group:
            copy.start()

    columns, places = [], []
    for order, begin, size in bands:
        column = as_column(row_ref[:, order * SLICE : order * SLICE + SLICE])
        columns.append(column[begin : begin + size])
        places.append(lax.broadcasted_iota(jnp.int32, (size, 128), 0) + (order * SLICE + begin))
    row_inv = 1.0 / jnp.concatenate(columns, axis=0)
    row_ids = jnp.concatenate(places, axis=0)
    for k in range(steps):
        col_inv = 1.0 / (own_ref[...] if k == 0 else everyone_ref[partner_ref[k - 1]])
        for copy in copies[k]:
            copy.wait()
        his, los = [], []
        for at in range(0, wide, 128):
            weight = e_buf[k, :, at : at + 128] * (row_inv + col_inv[:, at : at + 128])
            if k == 0:
                weight = weight - jnp.where(row_ids == pos_ref[:, at : at + 128], 2.0, 0.0)
            hi, lo = split(weight)
            his.append(hi)
            los.append(lo)
        cols = c_buf[k * wide : k * wide + wide]
        c_hi, c_lo = cols[:, :WIDTH], cols[:, WIDTH:]
        part = jnp.dot(
            jnp.concatenate(his + his + los, axis=1),
            jnp.concatenate([c_hi, c_lo, c_hi], axis=0),
            preferred_element_type=jnp.float32,
        )
        if k == 0:
            run_ref[...] = part
        elif k + 1 < steps:
            run_ref[...] += part
        else:
            part = run_ref[...] + part
            size = part.shape[0] // len(out_refs)
            for which, ref in enumerate(out_refs):
                ref[...] = part[which * size : which * size + size]


def backward(bands, pieces, e0, partners, row_den, own_den, everyone, pos, e1, c0, c1):
    count = 6 * SLICE
    return pl.pallas_call(
        functools.partial(backward_kernel, bands),
        in_specs=[SMEM] + [pl.BlockSpec()] * 4 + [HBM] * 4,
        out_shape=[jax.ShapeDtypeStruct((SLICE // pieces, WIDTH), jnp.float32)] * pieces,
        scratch_shapes=[
            pltpu.VMEM((SLICE, WIDTH), jnp.float32),
            pltpu.VMEM((3, SLICE, 2 * SLICE), jnp.float32),
            pltpu.VMEM((count, 2 * WIDTH), jnp.bfloat16),
            pltpu.SemaphoreType.DMA((3, len(bands))),
            pltpu.SemaphoreType.DMA((3,)),
        ],
        cost_estimate=pl.CostEstimate(
            flops=6 * SLICE * count * WIDTH, bytes_accessed=4 * SLICE * count, transcendentals=0
        ),
        compiler_params=params(VMEM_LARGE),
        name="backward_%d_%d" % bands[0][:2],
    )(partners, row_den, own_den, everyone, pos, *map(in_hbm, (e0, e1, c0, c1)))


def add_kernel(a_ref, b_ref, c_ref, d_ref, ab_ref, cd_ref):
    ab_ref[...] = a_ref[...] + b_ref[...]
    cd_ref[...] = c_ref[...] + d_ref[...]


def add_pairs(a, b, c, d):
    out = jax.ShapeDtypeStruct(a.shape, jnp.float32)
    return pl.pallas_call(add_kernel, out_shape=(out, out), compiler_params=params(), name="add_pairs")(
        a, b, c, d
    )


def finish_kernel(emb_ref, run_ref, low0, low1, high0, high1, line_ref, loss_ref, grad_ref):
    values = emb_ref[...]
    radius = radius_of(values)
    unit = values / radius
    low, high = low0[...] + low1[...], high0[...] + high1[...]
    slope = (run_ref[...] + jnp.concatenate([low, high], axis=0)) / LOGIT_DIVISOR
    grad_ref[...] = (slope - unit * jnp.sum(unit * slope, axis=-1, keepdims=True)) / radius
    loss_ref[...] = (jnp.log(line_ref[0:1]) - line_ref[1:2]).reshape(loss_ref.shape)


def finish(embeddings, run, lows, highs, line):
    rows, width = embeddings.shape
    return pl.pallas_call(
        finish_kernel,
        out_shape=(
            jax.ShapeDtypeStruct((rows,), jnp.float32),
            jax.ShapeDtypeStruct((rows, width), jnp.float32),
        ),
        compiler_params=params(),
        name="finish",
    )(embeddings, run, *lows, *highs, line)


def local(embeddings, positive, pairing):
    rows, width = embeddings.shape
    members = lax.axis_size("mem")
    groups = lax.axis_size("grp")
    block = rows * members
    rounds = pairing.shape[0]
    group = lax.axis_index("grp")
    member = lax.axis_index("mem")
    half = rows // 2

    def shift(value, by):
        return lax.ppermute(value, "mem", [(m, (m + by) % members) for m in range(members)])

    def swap(value):
        return lax.ppermute(value, "mem", [(m, m ^ 1) for m in range(members)])

    left, right = shift(embeddings, 2), shift(embeddings, -2)
    far = (shift(left[:half], 2), shift(right[half:], -2))
    per = rows * width // (groups * 128)
    pieces = lax.all_to_all(as_tiles(embeddings).reshape(groups, per, 128), "grp", 0, 0, tiled=True)
    ready = prepare("prepare", left, right, embeddings)
    picked, ready = lax.optimization_barrier((pick(pairing, pieces), ready))
    got = lax.all_to_all(picked, "grp", 0, 0, tiled=True)
    sib, pos_sib = swap(embeddings), swap(positive)

    both = jnp.concatenate([positive, pos_sib]) - group * block
    owner = both // rows
    turn = (owner // 2 - member // 2) % (members // 2)
    order = jnp.where(turn == 0, SELF, jnp.where(turn == 3, 0, jnp.where(turn == 1, 1, 3)))
    pos = jnp.where(owner % 2 == member % 2, order * rows + both % rows, -1).reshape(1, 2 * rows)

    c_own, e_own, line = own_scores(ready, embeddings, sib, pos)
    ready_far = prepare("prepare_far", *far)
    got, line, ready_far = lax.optimization_barrier((got, line, ready_far))
    e_far, e_part, c_part, line = forward(ready, c_own, ready_far, line, got, swap(got), pos, members)

    everything = lax.all_to_all(line, "mem", 0, 0, tiled=True)
    row_den, own_den, line, spread = denominators(jnp.reshape(member, (1,)), everything, groups)
    everyone = lax.all_to_all(spread, "grp", 0, 0, tiled=True)

    shared = (pairing[:, group], row_den, own_den, everyone, pos, e_part, c_own, c_part)
    far_low, far_high = backward(((3, 0, rows),), 2, e_far, *shared)
    far_low, far_high = shift(far_low, 2), shift(far_high, -2)
    left_low, right_high = backward(((0, 0, half), (1, half, half)), 2, e_own, *shared)
    high0, low1 = shift(right_high, 2), shift(left_low, -2)
    left_high, right_low = backward(((0, half, half), (1, 0, half)), 2, e_own, *shared)
    right_low, left_high = add_pairs(right_low, far_low, left_high, far_high)
    low0, high1 = shift(right_low, 2), shift(left_high, -2)
    (run,) = backward(((SELF, 0, rows),), 1, e_own, *shared)
    return finish(embeddings, run, (low0, low1), (high0, high1), line)


def solution(mesh):
    placed = (P(("grp", "mem"), None), P(("grp", "mem")), P())
    return jax.shard_map(
        local,
        mesh=mesh,
        in_specs=placed,
        out_specs=(P(("grp", "mem")), P(("grp", "mem"), None)),
        check_vma=False,
    )
```

```python
import functools

import jax
import jax.numpy as jnp
from jax import lax
from jax.experimental import pallas as pl
from jax.experimental.pallas import tpu as pltpu
from jax.sharding import PartitionSpec as P

LOGIT_DIVISOR = 0.1
EPSILON = 1e-06
SLICE = 384
WIDTH = 256
SELF = 2
VMEM = 16 * 1024 * 1024
VMEM_LARGE = 44 * 1024 * 1024
HBM = pl.BlockSpec(memory_space=pltpu.HBM)
SMEM = pl.BlockSpec(memory_space=pltpu.SMEM)


def split(values):
    hi = values.astype(jnp.bfloat16)
    lo = (values - hi.astype(jnp.float32)).astype(jnp.bfloat16)
    return hi, lo


def rows_of(tiles):
    pairs = tiles.reshape(tiles.shape[0] // 2, 2, 8, 128)
    rows = tiles.shape[0] * 4
    return jnp.concatenate([pairs[:, 0].reshape(rows, 128), pairs[:, 1].reshape(rows, 128)], axis=1)


def radius_of(values):
    return jnp.sqrt(jnp.sum(values * values, axis=-1, keepdims=True) + EPSILON)


def as_column(line):
    return jnp.broadcast_to(line, (128, line.shape[1])).T


def in_hbm(value):
    return pltpu.with_memory_space_constraint(value, pltpu.HBM)


def params(limit=VMEM):
    return pltpu.CompilerParams(vmem_limit_bytes=limit)


def tile_kernel(emb_ref, tile_ref):
    rows = emb_ref.shape[0]
    for half in range(2):
        tile_ref[:, half] = emb_ref[:, half * 128 : half * 128 + 128].reshape(rows // 8, 8, 128)


def as_tiles(embeddings):
    rows, _ = embeddings.shape
    return pl.pallas_call(
        tile_kernel,
        out_shape=jax.ShapeDtypeStruct((rows // 8, 2, 8, 128), jnp.float32),
        compiler_params=params(),
        name="as_tiles",
    )(embeddings)


def pick_kernel(pairing_ref, pieces_ref, out_ref):
    size = pieces_ref.shape[1]
    for which in range(out_ref.shape[1] // size):
        for group in range(out_ref.shape[0]):
            out_ref[group, which * size : which * size + size] = pieces_ref[pairing_ref[which, group]]


def pick(pairing, pieces):
    rounds, groups = pairing.shape
    return pl.pallas_call(
        pick_kernel,
        in_specs=[SMEM, pl.BlockSpec()],
        out_shape=jax.ShapeDtypeStruct((groups, rounds * pieces.shape[1], 128), jnp.float32),
        compiler_params=params(),
        name="pick",
    )(pairing, pieces)


def scaled_rows(refs, out_ref, at=0):
    for ref in refs:
        values = ref[...]
        hi, lo = split(values * (1.0 / (radius_of(values) * LOGIT_DIVISOR)))
        out_ref[at : at + hi.shape[0]] = jnp.concatenate([hi, lo, hi], axis=1)
        at += hi.shape[0]


def unit_parts(values):
    unit = values * (1.0 / radius_of(values))
    hi, lo = split(unit)
    hi_t, lo_t = split(unit.T)
    return jnp.concatenate([hi, lo], axis=1), jnp.concatenate([hi_t, hi_t, lo_t], axis=0)


def product(left, right):
    return jnp.dot(left, right, preferred_element_type=jnp.float32)


def exponentials(scores, first_row, pos_ref, store):
    height = scores.shape[0]
    total = jnp.zeros((height, 128), jnp.float32)
    match = jnp.zeros((height, 128), jnp.float32)
    if first_row is not None:
        row_ids = lax.broadcasted_iota(jnp.int32, (height, 128), 0) + first_row
        lane_ids = lax.broadcasted_iota(jnp.int32, (height, 128), 1)
    for k in range(0, scores.shape[1], 128):
        score = scores[:, k : k + 128]
        e = jnp.exp(score)
        if first_row is not None:
            match = match + jnp.where(row_ids == pos_ref[:, k : k + 128], score, 0.0)
            if first_row <= SELF * SLICE < first_row + height and k < SLICE:
                e = jnp.where(row_ids - SELF * SLICE == lane_ids + k, 0.0, e)
        total = total + e
        store(k, e)
    return total, match


def as_line(total):
    return jnp.sum(total.T, axis=0, keepdims=True)


def own_kernel(
    ready, ready_far, mine, sib, pos_ref, c_out, e_out, line_ref, left_ref, c_buf, right_ref, e_buf, in_sem, c_sem, e_sem
):
    at = ready.shape[0]
    ready_copies = [
        pltpu.make_async_copy(ready, left_ref.at[pl.ds(0, at)], in_sem.at[0]),
        pltpu.make_async_copy(ready_far, left_ref.at[pl.ds(at, SLICE)], in_sem.at[1]),
    ]
    for copy in ready_copies:
        copy.start()
    for which, ref in enumerate((mine, sib)):
        here = slice(which * SLICE, which * SLICE + SLICE)
        c_buf[here], right_ref[:, here] = unit_parts(ref[...])
    copies = [pltpu.make_async_copy(c_buf, c_out, c_sem)]
    copies[0].start()
    for copy in ready_copies:
        copy.wait()

    coming = product(left_ref[:SLICE], right_ref[...])
    totals, matches = [], []
    for order in range(4):
        scores = coming
        if order < 3:
            at = (order + 1) * SLICE
            coming = product(left_ref[at : at + SLICE], right_ref[...])

        def store(k, e):
            e_buf[order, :, k : k + 128] = e

        total, match = exponentials(scores, order * SLICE, pos_ref, store)
        totals.append(as_line(total))
        matches.append(as_line(match))
        copies.append(pltpu.make_async_copy(e_buf.at[order], e_out.at[order], e_sem.at[order]))
        copies[-1].start()
    line_ref[0:1] = jnp.concatenate(totals, axis=1)
    line_ref[1:2] = jnp.concatenate(matches, axis=1)
    for copy in copies:
        copy.wait()


def own_scores(ready, ready_far, mine, sib, pos):
    rows, wide = 4 * SLICE, 2 * SLICE
    shapes = [((wide, 2 * WIDTH), jnp.bfloat16), ((4, SLICE, wide), jnp.float32)]
    return pl.pallas_call(
        own_kernel,
        in_specs=[HBM] * 2 + [pl.BlockSpec()] * 3,
        out_specs=[HBM] * 2 + [pl.BlockSpec()],
        out_shape=[pltpu.HBM(*shape) for shape in shapes] + [jax.ShapeDtypeStruct((2, rows), jnp.float32)],
        scratch_shapes=[
            pltpu.VMEM((rows, 3 * WIDTH), jnp.bfloat16),
            pltpu.VMEM(*shapes[0]),
            pltpu.VMEM((3 * WIDTH, wide), jnp.bfloat16),
            pltpu.VMEM(*shapes[1]),
            pltpu.SemaphoreType.DMA((2,)),
            pltpu.SemaphoreType.DMA,
            pltpu.SemaphoreType.DMA((4,)),
        ],
        cost_estimate=pl.CostEstimate(
            flops=6 * rows * wide * WIDTH, bytes_accessed=4 * rows * wide, transcendentals=rows * wide
        ),
        compiler_params=params(VMEM_LARGE),
        name="own_scores",
    )(in_hbm(ready), in_hbm(ready_far), mine, sib, pos)


def prepare_kernel(*refs):
    pieces, (out_ref, buf, sem) = refs[:-3], refs[-3:]
    scaled_rows(pieces, buf)
    copy = pltpu.make_async_copy(buf, out_ref, sem)
    copy.start()
    copy.wait()


def prepare(name, *pieces):
    rows = sum(piece.shape[0] for piece in pieces)
    shape = ((rows, 3 * WIDTH), jnp.bfloat16)
    return pl.pallas_call(
        prepare_kernel,
        out_specs=HBM,
        out_shape=pltpu.HBM(*shape),
        scratch_shapes=[pltpu.VMEM(*shape), pltpu.SemaphoreType.DMA],
        cost_estimate=pl.CostEstimate(flops=20 * 10**9, bytes_accessed=8 * rows * WIDTH, transcendentals=0),
        compiler_params=params(),
        name=name,
    )(*pieces)


def forward_kernel(
    ready, ready_far, line_in, got, got_sib, e_out, c_out, line_ref,
    left_ref, c_buf, right_ref, e_buf, tot_ref, in_sem, c_sem, e_sem,
):
    chunks, orders, _, wide = e_buf.shape
    at = ready.shape[0]
    ready_copies = [
        pltpu.make_async_copy(ready, left_ref.at[pl.ds(0, at)], in_sem.at[0]),
        pltpu.make_async_copy(ready_far, left_ref.at[pl.ds(at, SLICE)], in_sem.at[1]),
    ]
    for copy in ready_copies:
        copy.start()
    half = got.shape[1] // 2
    tiles = got.shape[0] * half // 8
    copies = []

    def columns(chunk):
        for which, ref in enumerate((got, got_sib)):
            piece = rows_of(ref[:, chunk * half : chunk * half + half].reshape(tiles, 8, 128))
            here = slice(which * SLICE, which * SLICE + SLICE)
            c_buf[chunk, here], right_ref[chunk, :, here] = unit_parts(piece)
        copies.append(pltpu.make_async_copy(c_buf.at[chunk], c_out.at[chunk], c_sem.at[chunk]))
        copies[-1].start()

    def scores_of(chunk, band):
        return product(left_ref[band * wide : band * wide + wide], right_ref[chunk])

    columns(0)
    for copy in ready_copies:
        copy.wait()
    items = [(chunk, band) for chunk in range(chunks) for band in range(orders // 2)]
    coming = scores_of(*items[0])
    for turn, (chunk, band) in enumerate(items):
        scores = coming
        if turn + 1 < len(items):
            if items[turn + 1][0] != chunk:
                columns(items[turn + 1][0])
            coming = scores_of(*items[turn + 1])

        def store(k, e):
            e_buf[chunk, 2 * band : 2 * band + 2, :, k : k + 128] = e.reshape(2, SLICE, 128)

        total, _ = exponentials(scores, None, None, store)
        if chunk == 0:
            tot_ref[band * wide : band * wide + wide] = total
        else:
            tot_ref[band * wide : band * wide + wide] += total
        view = (chunk, pl.ds(2 * band, 2))
        copies.append(pltpu.make_async_copy(e_buf.at[view], e_out.at[view], e_sem.at[turn]))
        copies[-1].start()

    line_ref[0:1] = as_line(tot_ref[...]) + line_in[0:1]
    line_ref[1:2] = line_in[1:2]
    for copy in copies:
        copy.wait()


def forward(ready, ready_far, line, got, got_sib):
    rows, wide = 4 * SLICE, 2 * SLICE
    e_shape, c_shape = ((2, 4, SLICE, wide), jnp.float32), ((2, wide, 2 * WIDTH), jnp.bfloat16)
    return pl.pallas_call(
        forward_kernel,
        in_specs=[HBM] * 2 + [pl.BlockSpec()] * 3,
        out_specs=[HBM] * 2 + [pl.BlockSpec()],
        out_shape=(pltpu.HBM(*e_shape), pltpu.HBM(*c_shape), jax.ShapeDtypeStruct((2, rows), jnp.float32)),
        scratch_shapes=[
            pltpu.VMEM((rows, 3 * WIDTH), jnp.bfloat16),
            pltpu.VMEM(*c_shape),
            pltpu.VMEM((2, 3 * WIDTH, wide), jnp.bfloat16),
            pltpu.VMEM(*e_shape),
            pltpu.VMEM((rows, 128), jnp.float32),
            pltpu.SemaphoreType.DMA((2,)),
            pltpu.SemaphoreType.DMA((2,)),
            pltpu.SemaphoreType.DMA((4,)),
        ],
        cost_estimate=pl.CostEstimate(
            flops=12 * rows * wide * WIDTH, bytes_accessed=8 * rows * wide, transcendentals=2 * rows * wide
        ),
        compiler_params=params(VMEM_LARGE),
        name="forward",
    )(in_hbm(ready), in_hbm(ready_far), line, got, got_sib)


def denominator_kernel(mine, at_left, at_right, at_far, row_ref, line_ref):
    def part(ref, order):
        return ref[:, order * SLICE : order * SLICE + SLICE]

    for order, (a, b, c) in enumerate(((2, 3, 1), (3, 2, 0), (1, 0, 3), (0, 1, 2))):
        value = (part(mine, order) + part(at_left, a)) + (part(at_right, b) + part(at_far, c))
        row_ref[:, order * SLICE : order * SLICE + SLICE] = value[0:1]
        if order == SELF:
            line_ref[...] = value


def denominators(*lines):
    return pl.pallas_call(
        denominator_kernel,
        out_shape=(
            jax.ShapeDtypeStruct((1, 4 * SLICE), jnp.float32),
            jax.ShapeDtypeStruct((2, SLICE), jnp.float32),
        ),
        compiler_params=params(),
        name="denominators",
    )(*lines)


def spread_kernel(line_ref, sib_ref, own_ref, spread_ref):
    both = jnp.concatenate([line_ref[0:1], sib_ref[0:1]], axis=1)
    own_ref[...] = both
    spread_ref[...] = jnp.broadcast_to(both.reshape(1, 1, 2 * SLICE), spread_ref.shape)


def spread(line, sib, groups):
    return pl.pallas_call(
        spread_kernel,
        out_shape=(
            jax.ShapeDtypeStruct((1, 2 * SLICE), jnp.float32),
            jax.ShapeDtypeStruct((groups, 1, 2 * SLICE), jnp.float32),
        ),
        compiler_params=params(),
        name="spread",
    )(line, sib)


def backward_kernel(
    bands, partner_ref, row_ref, own_ref, everyone_ref, pos_ref, e0_in, e1_in, c0_in, c1_in, *refs
):
    out_refs, (run_ref, e_buf, c_buf, e_sem, c_sem) = refs[:-5], refs[-5:]
    wide = 2 * SLICE
    steps = e_buf.shape[0]
    copies = []
    for k in range(steps):
        group = []
        at = 0
        for which, (order, begin, size) in enumerate(bands):
            rows = pl.ds(begin, size)
            if k == 0:
                src = e0_in.at[order, rows]
            else:
                src = e1_in.at[k - 1, order, rows]
            group.append(pltpu.make_async_copy(src, e_buf.at[k, pl.ds(at, size)], e_sem.at[k, which]))
            at += size
        src = c0_in if k == 0 else c1_in.at[k - 1]
        group.append(pltpu.make_async_copy(src, c_buf.at[k], c_sem.at[k]))
        copies.append(group)
        for copy in group:
            copy.start()

    columns, places = [], []
    for order, begin, size in bands:
        column = as_column(row_ref[:, order * SLICE : order * SLICE + SLICE])
        columns.append(column[begin : begin + size])
        places.append(lax.broadcasted_iota(jnp.int32, (size, 128), 0) + (order * SLICE + begin))
    row_inv = 1.0 / jnp.concatenate(columns, axis=0)
    row_ids = jnp.concatenate(places, axis=0)
    for k in range(steps):
        col_inv = 1.0 / (own_ref[...] if k == 0 else everyone_ref[partner_ref[k - 1]])
        for copy in copies[k]:
            copy.wait()
        his, los = [], []
        for at in range(0, wide, 128):
            weight = e_buf[k, :, at : at + 128] * (row_inv + col_inv[:, at : at + 128])
            if k == 0:
                weight = weight - jnp.where(row_ids == pos_ref[:, at : at + 128], 2.0, 0.0)
            hi, lo = split(weight)
            his.append(hi)
            los.append(lo)
        both = product(jnp.concatenate(his, axis=1), c_buf[k])
        part = both[:, :WIDTH] + both[:, WIDTH:]
        part = part + product(jnp.concatenate(los, axis=1), c_buf[k, :, :WIDTH])
        if k == 0:
            run_ref[...] = part
        elif k + 1 < steps:
            run_ref[...] += part
        else:
            part = run_ref[...] + part
            size = part.shape[0] // len(out_refs)
            for which, ref in enumerate(out_refs):
                ref[...] = part[which * size : which * size + size]


def backward(bands, pieces, e0, partners, row_den, own_den, everyone, pos, e1, c0, c1):
    count = 6 * SLICE
    return pl.pallas_call(
        functools.partial(backward_kernel, bands),
        in_specs=[SMEM] + [pl.BlockSpec()] * 4 + [HBM] * 4,
        out_shape=[jax.ShapeDtypeStruct((SLICE // pieces, WIDTH), jnp.float32)] * pieces,
        scratch_shapes=[
            pltpu.VMEM((SLICE, WIDTH), jnp.float32),
            pltpu.VMEM((3, SLICE, 2 * SLICE), jnp.float32),
            pltpu.VMEM((3, 2 * SLICE, 2 * WIDTH), jnp.bfloat16),
            pltpu.SemaphoreType.DMA((3, len(bands))),
            pltpu.SemaphoreType.DMA((3,)),
        ],
        cost_estimate=pl.CostEstimate(
            flops=6 * SLICE * count * WIDTH, bytes_accessed=4 * SLICE * count, transcendentals=0
        ),
        compiler_params=params(VMEM_LARGE),
        name="backward_%d_%d" % bands[0][:2],
    )(partners, row_den, own_den, everyone, pos, *map(in_hbm, (e0, e1, c0, c1)))


def add_kernel(a_ref, b_ref, c_ref, d_ref, ab_ref, cd_ref):
    ab_ref[...] = a_ref[...] + b_ref[...]
    cd_ref[...] = c_ref[...] + d_ref[...]


def add_pairs(a, b, c, d):
    out = jax.ShapeDtypeStruct(a.shape, jnp.float32)
    return pl.pallas_call(add_kernel, out_shape=(out, out), compiler_params=params(), name="add_pairs")(
        a, b, c, d
    )


def finish_kernel(emb_ref, run_ref, low0, low1, high0, high1, line_ref, loss_ref, grad_ref):
    values = emb_ref[...]
    radius = radius_of(values)
    unit = values / radius
    low, high = low0[...] + low1[...], high0[...] + high1[...]
    slope = (run_ref[...] + jnp.concatenate([low, high], axis=0)) / LOGIT_DIVISOR
    grad_ref[...] = (slope - unit * jnp.sum(unit * slope, axis=-1, keepdims=True)) / radius
    loss_ref[...] = (jnp.log(line_ref[0:1]) - line_ref[1:2]).reshape(loss_ref.shape)


def finish(embeddings, run, lows, highs, line):
    rows, width = embeddings.shape
    return pl.pallas_call(
        finish_kernel,
        out_shape=(
            jax.ShapeDtypeStruct((rows,), jnp.float32),
            jax.ShapeDtypeStruct((rows, width), jnp.float32),
        ),
        compiler_params=params(),
        name="finish",
    )(embeddings, run, *lows, *highs, line)


def local(embeddings, positive, pairing):
    rows, width = embeddings.shape
    members = lax.axis_size("mem")
    groups = lax.axis_size("grp")
    block = rows * members
    rounds = pairing.shape[0]
    group = lax.axis_index("grp")
    member = lax.axis_index("mem")
    half = rows // 2

    def shift(value, by):
        return lax.ppermute(value, "mem", [(m, (m + by) % members) for m in range(members)])

    def swap(value):
        return lax.ppermute(value, "mem", [(m, m ^ 1) for m in range(members)])

    left, right = shift(embeddings, 2), shift(embeddings, -2)
    far = (shift(left[:half], 2), shift(right[half:], -2))
    per = rows * width // (groups * 128)
    pieces = lax.all_to_all(as_tiles(embeddings).reshape(groups, per, 128), "grp", 0, 0, tiled=True)
    ready = prepare("prepare", left, right, embeddings)
    picked, ready = lax.optimization_barrier((pick(pairing, pieces), ready))
    got = lax.all_to_all(picked, "grp", 0, 0, tiled=True)
    sib, pos_sib = swap(embeddings), swap(positive)

    both = jnp.concatenate([positive, pos_sib]) - group * block
    owner = both // rows
    turn = (owner // 2 - member // 2) % (members // 2)
    order = jnp.where(turn == 0, SELF, jnp.where(turn == 3, 0, jnp.where(turn == 1, 1, 3)))
    pos = jnp.where(owner % 2 == member % 2, order * rows + both % rows, -1).reshape(1, 2 * rows)

    ready_far = prepare("prepare_far", *far)
    c_own, e_own, line = own_scores(ready, ready_far, embeddings, sib, pos)
    got, line = lax.optimization_barrier((got, line))
    e_part, c_part, line = forward(ready, ready_far, line, got, swap(got))

    row_den, line = denominators(line, shift(line, 2), shift(line, -2), shift(line, 4))
    own_den, spread_den = spread(line, swap(line), groups)
    everyone = lax.all_to_all(spread_den, "grp", 0, 0, tiled=True)

    shared = (e_own, pairing[:, group], row_den, own_den, everyone, pos, e_part, c_own, c_part)
    far_low, far_high = backward(((3, 0, rows),), 2, *shared)
    far_low, far_high = shift(far_low, 2), shift(far_high, -2)
    left_low, right_high = backward(((0, 0, half), (1, half, half)), 2, *shared)
    high0, low1 = shift(right_high, 2), shift(left_low, -2)
    left_high, right_low = backward(((0, half, half), (1, 0, half)), 2, *shared)
    right_low, left_high = add_pairs(right_low, far_low, left_high, far_high)
    low0, high1 = shift(right_low, 2), shift(left_high, -2)
    (run,) = backward(((SELF, 0, rows),), 1, *shared)
    return finish(embeddings, run, (low0, low1), (high0, high1), line)


def solution(mesh):
    placed = (P(("grp", "mem"), None), P(("grp", "mem")), P())
    return jax.shard_map(
        local,
        mesh=mesh,
        in_specs=placed,
        out_specs=(P(("grp", "mem")), P(("grp", "mem"), None)),
        check_vma=False,
    )
```

```python
import functools

import jax
import jax.numpy as jnp
from jax import lax
from jax.experimental import pallas as pl
from jax.experimental.pallas import tpu as pltpu
from jax.sharding import PartitionSpec as P

LOGIT_DIVISOR = 0.1
EPSILON = 1e-06
SLICE = 384
WIDTH = 256
SELF = 2
PIECE = 256
STEPS = ((0, 2), (2, 3), (5, 3), (8, 1))
VMEM = 16 * 1024 * 1024
VMEM_LARGE = 44 * 1024 * 1024
VMEM_BACKWARD = 28 * 1024 * 1024
HBM = pl.BlockSpec(memory_space=pltpu.HBM)
SMEM = pl.BlockSpec(memory_space=pltpu.SMEM)


def split(values):
    hi = values.astype(jnp.bfloat16)
    lo = (values - hi.astype(jnp.float32)).astype(jnp.bfloat16)
    return hi, lo


def rows_of(tiles):
    pairs = tiles.reshape(tiles.shape[0] // 2, 2, 8, 128)
    rows = tiles.shape[0] * 4
    return jnp.concatenate([pairs[:, 0].reshape(rows, 128), pairs[:, 1].reshape(rows, 128)], axis=1)


def radius_of(values):
    return jnp.sqrt(jnp.sum(values * values, axis=-1, keepdims=True) + EPSILON)


def as_column(line):
    return jnp.broadcast_to(line, (128, line.shape[1])).T


def in_hbm(value):
    return pltpu.with_memory_space_constraint(value, pltpu.HBM)


def params(limit=VMEM):
    return pltpu.CompilerParams(vmem_limit_bytes=limit)


def tile_kernel(emb_ref, tile_ref):
    rows = emb_ref.shape[0]
    for half in range(2):
        tile_ref[:, half] = emb_ref[:, half * 128 : half * 128 + 128].reshape(rows // 8, 8, 128)


def as_tiles(embeddings):
    rows, _ = embeddings.shape
    return pl.pallas_call(
        tile_kernel,
        out_shape=jax.ShapeDtypeStruct((rows // 8, 2, 8, 128), jnp.float32),
        compiler_params=params(),
        name="as_tiles",
    )(embeddings)


def pick_kernel(pairing_ref, pieces_ref, out_ref):
    size = pieces_ref.shape[1]
    for which in range(out_ref.shape[1] // size):
        for group in range(out_ref.shape[0]):
            out_ref[group, which * size : which * size + size] = pieces_ref[pairing_ref[which, group]]


def pick(pairing, pieces):
    rounds, groups = pairing.shape
    return pl.pallas_call(
        pick_kernel,
        in_specs=[SMEM, pl.BlockSpec()],
        out_shape=jax.ShapeDtypeStruct((groups, rounds * pieces.shape[1], 128), jnp.float32),
        compiler_params=params(),
        name="pick",
    )(pairing, pieces)


def scaled_rows(refs, out_ref, at=0):
    for ref in refs:
        values = ref[...]
        hi, lo = split(values * (1.0 / (radius_of(values) * LOGIT_DIVISOR)))
        out_ref[at : at + hi.shape[0]] = jnp.concatenate([hi, lo, hi], axis=1)
        at += hi.shape[0]


def unit_parts(values):
    hi, lo = split(values * (1.0 / radius_of(values)))
    return jnp.concatenate([hi, lo], axis=1)


def product(left, cols):
    hi, lo = cols[:, :WIDTH], cols[:, WIDTH:]
    return lax.dot_general(
        left,
        jnp.concatenate([hi, hi, lo], axis=1),
        (((1,), (1,)), ((), ())),
        preferred_element_type=jnp.float32,
    )


def exponentials(scores, first_row, pos_ref, store):
    height = scores.shape[0]
    total = jnp.zeros((height, 128), jnp.float32)
    match = jnp.zeros((height, 128), jnp.float32)
    if first_row is not None:
        row_ids = lax.broadcasted_iota(jnp.int32, (height, 128), 0) + first_row
        lane_ids = lax.broadcasted_iota(jnp.int32, (height, 128), 1)
    for k in range(0, scores.shape[1], 128):
        score = scores[:, k : k + 128]
        e = jnp.exp(score)
        if first_row is not None:
            match = match + jnp.where(row_ids == pos_ref[:, k : k + 128], score, 0.0)
            if first_row <= SELF * SLICE < first_row + height and k < SLICE:
                e = jnp.where(row_ids - SELF * SLICE == lane_ids + k, 0.0, e)
        total = total + e
        store(k, e)
    return total, match


def as_line(total):
    return jnp.sum(total.T, axis=0, keepdims=True)


def put_columns(c_buf, at, parts):
    done = 0
    while done < parts.shape[0]:
        inside = (at + done) % PIECE
        size = min(PIECE - inside, parts.shape[0] - done)
        c_buf[(at + done) // PIECE, inside : inside + size] = parts[done : done + size]
        done += size


def own_kernel(
    ready, ready_far, mine, sib, pos_ref, c_out, e_out, line_ref, left_ref, c_buf, e_buf, in_sem, c_sem, e_sem
):
    at = ready.shape[0]
    ready_copies = [
        pltpu.make_async_copy(ready, left_ref.at[pl.ds(0, at)], in_sem.at[0]),
        pltpu.make_async_copy(ready_far, left_ref.at[pl.ds(at, SLICE)], in_sem.at[1]),
    ]
    for copy in ready_copies:
        copy.start()
    for which, ref in enumerate((mine, sib)):
        put_columns(c_buf, which * SLICE, unit_parts(ref[...]))
    cols = c_buf[...].reshape(2 * SLICE, 2 * WIDTH)
    copies = [pltpu.make_async_copy(c_buf, c_out, c_sem)]
    copies[0].start()
    for copy in ready_copies:
        copy.wait()

    coming = product(left_ref[:SLICE], cols)
    totals, matches = [], []
    for order in range(4):
        scores = coming
        if order < 3:
            at = (order + 1) * SLICE
            coming = product(left_ref[at : at + SLICE], cols)

        def store(k, e):
            e_buf[k // PIECE, order, :, k % PIECE : k % PIECE + 128] = e

        total, match = exponentials(scores, order * SLICE, pos_ref, store)
        totals.append(as_line(total))
        matches.append(as_line(match))
        copies.append(pltpu.make_async_copy(e_buf.at[:, order], e_out.at[:, order], e_sem.at[order]))
        copies[-1].start()
    line_ref[0:1] = jnp.concatenate(totals, axis=1)
    line_ref[1:2] = jnp.concatenate(matches, axis=1)
    for copy in copies:
        copy.wait()


def own_scores(ready, ready_far, mine, sib, pos):
    rows, wide = 4 * SLICE, 2 * SLICE
    shapes = [((3, PIECE, 2 * WIDTH), jnp.bfloat16), ((3, 4, SLICE, PIECE), jnp.float32)]
    return pl.pallas_call(
        own_kernel,
        in_specs=[HBM] * 2 + [pl.BlockSpec()] * 3,
        out_specs=[HBM] * 2 + [pl.BlockSpec()],
        out_shape=[pltpu.HBM(*shape) for shape in shapes] + [jax.ShapeDtypeStruct((2, rows), jnp.float32)],
        scratch_shapes=[
            pltpu.VMEM((rows, 3 * WIDTH), jnp.bfloat16),
            pltpu.VMEM(*shapes[0]),
            pltpu.VMEM(*shapes[1]),
            pltpu.SemaphoreType.DMA((2,)),
            pltpu.SemaphoreType.DMA,
            pltpu.SemaphoreType.DMA((4,)),
        ],
        cost_estimate=pl.CostEstimate(
            flops=6 * rows * wide * WIDTH, bytes_accessed=4 * rows * wide, transcendentals=rows * wide
        ),
        compiler_params=params(VMEM_LARGE),
        name="own_scores",
    )(in_hbm(ready), in_hbm(ready_far), mine, sib, pos)


def prepare_kernel(*refs):
    pieces, (out_ref, buf, sem) = refs[:-3], refs[-3:]
    scaled_rows(pieces, buf)
    copy = pltpu.make_async_copy(buf, out_ref, sem)
    copy.start()
    copy.wait()


def prepare(name, *pieces):
    rows = sum(piece.shape[0] for piece in pieces)
    shape = ((rows, 3 * WIDTH), jnp.bfloat16)
    return pl.pallas_call(
        prepare_kernel,
        out_specs=HBM,
        out_shape=pltpu.HBM(*shape),
        scratch_shapes=[pltpu.VMEM(*shape), pltpu.SemaphoreType.DMA],
        cost_estimate=pl.CostEstimate(flops=20 * 10**9, bytes_accessed=8 * rows * WIDTH, transcendentals=0),
        compiler_params=params(),
        name=name,
    )(*pieces)


def forward_kernel(
    ready, ready_far, line_in, got, got_sib, e_out, c_out, line_ref,
    left_ref, c_buf, e_buf, tot_ref, in_sem, c_sem, e_sem,
):
    orders, wide = e_buf.shape[1], 2 * SLICE
    many = wide // PIECE
    chunks = e_buf.shape[0] // many
    at = ready.shape[0]
    ready_copies = [
        pltpu.make_async_copy(ready, left_ref.at[pl.ds(0, at)], in_sem.at[0]),
        pltpu.make_async_copy(ready_far, left_ref.at[pl.ds(at, SLICE)], in_sem.at[1]),
    ]
    for copy in ready_copies:
        copy.start()
    half = got.shape[1] // 2
    tiles = got.shape[0] * half // 8
    copies = []

    def columns(chunk):
        for which, ref in enumerate((got, got_sib)):
            piece = rows_of(ref[:, chunk * half : chunk * half + half].reshape(tiles, 8, 128))
            put_columns(c_buf, chunk * wide + which * SLICE, unit_parts(piece))
        view = (pl.ds(chunk * many, many),)
        copies.append(pltpu.make_async_copy(c_buf.at[view], c_out.at[view], c_sem.at[chunk]))
        copies[-1].start()

    def scores_of(chunk, band):
        cols = c_buf[chunk * many : chunk * many + many].reshape(wide, 2 * WIDTH)
        return product(left_ref[band * wide : band * wide + wide], cols)

    columns(0)
    for copy in ready_copies:
        copy.wait()
    items = [(chunk, band) for chunk in range(chunks) for band in range(orders // 2)]
    coming = scores_of(*items[0])
    for turn, (chunk, band) in enumerate(items):
        scores = coming
        if turn + 1 < len(items):
            if items[turn + 1][0] != chunk:
                columns(items[turn + 1][0])
            coming = scores_of(*items[turn + 1])

        def store(k, e):
            lane = k % PIECE
            e = e.reshape(2, SLICE, 128)
            e_buf[chunk * many + k // PIECE, 2 * band : 2 * band + 2, :, lane : lane + 128] = e

        total, _ = exponentials(scores, None, None, store)
        if chunk == 0:
            tot_ref[band * wide : band * wide + wide] = total
        else:
            tot_ref[band * wide : band * wide + wide] += total
        view = (pl.ds(chunk * many, many), pl.ds(2 * band, 2))
        copies.append(pltpu.make_async_copy(e_buf.at[view], e_out.at[view], e_sem.at[turn]))
        copies[-1].start()

    total = as_line(tot_ref[...]) + line_in[0:1]
    for member in range(line_ref.shape[0]):
        line_ref[member, 0:1] = total
        line_ref[member, 1:2] = line_in[1:2]
    for copy in copies:
        copy.wait()


def forward(ready, ready_far, line, got, got_sib, members):
    rows, wide = 4 * SLICE, 2 * SLICE
    e_shape, c_shape = ((6, 4, SLICE, PIECE), jnp.float32), ((6, PIECE, 2 * WIDTH), jnp.bfloat16)
    return pl.pallas_call(
        forward_kernel,
        in_specs=[HBM] * 2 + [pl.BlockSpec()] * 3,
        out_specs=[HBM] * 2 + [pl.BlockSpec()],
        out_shape=(
            pltpu.HBM(*e_shape),
            pltpu.HBM(*c_shape),
            jax.ShapeDtypeStruct((members, 2, rows), jnp.float32),
        ),
        scratch_shapes=[
            pltpu.VMEM((rows, 3 * WIDTH), jnp.bfloat16),
            pltpu.VMEM(*c_shape),
            pltpu.VMEM(*e_shape),
            pltpu.VMEM((rows, 128), jnp.float32),
            pltpu.SemaphoreType.DMA((2,)),
            pltpu.SemaphoreType.DMA((2,)),
            pltpu.SemaphoreType.DMA((4,)),
        ],
        cost_estimate=pl.CostEstimate(
            flops=12 * rows * wide * WIDTH, bytes_accessed=8 * rows * wide, transcendentals=2 * rows * wide
        ),
        compiler_params=params(VMEM_LARGE),
        name="forward",
    )(in_hbm(ready), in_hbm(ready_far), line, got, got_sib)


def denominator_kernel(member_ref, all_ref, row_ref, own_ref, line_ref, spread_ref):
    member = member_ref[0]
    members = all_ref.shape[0]

    def summed(owner, kind):
        value = 0.0
        for by, order in ((0, SELF), (2, 0), (members - 2, 1), (4, 3)):
            held = all_ref[lax.rem(owner + by, members)]
            value = value + held[kind : kind + 1, order * SLICE : order * SLICE + SLICE]
        return value

    mate = member + 1 - 2 * lax.rem(member, 2)
    own = summed(member, 0)
    line_ref[0:1] = own
    line_ref[1:2] = summed(member, 1)
    both = jnp.concatenate([own, summed(mate, 0)], axis=1)
    own_ref[...] = both
    spread_ref[...] = jnp.broadcast_to(both.reshape(1, 1, 2 * SLICE), spread_ref.shape)
    for order, by in enumerate((members - 2, 2, 0, 4)):
        value = own if by == 0 else summed(lax.rem(member + by, members), 0)
        row_ref[:, order * SLICE : order * SLICE + SLICE] = value


def denominators(member, everything, groups):
    return pl.pallas_call(
        denominator_kernel,
        in_specs=[SMEM, pl.BlockSpec()],
        out_shape=(
            jax.ShapeDtypeStruct((1, 4 * SLICE), jnp.float32),
            jax.ShapeDtypeStruct((1, 2 * SLICE), jnp.float32),
            jax.ShapeDtypeStruct((2, SLICE), jnp.float32),
            jax.ShapeDtypeStruct((groups, 1, 2 * SLICE), jnp.float32),
        ),
        compiler_params=params(),
        name="denominators",
    )(member, everything)


def backward_kernel(
    bands, first, partner_ref, row_ref, own_ref, everyone_ref, pos_ref, e0_in, e1_in, *refs
):
    if first:
        c0_in, c1_in, c_ref, refs = refs[0], refs[1], refs[2], refs[3:]
    else:
        c_ref, refs = refs[0], refs[1:]
    out_refs, (run_ref, e_buf, e_sem, c_sem) = refs[:-4], refs[-4:]
    own_pieces = e0_in.shape[0]
    copies = []
    for step, (start, many) in enumerate(STEPS):
        group = []
        for k, (source, low, high) in enumerate(
            ((0, 0, own_pieces), (1, own_pieces, own_pieces + e1_in.shape[0]))
        ):
            begin, end = max(start, low), min(start + many, high)
            if begin >= end:
                continue
            here, there = pl.ds(begin, end - begin), pl.ds(begin - low, end - begin)
            at = 0
            for which, (order, row, size) in enumerate(bands):
                group.append(
                    pltpu.make_async_copy(
                        (e0_in, e1_in)[source].at[there, order, pl.ds(row, size)],
                        e_buf.at[here, pl.ds(at, size)],
                        e_sem.at[step, k, which],
                    )
                )
                at += size
            if first:
                src = (c0_in, c1_in)[source].at[there]
                group.append(pltpu.make_async_copy(src, c_ref.at[here], c_sem.at[step, k]))
        copies.append(group)
        for copy in group:
            copy.start()

    columns, places = [], []
    for order, row, size in bands:
        column = as_column(row_ref[:, order * SLICE : order * SLICE + SLICE])
        columns.append(column[row : row + size])
        places.append(lax.broadcasted_iota(jnp.int32, (size, 128), 0) + (order * SLICE + row))
    row_inv = 1.0 / jnp.concatenate(columns, axis=0)
    row_ids = jnp.concatenate(places, axis=0)
    wide = 2 * SLICE
    col_inv = [1.0 / own_ref[...]] + [1.0 / everyone_ref[partner_ref[k]] for k in range(2)]
    for step, (start, many) in enumerate(STEPS):
        for copy in copies[step]:
            copy.wait()
        his, los = [], []
        for at in range(start * PIECE, (start + many) * PIECE, 128):
            inv = col_inv[at // wide][:, at % wide : at % wide + 128]
            weight = e_buf[at // PIECE, :, at % PIECE : at % PIECE + 128] * (row_inv + inv)
            if at < wide:
                weight = weight - jnp.where(row_ids == pos_ref[:, at : at + 128], 2.0, 0.0)
            hi, lo = split(weight)
            his.append(hi)
            los.append(lo)
        cols = c_ref[start : start + many].reshape(many * PIECE, 2 * WIDTH)
        c_hi, c_lo = cols[:, :WIDTH], cols[:, WIDTH:]
        part = jnp.dot(
            jnp.concatenate(his + his + los, axis=1),
            jnp.concatenate([c_hi, c_lo, c_hi], axis=0),
            preferred_element_type=jnp.float32,
        )
        if step == 0:
            run_ref[...] = part
        elif step + 1 < len(STEPS):
            run_ref[...] += part
        else:
            part = run_ref[...] + part
            size = part.shape[0] // len(out_refs)
            for which, ref in enumerate(out_refs):
                ref[...] = part[which * size : which * size + size]


def backward(bands, pieces, partners, row_den, own_den, everyone, pos, e0, e1, *cols):
    first = len(cols) == 2
    count = 9 * PIECE
    col_shape = [jax.ShapeDtypeStruct((9, PIECE, 2 * WIDTH), jnp.bfloat16)]
    return pl.pallas_call(
        functools.partial(backward_kernel, bands, first),
        in_specs=[SMEM] + [pl.BlockSpec()] * 4 + [HBM] * 2 + ([HBM] * 2 if first else [pl.BlockSpec()]),
        out_shape=col_shape * first + [jax.ShapeDtypeStruct((SLICE // pieces, WIDTH), jnp.float32)] * pieces,
        scratch_shapes=[
            pltpu.VMEM((SLICE, WIDTH), jnp.float32),
            pltpu.VMEM((9, SLICE, PIECE), jnp.float32),
            pltpu.SemaphoreType.DMA((len(STEPS), 2, len(bands))),
            pltpu.SemaphoreType.DMA((len(STEPS), 2)),
        ],
        cost_estimate=pl.CostEstimate(
            flops=6 * SLICE * count * WIDTH, bytes_accessed=4 * SLICE * count, transcendentals=0
        ),
        compiler_params=params(VMEM_BACKWARD),
        name="backward_%d_%d" % bands[0][:2],
    )(partners, row_den, own_den, everyone, pos, in_hbm(e0), in_hbm(e1), *(map(in_hbm, cols) if first else cols))


def add_kernel(a_ref, b_ref, c_ref, d_ref, ab_ref, cd_ref):
    ab_ref[...] = a_ref[...] + b_ref[...]
    cd_ref[...] = c_ref[...] + d_ref[...]


def add_pairs(a, b, c, d):
    out = jax.ShapeDtypeStruct(a.shape, jnp.float32)
    return pl.pallas_call(add_kernel, out_shape=(out, out), compiler_params=params(), name="add_pairs")(
        a, b, c, d
    )


def finish_kernel(emb_ref, run_ref, low0, low1, high0, high1, line_ref, loss_ref, grad_ref):
    values = emb_ref[...]
    radius = radius_of(values)
    unit = values / radius
    low, high = low0[...] + low1[...], high0[...] + high1[...]
    slope = (run_ref[...] + jnp.concatenate([low, high], axis=0)) / LOGIT_DIVISOR
    grad_ref[...] = (slope - unit * jnp.sum(unit * slope, axis=-1, keepdims=True)) / radius
    loss_ref[...] = (jnp.log(line_ref[0:1]) - line_ref[1:2]).reshape(loss_ref.shape)


def finish(embeddings, run, lows, highs, line):
    rows, width = embeddings.shape
    return pl.pallas_call(
        finish_kernel,
        out_shape=(
            jax.ShapeDtypeStruct((rows,), jnp.float32),
            jax.ShapeDtypeStruct((rows, width), jnp.float32),
        ),
        compiler_params=params(),
        name="finish",
    )(embeddings, run, *lows, *highs, line)


def local(embeddings, positive, pairing):
    rows, width = embeddings.shape
    members = lax.axis_size("mem")
    groups = lax.axis_size("grp")
    block = rows * members
    rounds = pairing.shape[0]
    group = lax.axis_index("grp")
    member = lax.axis_index("mem")
    half = rows // 2

    def shift(value, by):
        return lax.ppermute(value, "mem", [(m, (m + by) % members) for m in range(members)])

    def swap(value):
        return lax.ppermute(value, "mem", [(m, m ^ 1) for m in range(members)])

    left, right = shift(embeddings, 2), shift(embeddings, -2)
    far = (shift(left[:half], 2), shift(right[half:], -2))
    per = rows * width // (groups * 128)
    pieces = lax.all_to_all(as_tiles(embeddings).reshape(groups, per, 128), "grp", 0, 0, tiled=True)
    ready = prepare("prepare", left, right, embeddings)
    picked, ready = lax.optimization_barrier((pick(pairing, pieces), ready))
    got = lax.all_to_all(picked, "grp", 0, 0, tiled=True)
    sib, pos_sib = swap(embeddings), swap(positive)

    both = jnp.concatenate([positive, pos_sib]) - group * block
    owner = both // rows
    turn = (owner // 2 - member // 2) % (members // 2)
    order = jnp.where(turn == 0, SELF, jnp.where(turn == 3, 0, jnp.where(turn == 1, 1, 3)))
    pos = jnp.where(owner % 2 == member % 2, order * rows + both % rows, -1).reshape(1, 2 * rows)

    ready_far = prepare("prepare_far", *far)
    c_own, e_own, line = own_scores(ready, ready_far, embeddings, sib, pos)
    got, line = lax.optimization_barrier((got, line))
    e_part, c_part, line = forward(ready, ready_far, line, got, swap(got), members)

    everything = lax.all_to_all(line, "mem", 0, 0, tiled=True)
    row_den, own_den, line, spread = denominators(jnp.reshape(member, (1,)), everything, groups)
    everyone = lax.all_to_all(spread, "grp", 0, 0, tiled=True)

    shared = (pairing[:, group], row_den, own_den, everyone, pos, e_own, e_part)
    cols, far_low, far_high = backward(((3, 0, rows),), 2, *shared, c_own, c_part)
    shared += (cols,)
    far_low, far_high = shift(far_low, 2), shift(far_high, -2)
    left_low, right_high = backward(((0, 0, half), (1, half, half)), 2, *shared)
    high0, low1 = shift(right_high, 2), shift(left_low, -2)
    left_high, right_low = backward(((0, half, half), (1, 0, half)), 2, *shared)
    right_low, left_high = add_pairs(right_low, far_low, left_high, far_high)
    low0, high1 = shift(right_low, 2), shift(left_high, -2)
    (run,) = backward(((SELF, 0, rows),), 1, *shared)
    return finish(embeddings, run, (low0, low1), (high0, high1), line)


def solution(mesh):
    placed = (P(("grp", "mem"), None), P(("grp", "mem")), P())
    return jax.shard_map(
        local,
        mesh=mesh,
        in_specs=placed,
        out_specs=(P(("grp", "mem")), P(("grp", "mem"), None)),
        check_vma=False,
    )
```

```python
import functools

import jax
import jax.numpy as jnp
from jax import lax
from jax.experimental import pallas as pl
from jax.experimental.pallas import tpu as pltpu
from jax.sharding import PartitionSpec as P

LOGIT_DIVISOR = 0.1
EPSILON = 1e-06
SLICE = 384
WIDTH = 256
SELF = 2
PIECE = 256
STEPS = ((0, 2), (2, 3), (5, 3), (8, 1))
VMEM = 16 * 1024 * 1024
VMEM_LARGE = 44 * 1024 * 1024
HBM = pl.BlockSpec(memory_space=pltpu.HBM)
SMEM = pl.BlockSpec(memory_space=pltpu.SMEM)


def split(values):
    hi = values.astype(jnp.bfloat16)
    lo = (values - hi.astype(jnp.float32)).astype(jnp.bfloat16)
    return hi, lo


def rows_of(tiles):
    pairs = tiles.reshape(tiles.shape[0] // 2, 2, 8, 128)
    rows = tiles.shape[0] * 4
    return jnp.concatenate([pairs[:, 0].reshape(rows, 128), pairs[:, 1].reshape(rows, 128)], axis=1)


def radius_of(values):
    return jnp.sqrt(jnp.sum(values * values, axis=-1, keepdims=True) + EPSILON)


def as_column(line):
    return jnp.broadcast_to(line, (128, line.shape[1])).T


def in_hbm(value):
    return pltpu.with_memory_space_constraint(value, pltpu.HBM)


def params(limit=VMEM):
    return pltpu.CompilerParams(vmem_limit_bytes=limit)


def tile_kernel(emb_ref, tile_ref):
    rows = emb_ref.shape[0]
    for half in range(2):
        tile_ref[:, half] = emb_ref[:, half * 128 : half * 128 + 128].reshape(rows // 8, 8, 128)


def as_tiles(embeddings):
    rows, _ = embeddings.shape
    return pl.pallas_call(
        tile_kernel,
        out_shape=jax.ShapeDtypeStruct((rows // 8, 2, 8, 128), jnp.float32),
        compiler_params=params(),
        name="as_tiles",
    )(embeddings)


def pick_kernel(pairing_ref, pieces_ref, out_ref):
    size = pieces_ref.shape[1]
    for which in range(out_ref.shape[1] // size):
        for group in range(out_ref.shape[0]):
            out_ref[group, which * size : which * size + size] = pieces_ref[pairing_ref[which, group]]


def pick(pairing, pieces):
    rounds, groups = pairing.shape
    return pl.pallas_call(
        pick_kernel,
        in_specs=[SMEM, pl.BlockSpec()],
        out_shape=jax.ShapeDtypeStruct((groups, rounds * pieces.shape[1], 128), jnp.float32),
        compiler_params=params(),
        name="pick",
    )(pairing, pieces)


def scaled_rows(refs, out_ref, at=0):
    for ref in refs:
        values = ref[...]
        hi, lo = split(values * (1.0 / (radius_of(values) * LOGIT_DIVISOR)))
        out_ref[at : at + hi.shape[0]] = jnp.concatenate([hi, lo, hi], axis=1)
        at += hi.shape[0]


def unit_parts(values):
    hi, lo = split(values * (1.0 / radius_of(values)))
    return jnp.concatenate([hi, lo], axis=1)


def product(left, cols):
    hi, lo = cols[:, :WIDTH], cols[:, WIDTH:]
    return lax.dot_general(
        left,
        jnp.concatenate([hi, hi, lo], axis=1),
        (((1,), (1,)), ((), ())),
        preferred_element_type=jnp.float32,
    )


def exponentials(scores, own, pos_ref, store):
    totals, matches = [], []
    lane_ids = lax.broadcasted_iota(jnp.int32, (128, 128), 1)
    place_ids = lax.broadcasted_iota(jnp.int32, (128, 128), 0)
    for top in range(0, scores.shape[0], 128):
        total = jnp.zeros((128, 128), jnp.float32)
        match = jnp.zeros((128, 128), jnp.float32)
        for k in range(0, scores.shape[1], 128):
            score = scores[top : top + 128, k : k + 128]
            e = jnp.exp(score)
            if own is not None:
                here = place_ids + top == pos_ref[:, own + k : own + k + 128]
                match = match + jnp.where(here, score, 0.0)
                if top // SLICE == SELF and top - SELF * SLICE == own + k:
                    e = jnp.where(place_ids == lane_ids, 0.0, e)
            total = total + e
            store(top // SLICE, slice(top % SLICE, top % SLICE + 128), slice(k, k + 128), e)
        totals.append(total)
        matches.append(match)
    return jnp.concatenate(totals, axis=0), jnp.concatenate(matches, axis=0)


def as_line(total):
    return jnp.sum(total.T, axis=0, keepdims=True)


def put_columns(c_buf, at, parts):
    done = 0
    while done < parts.shape[0]:
        inside = (at + done) % PIECE
        size = min(PIECE - inside, parts.shape[0] - done)
        c_buf[(at + done) // PIECE, inside : inside + size] = parts[done : done + size]
        done += size


def own_kernel(
    ready, ready_far, mine, sib, pos_ref, c_out, e_out, line_ref, left_ref, c_buf, e_buf, tot_ref, in_sem, c_sem, e_sem
):
    at = ready.shape[0]
    ready_copies = [
        pltpu.make_async_copy(ready, left_ref.at[pl.ds(0, at)], in_sem.at[0]),
        pltpu.make_async_copy(ready_far, left_ref.at[pl.ds(at, SLICE)], in_sem.at[1]),
    ]
    for copy in ready_copies:
        copy.start()
    for which, ref in enumerate((mine, sib)):
        put_columns(c_buf, which * SLICE, unit_parts(ref[...]))
    copies = [pltpu.make_async_copy(c_buf, c_out, c_sem)]
    copies[0].start()
    for copy in ready_copies:
        copy.wait()

    pieces = e_buf.shape[0]
    coming = product(left_ref[...], c_buf[0])
    for piece in range(pieces):
        scores = coming
        if piece + 1 < pieces:
            coming = product(left_ref[...], c_buf[piece + 1])

        def store(order, rows, lanes, e):
            e_buf[piece, order, rows, lanes] = e

        total, match = exponentials(scores, piece * PIECE, pos_ref, store)
        for which, value in enumerate((total, match)):
            tot_ref[which] = value if piece == 0 else tot_ref[which] + value
        copies.append(pltpu.make_async_copy(e_buf.at[piece], e_out.at[piece], e_sem.at[piece]))
        copies[-1].start()
    for which in range(2):
        line_ref[which : which + 1] = as_line(tot_ref[which])
    for copy in copies:
        copy.wait()


def own_scores(ready, ready_far, mine, sib, pos):
    rows, wide = 4 * SLICE, 2 * SLICE
    shapes = [((3, PIECE, 2 * WIDTH), jnp.bfloat16), ((3, 4, SLICE, PIECE), jnp.float32)]
    return pl.pallas_call(
        own_kernel,
        in_specs=[HBM] * 2 + [pl.BlockSpec()] * 3,
        out_specs=[HBM] * 2 + [pl.BlockSpec()],
        out_shape=[pltpu.HBM(*shape) for shape in shapes] + [jax.ShapeDtypeStruct((2, rows), jnp.float32)],
        scratch_shapes=[
            pltpu.VMEM((rows, 3 * WIDTH), jnp.bfloat16),
            pltpu.VMEM(*shapes[0]),
            pltpu.VMEM(*shapes[1]),
            pltpu.VMEM((2, rows, 128), jnp.float32),
            pltpu.SemaphoreType.DMA((2,)),
            pltpu.SemaphoreType.DMA,
            pltpu.SemaphoreType.DMA((3,)),
        ],
        cost_estimate=pl.CostEstimate(
            flops=6 * rows * wide * WIDTH, bytes_accessed=4 * rows * wide, transcendentals=rows * wide
        ),
        compiler_params=params(VMEM_LARGE),
        name="own_scores",
    )(in_hbm(ready), in_hbm(ready_far), mine, sib, pos)


def prepare_kernel(*refs):
    pieces, (out_ref, buf, sem) = refs[:-3], refs[-3:]
    scaled_rows(pieces, buf)
    copy = pltpu.make_async_copy(buf, out_ref, sem)
    copy.start()
    copy.wait()


def prepare(name, *pieces):
    rows = sum(piece.shape[0] for piece in pieces)
    shape = ((rows, 3 * WIDTH), jnp.bfloat16)
    return pl.pallas_call(
        prepare_kernel,
        out_specs=HBM,
        out_shape=pltpu.HBM(*shape),
        scratch_shapes=[pltpu.VMEM(*shape), pltpu.SemaphoreType.DMA],
        cost_estimate=pl.CostEstimate(flops=20 * 10**9, bytes_accessed=8 * rows * WIDTH, transcendentals=0),
        compiler_params=params(),
        name=name,
    )(*pieces)


def forward_kernel(
    ready, ready_far, line_in, got, got_sib, e_out, c_out, line_ref,
    left_ref, c_buf, e_buf, tot_ref, in_sem, c_sem, e_sem,
):
    wide, pieces = 2 * SLICE, e_buf.shape[0]
    many = wide // PIECE
    at = ready.shape[0]
    ready_copies = [
        pltpu.make_async_copy(ready, left_ref.at[pl.ds(0, at)], in_sem.at[0]),
        pltpu.make_async_copy(ready_far, left_ref.at[pl.ds(at, SLICE)], in_sem.at[1]),
    ]
    for copy in ready_copies:
        copy.start()
    half = got.shape[1] // 2
    tiles = got.shape[0] * half // 8
    copies = []

    def columns(chunk):
        for which, ref in enumerate((got, got_sib)):
            piece = rows_of(ref[:, chunk * half : chunk * half + half].reshape(tiles, 8, 128))
            put_columns(c_buf, chunk * wide + which * SLICE, unit_parts(piece))
        view = (pl.ds(chunk * many, many),)
        copies.append(pltpu.make_async_copy(c_buf.at[view], c_out.at[view], c_sem.at[chunk]))
        copies[-1].start()

    columns(0)
    for copy in ready_copies:
        copy.wait()
    coming = product(left_ref[...], c_buf[0])
    for piece in range(pieces):
        scores = coming
        if piece + 1 < pieces:
            if (piece + 1) % many == 0:
                columns((piece + 1) // many)
            coming = product(left_ref[...], c_buf[piece + 1])

        def store(order, rows, lanes, e):
            e_buf[piece, order, rows, lanes] = e

        total, _ = exponentials(scores, None, None, store)
        tot_ref[...] = total if piece == 0 else tot_ref[...] + total
        copies.append(pltpu.make_async_copy(e_buf.at[piece], e_out.at[piece], e_sem.at[piece]))
        copies[-1].start()

    total = as_line(tot_ref[...]) + line_in[0:1]
    for member in range(line_ref.shape[0]):
        line_ref[member, 0:1] = total
        line_ref[member, 1:2] = line_in[1:2]
    for copy in copies:
        copy.wait()


def forward(ready, ready_far, line, got, got_sib, members):
    rows, wide = 4 * SLICE, 2 * SLICE
    e_shape, c_shape = ((6, 4, SLICE, PIECE), jnp.float32), ((6, PIECE, 2 * WIDTH), jnp.bfloat16)
    return pl.pallas_call(
        forward_kernel,
        in_specs=[HBM] * 2 + [pl.BlockSpec()] * 3,
        out_specs=[HBM] * 2 + [pl.BlockSpec()],
        out_shape=(
            pltpu.HBM(*e_shape),
            pltpu.HBM(*c_shape),
            jax.ShapeDtypeStruct((members, 2, rows), jnp.float32),
        ),
        scratch_shapes=[
            pltpu.VMEM((rows, 3 * WIDTH), jnp.bfloat16),
            pltpu.VMEM(*c_shape),
            pltpu.VMEM(*e_shape),
            pltpu.VMEM((rows, 128), jnp.float32),
            pltpu.SemaphoreType.DMA((2,)),
            pltpu.SemaphoreType.DMA((2,)),
            pltpu.SemaphoreType.DMA((6,)),
        ],
        cost_estimate=pl.CostEstimate(
            flops=12 * rows * wide * WIDTH, bytes_accessed=8 * rows * wide, transcendentals=2 * rows * wide
        ),
        compiler_params=params(VMEM_LARGE),
        name="forward",
    )(in_hbm(ready), in_hbm(ready_far), line, got, got_sib)


def denominator_kernel(member_ref, all_ref, row_ref, own_ref, line_ref, spread_ref):
    member = member_ref[0]
    members = all_ref.shape[0]

    def summed(owner, kind):
        value = 0.0
        for by, order in ((0, SELF), (2, 0), (members - 2, 1), (4, 3)):
            held = all_ref[lax.rem(owner + by, members)]
            value = value + held[kind : kind + 1, order * SLICE : order * SLICE + SLICE]
        return value

    mate = member + 1 - 2 * lax.rem(member, 2)
    own = summed(member, 0)
    line_ref[0:1] = own
    line_ref[1:2] = summed(member, 1)
    both = jnp.concatenate([own, summed(mate, 0)], axis=1)
    own_ref[...] = both
    spread_ref[...] = jnp.broadcast_to(both.reshape(1, 1, 2 * SLICE), spread_ref.shape)
    for order, by in enumerate((members - 2, 2, 0, 4)):
        value = own if by == 0 else summed(lax.rem(member + by, members), 0)
        row_ref[:, order * SLICE : order * SLICE + SLICE] = value


def denominators(member, everything, groups):
    return pl.pallas_call(
        denominator_kernel,
        in_specs=[SMEM, pl.BlockSpec()],
        out_shape=(
            jax.ShapeDtypeStruct((1, 4 * SLICE), jnp.float32),
            jax.ShapeDtypeStruct((1, 2 * SLICE), jnp.float32),
            jax.ShapeDtypeStruct((2, SLICE), jnp.float32),
            jax.ShapeDtypeStruct((groups, 1, 2 * SLICE), jnp.float32),
        ),
        compiler_params=params(),
        name="denominators",
    )(member, everything)


def backward_kernel(
    bands, first, partner_ref, row_ref, own_ref, everyone_ref, pos_ref, e0_in, e1_in, *refs
):
    if first:
        c0_in, c1_in, c_ref, refs = refs[0], refs[1], refs[2], refs[3:]
    else:
        c_ref, refs = refs[0], refs[1:]
    out_refs, (run_ref, e_buf, e_sem, c_sem) = refs[:-4], refs[-4:]
    own_pieces = e0_in.shape[0]
    copies = []
    for step, (start, many) in enumerate(STEPS):
        group = []
        for k, (source, low, high) in enumerate(
            ((0, 0, own_pieces), (1, own_pieces, own_pieces + e1_in.shape[0]))
        ):
            begin, end = max(start, low), min(start + many, high)
            if begin >= end:
                continue
            here, there = pl.ds(begin, end - begin), pl.ds(begin - low, end - begin)
            at = 0
            for which, (order, row, size) in enumerate(bands):
                group.append(
                    pltpu.make_async_copy(
                        (e0_in, e1_in)[source].at[there, order, pl.ds(row, size)],
                        e_buf.at[here, pl.ds(at, size)],
                        e_sem.at[step, k, which],
                    )
                )
                at += size
            if first:
                src = (c0_in, c1_in)[source].at[there]
                group.append(pltpu.make_async_copy(src, c_ref.at[here], c_sem.at[step, k]))
        copies.append(group)
        for copy in group:
            copy.start()

    columns, places = [], []
    for order, row, size in bands:
        column = as_column(row_ref[:, order * SLICE : order * SLICE + SLICE])
        columns.append(column[row : row + size])
        places.append(lax.broadcasted_iota(jnp.int32, (size, 128), 0) + (order * SLICE + row))
    row_inv = 1.0 / jnp.concatenate(columns, axis=0)
    row_ids = jnp.concatenate(places, axis=0)
    wide = 2 * SLICE
    col_inv = [1.0 / own_ref[...]] + [1.0 / everyone_ref[partner_ref[k]] for k in range(2)]
    for step, (start, many) in enumerate(STEPS):
        for copy in copies[step]:
            copy.wait()
        his, los = [], []
        for at in range(start * PIECE, (start + many) * PIECE, 128):
            inv = col_inv[at // wide][:, at % wide : at % wide + 128]
            weight = e_buf[at // PIECE, :, at % PIECE : at % PIECE + 128] * (row_inv + inv)
            if at < wide:
                weight = weight - jnp.where(row_ids == pos_ref[:, at : at + 128], 2.0, 0.0)
            hi, lo = split(weight)
            his.append(hi)
            los.append(lo)
        cols = c_ref[start : start + many].reshape(many * PIECE, 2 * WIDTH)
        c_hi, c_lo = cols[:, :WIDTH], cols[:, WIDTH:]
        part = jnp.dot(
            jnp.concatenate(his + his + los, axis=1),
            jnp.concatenate([c_hi, c_lo, c_hi], axis=0),
            preferred_element_type=jnp.float32,
        )
        if step == 0:
            run_ref[...] = part
        elif step + 1 < len(STEPS):
            run_ref[...] += part
        else:
            part = run_ref[...] + part
            size = part.shape[0] // len(out_refs)
            for which, ref in enumerate(out_refs):
                ref[...] = part[which * size : which * size + size]


def backward(bands, pieces, partners, row_den, own_den, everyone, pos, e0, e1, *cols):
    first = len(cols) == 2
    count = 9 * PIECE
    height = sum(size for _, _, size in bands)
    col_shape = [jax.ShapeDtypeStruct((9, PIECE, 2 * WIDTH), jnp.bfloat16)]
    return pl.pallas_call(
        functools.partial(backward_kernel, bands, first),
        in_specs=[SMEM] + [pl.BlockSpec()] * 4 + [HBM] * 2 + ([HBM] * 2 if first else [pl.BlockSpec()]),
        out_shape=col_shape * first + [jax.ShapeDtypeStruct((height // pieces, WIDTH), jnp.float32)] * pieces,
        scratch_shapes=[
            pltpu.VMEM((height, WIDTH), jnp.float32),
            pltpu.VMEM((9, height, PIECE), jnp.float32),
            pltpu.SemaphoreType.DMA((len(STEPS), 2, len(bands))),
            pltpu.SemaphoreType.DMA((len(STEPS), 2)),
        ],
        cost_estimate=pl.CostEstimate(
            flops=6 * height * count * WIDTH, bytes_accessed=4 * height * count, transcendentals=0
        ),
        compiler_params=params(VMEM_LARGE),
        name="backward_%d_%d" % bands[0][:2],
    )(partners, row_den, own_den, everyone, pos, in_hbm(e0), in_hbm(e1), *(map(in_hbm, cols) if first else cols))


def add_kernel(a_ref, b_ref, c_ref, d_ref, ab_ref, cd_ref):
    ab_ref[...] = a_ref[...] + b_ref[...]
    cd_ref[...] = c_ref[...] + d_ref[...]


def add_pairs(a, b, c, d):
    out = jax.ShapeDtypeStruct(a.shape, jnp.float32)
    return pl.pallas_call(add_kernel, out_shape=(out, out), compiler_params=params(), name="add_pairs")(
        a, b, c, d
    )


def finish_kernel(emb_ref, run_ref, low0, low1, high0, high1, line_ref, loss_ref, grad_ref):
    values = emb_ref[...]
    radius = radius_of(values)
    unit = values / radius
    low, high = low0[...] + low1[...], high0[...] + high1[...]
    slope = (run_ref[...] + jnp.concatenate([low, high], axis=0)) / LOGIT_DIVISOR
    grad_ref[...] = (slope - unit * jnp.sum(unit * slope, axis=-1, keepdims=True)) / radius
    loss_ref[...] = (jnp.log(line_ref[0:1]) - line_ref[1:2]).reshape(loss_ref.shape)


def finish(embeddings, run, lows, highs, line):
    rows, width = embeddings.shape
    return pl.pallas_call(
        finish_kernel,
        out_shape=(
            jax.ShapeDtypeStruct((rows,), jnp.float32),
            jax.ShapeDtypeStruct((rows, width), jnp.float32),
        ),
        compiler_params=params(),
        name="finish",
    )(embeddings, run, *lows, *highs, line)


def local(embeddings, positive, pairing):
    rows, width = embeddings.shape
    members = lax.axis_size("mem")
    groups = lax.axis_size("grp")
    block = rows * members
    rounds = pairing.shape[0]
    group = lax.axis_index("grp")
    member = lax.axis_index("mem")
    half = rows // 2

    def shift(value, by):
        return lax.ppermute(value, "mem", [(m, (m + by) % members) for m in range(members)])

    def swap(value):
        return lax.ppermute(value, "mem", [(m, m ^ 1) for m in range(members)])

    left, right = shift(embeddings, 2), shift(embeddings, -2)
    far = (shift(left[:half], 2), shift(right[half:], -2))
    per = rows * width // (groups * 128)
    pieces = lax.all_to_all(as_tiles(embeddings).reshape(groups, per, 128), "grp", 0, 0, tiled=True)
    ready = prepare("prepare", left, right, embeddings)
    picked, ready = lax.optimization_barrier((pick(pairing, pieces), ready))
    got = lax.all_to_all(picked, "grp", 0, 0, tiled=True)
    sib, pos_sib = swap(embeddings), swap(positive)

    both = jnp.concatenate([positive, pos_sib]) - group * block
    owner = both // rows
    turn = (owner // 2 - member // 2) % (members // 2)
    order = jnp.where(turn == 0, SELF, jnp.where(turn == 3, 0, jnp.where(turn == 1, 1, 3)))
    pos = jnp.where(owner % 2 == member % 2, order * rows + both % rows, -1).reshape(1, 2 * rows)

    ready_far = prepare("prepare_far", *far)
    c_own, e_own, line = own_scores(ready, ready_far, embeddings, sib, pos)
    got, line = lax.optimization_barrier((got, line))
    e_part, c_part, line = forward(ready, ready_far, line, got, swap(got), members)

    everything = lax.all_to_all(line, "mem", 0, 0, tiled=True)
    row_den, own_den, line, spread = denominators(jnp.reshape(member, (1,)), everything, groups)
    everyone = lax.all_to_all(spread, "grp", 0, 0, tiled=True)

    shared = (pairing[:, group], row_den, own_den, everyone, pos, e_own, e_part)
    bands = ((3, 0, rows), (0, 0, half), (1, half, half))
    cols, far_low, far_high, left_low, right_high = backward(bands, 4, *shared, c_own, c_part)
    shared += (cols,)
    far_low, far_high = shift(far_low, 2), shift(far_high, -2)
    high0, low1 = shift(right_high, 2), shift(left_low, -2)
    left_high, right_low = backward(((0, half, half), (1, 0, half)), 2, *shared)
    right_low, left_high = add_pairs(right_low, far_low, left_high, far_high)
    low0, high1 = shift(right_low, 2), shift(left_high, -2)
    (run,) = backward(((SELF, 0, rows),), 1, *shared)
    return finish(embeddings, run, (low0, low1), (high0, high1), line)


def solution(mesh):
    placed = (P(("grp", "mem"), None), P(("grp", "mem")), P())
    return jax.shard_map(
        local,
        mesh=mesh,
        in_specs=placed,
        out_specs=(P(("grp", "mem")), P(("grp", "mem"), None)),
        check_vma=False,
    )
```

```python
import functools

import jax
import jax.numpy as jnp
from jax import lax
from jax.experimental import pallas as pl
from jax.experimental.pallas import tpu as pltpu
from jax.sharding import PartitionSpec as P

LOGIT_DIVISOR = 0.1
EPSILON = 1e-06
SLICE = 384
WIDTH = 256
SELF = 2
PIECE = 256
STEPS = ((0, 3), (3, 3), (6, 3))
VMEM = 16 * 1024 * 1024
VMEM_LARGE = 44 * 1024 * 1024
VMEM_BACKWARD = 28 * 1024 * 1024
HBM = pl.BlockSpec(memory_space=pltpu.HBM)
SMEM = pl.BlockSpec(memory_space=pltpu.SMEM)


def split(values):
    hi = values.astype(jnp.bfloat16)
    lo = (values - hi.astype(jnp.float32)).astype(jnp.bfloat16)
    return hi, lo


def rows_of(tiles):
    pairs = tiles.reshape(tiles.shape[0] // 2, 2, 8, 128)
    rows = tiles.shape[0] * 4
    return jnp.concatenate([pairs[:, 0].reshape(rows, 128), pairs[:, 1].reshape(rows, 128)], axis=1)


def radius_of(values):
    return jnp.sqrt(jnp.sum(values * values, axis=-1, keepdims=True) + EPSILON)


def as_column(line):
    return jnp.broadcast_to(line, (128, line.shape[1])).T


def in_hbm(value):
    return pltpu.with_memory_space_constraint(value, pltpu.HBM)


def params(limit=VMEM):
    return pltpu.CompilerParams(vmem_limit_bytes=limit)


def pick_kernel(pairing_ref, pieces_ref, out_ref):
    size = pieces_ref.shape[1]
    for which in range(out_ref.shape[1] // size):
        for group in range(out_ref.shape[0]):
            out_ref[group, which * size : which * size + size] = pieces_ref[pairing_ref[which, group]]


def pick(pairing, pieces):
    rounds, groups = pairing.shape
    return pl.pallas_call(
        pick_kernel,
        in_specs=[SMEM, pl.BlockSpec()],
        out_shape=jax.ShapeDtypeStruct((groups, rounds * pieces.shape[1], 128), jnp.float32),
        compiler_params=params(),
        name="pick",
    )(pairing, pieces)


def scaled_rows(refs, out_ref, at=0):
    for ref in refs:
        values = ref[...]
        hi, lo = split(values * (1.0 / (radius_of(values) * LOGIT_DIVISOR)))
        out_ref[at : at + hi.shape[0]] = jnp.concatenate([hi, lo, hi], axis=1)
        at += hi.shape[0]


def unit_parts(values):
    hi, lo = split(values * (1.0 / radius_of(values)))
    return jnp.concatenate([hi, lo], axis=1)


def product(left, cols):
    hi, lo = cols[:, :WIDTH], cols[:, WIDTH:]
    return lax.dot_general(
        left,
        jnp.concatenate([hi, hi, lo], axis=1),
        (((1,), (1,)), ((), ())),
        preferred_element_type=jnp.float32,
    )


def exponentials(scores, first_row, pos_ref, store):
    height = scores.shape[0]
    total = jnp.zeros((height, 128), jnp.float32)
    match = jnp.zeros((height, 128), jnp.float32)
    if first_row is not None:
        row_ids = lax.broadcasted_iota(jnp.int32, (height, 128), 0) + first_row
        lane_ids = lax.broadcasted_iota(jnp.int32, (height, 128), 1)
    for k in range(0, scores.shape[1], 128):
        score = scores[:, k : k + 128]
        e = jnp.exp(score)
        if first_row is not None:
            match = match + jnp.where(row_ids == pos_ref[:, k : k + 128], score, 0.0)
            if first_row <= SELF * SLICE < first_row + height and k < SLICE:
                e = jnp.where(row_ids - SELF * SLICE == lane_ids + k, 0.0, e)
        total = total + e
        store(k, e)
    return total, match


def as_line(total):
    return jnp.sum(total.T, axis=0, keepdims=True)


def put_columns(c_buf, at, parts):
    done = 0
    while done < parts.shape[0]:
        inside = (at + done) % PIECE
        size = min(PIECE - inside, parts.shape[0] - done)
        c_buf[(at + done) // PIECE, inside : inside + size] = parts[done : done + size]
        done += size


def own_kernel(
    ready, ready_far, mine, sib, pos_ref, c_out, e_out, line_ref, left_ref, c_buf, e_buf, in_sem, c_sem, e_sem
):
    at = ready.shape[0]
    ready_copies = [
        pltpu.make_async_copy(ready, left_ref.at[pl.ds(0, at)], in_sem.at[0]),
        pltpu.make_async_copy(ready_far, left_ref.at[pl.ds(at, SLICE)], in_sem.at[1]),
    ]
    for copy in ready_copies:
        copy.start()
    for which, ref in enumerate((mine, sib)):
        put_columns(c_buf, which * SLICE, unit_parts(ref[...]))
    cols = c_buf[...].reshape(2 * SLICE, 2 * WIDTH)
    copies = [pltpu.make_async_copy(c_buf, c_out, c_sem)]
    copies[0].start()
    for copy in ready_copies:
        copy.wait()

    coming = product(left_ref[:SLICE], cols)
    totals, matches = [], []
    for order in range(4):
        scores = coming
        if order < 3:
            at = (order + 1) * SLICE
            coming = product(left_ref[at : at + SLICE], cols)

        def store(k, e):
            e_buf[k // PIECE, order, :, k % PIECE : k % PIECE + 128] = e

        total, match = exponentials(scores, order * SLICE, pos_ref, store)
        totals.append(as_line(total))
        matches.append(as_line(match))
        copies.append(pltpu.make_async_copy(e_buf.at[:, order], e_out.at[:, order], e_sem.at[order]))
        copies[-1].start()
    line_ref[0:1] = jnp.concatenate(totals, axis=1)
    line_ref[1:2] = jnp.concatenate(matches, axis=1)
    for copy in copies:
        copy.wait()


def own_scores(ready, ready_far, mine, sib, pos):
    rows, wide = 4 * SLICE, 2 * SLICE
    shapes = [((3, PIECE, 2 * WIDTH), jnp.bfloat16), ((3, 4, SLICE, PIECE), jnp.float32)]
    return pl.pallas_call(
        own_kernel,
        in_specs=[HBM] * 2 + [pl.BlockSpec()] * 3,
        out_specs=[HBM] * 2 + [pl.BlockSpec()],
        out_shape=[pltpu.HBM(*shape) for shape in shapes] + [jax.ShapeDtypeStruct((2, rows), jnp.float32)],
        scratch_shapes=[
            pltpu.VMEM((rows, 3 * WIDTH), jnp.bfloat16),
            pltpu.VMEM(*shapes[0]),
            pltpu.VMEM(*shapes[1]),
            pltpu.SemaphoreType.DMA((2,)),
            pltpu.SemaphoreType.DMA,
            pltpu.SemaphoreType.DMA((4,)),
        ],
        cost_estimate=pl.CostEstimate(
            flops=6 * rows * wide * WIDTH, bytes_accessed=4 * rows * wide, transcendentals=rows * wide
        ),
        compiler_params=params(VMEM_LARGE),
        name="own_scores",
    )(in_hbm(ready), in_hbm(ready_far), mine, sib, pos)


def prepare_kernel(*refs):
    pieces, (out_ref, buf, sem) = refs[:-3], refs[-3:]
    scaled_rows(pieces, buf)
    copy = pltpu.make_async_copy(buf, out_ref, sem)
    copy.start()
    copy.wait()


def prepare(name, *pieces):
    rows = sum(piece.shape[0] for piece in pieces)
    shape = ((rows, 3 * WIDTH), jnp.bfloat16)
    return pl.pallas_call(
        prepare_kernel,
        out_specs=HBM,
        out_shape=pltpu.HBM(*shape),
        scratch_shapes=[pltpu.VMEM(*shape), pltpu.SemaphoreType.DMA],
        cost_estimate=pl.CostEstimate(flops=20 * 10**9, bytes_accessed=8 * rows * WIDTH, transcendentals=0),
        compiler_params=params(),
        name=name,
    )(*pieces)


def forward_kernel(
    ready, ready_far, line_in, got, got_sib, e_out, c_out, line_ref,
    left_ref, c_buf, e_buf, tot_ref, in_sem, c_sem, e_sem,
):
    orders, wide = e_buf.shape[1], 2 * SLICE
    many = wide // PIECE
    chunks = e_buf.shape[0] // many
    at = ready.shape[0]
    ready_copies = [
        pltpu.make_async_copy(ready, left_ref.at[pl.ds(0, at)], in_sem.at[0]),
        pltpu.make_async_copy(ready_far, left_ref.at[pl.ds(at, SLICE)], in_sem.at[1]),
    ]
    for copy in ready_copies:
        copy.start()
    half = got.shape[1] // 2
    tiles = got.shape[0] * half // 8
    copies = []

    def columns(chunk):
        for which, ref in enumerate((got, got_sib)):
            piece = rows_of(ref[:, chunk * half : chunk * half + half].reshape(tiles, 8, 128))
            put_columns(c_buf, chunk * wide + which * SLICE, unit_parts(piece))
        view = (pl.ds(chunk * many, many),)
        copies.append(pltpu.make_async_copy(c_buf.at[view], c_out.at[view], c_sem.at[chunk]))
        copies[-1].start()

    def scores_of(chunk, band):
        cols = c_buf[chunk * many : chunk * many + many].reshape(wide, 2 * WIDTH)
        return product(left_ref[band * wide : band * wide + wide], cols)

    columns(0)
    for copy in ready_copies:
        copy.wait()
    items = [(chunk, band) for chunk in range(chunks) for band in range(orders // 2)]
    coming = scores_of(*items[0])
    for turn, (chunk, band) in enumerate(items):
        scores = coming
        if turn + 1 < len(items):
            if items[turn + 1][0] != chunk:
                columns(items[turn + 1][0])
            coming = scores_of(*items[turn + 1])

        def store(k, e):
            lane = k % PIECE
            e = e.reshape(2, SLICE, 128)
            e_buf[chunk * many + k // PIECE, 2 * band : 2 * band + 2, :, lane : lane + 128] = e

        total, _ = exponentials(scores, None, None, store)
        if chunk == 0:
            tot_ref[band * wide : band * wide + wide] = total
        else:
            tot_ref[band * wide : band * wide + wide] += total
        view = (pl.ds(chunk * many, many), pl.ds(2 * band, 2))
        copies.append(pltpu.make_async_copy(e_buf.at[view], e_out.at[view], e_sem.at[turn]))
        copies[-1].start()

    total = as_line(tot_ref[...]) + line_in[0:1]
    for member in range(line_ref.shape[0]):
        line_ref[member, 0:1] = total
        line_ref[member, 1:2] = line_in[1:2]
    for copy in copies:
        copy.wait()


def forward(ready, ready_far, line, got, got_sib, members):
    rows, wide = 4 * SLICE, 2 * SLICE
    e_shape, c_shape = ((6, 4, SLICE, PIECE), jnp.float32), ((6, PIECE, 2 * WIDTH), jnp.bfloat16)
    return pl.pallas_call(
        forward_kernel,
        in_specs=[HBM] * 2 + [pl.BlockSpec()] * 3,
        out_specs=[HBM] * 2 + [pl.BlockSpec()],
        out_shape=(
            pltpu.HBM(*e_shape),
            pltpu.HBM(*c_shape),
            jax.ShapeDtypeStruct((members, 2, rows), jnp.float32),
        ),
        scratch_shapes=[
            pltpu.VMEM((rows, 3 * WIDTH), jnp.bfloat16),
            pltpu.VMEM(*c_shape),
            pltpu.VMEM(*e_shape),
            pltpu.VMEM((rows, 128), jnp.float32),
            pltpu.SemaphoreType.DMA((2,)),
            pltpu.SemaphoreType.DMA((2,)),
            pltpu.SemaphoreType.DMA((4,)),
        ],
        cost_estimate=pl.CostEstimate(
            flops=12 * rows * wide * WIDTH, bytes_accessed=8 * rows * wide, transcendentals=2 * rows * wide
        ),
        compiler_params=params(VMEM_LARGE),
        name="forward",
    )(in_hbm(ready), in_hbm(ready_far), line, got, got_sib)


def denominator_kernel(member_ref, all_ref, row_ref, own_ref, line_ref, spread_ref):
    member = member_ref[0]
    members = all_ref.shape[0]

    def summed(owner, kind):
        value = 0.0
        for by, order in ((0, SELF), (2, 0), (members - 2, 1), (4, 3)):
            held = all_ref[lax.rem(owner + by, members)]
            value = value + held[kind : kind + 1, order * SLICE : order * SLICE + SLICE]
        return value

    mate = member + 1 - 2 * lax.rem(member, 2)
    own = summed(member, 0)
    line_ref[0:1] = own
    line_ref[1:2] = summed(member, 1)
    both = jnp.concatenate([own, summed(mate, 0)], axis=1)
    own_ref[...] = both
    spread_ref[...] = jnp.broadcast_to(both.reshape(1, 1, 2 * SLICE), spread_ref.shape)
    for order, by in enumerate((members - 2, 2, 0, 4)):
        value = own if by == 0 else summed(lax.rem(member + by, members), 0)
        row_ref[:, order * SLICE : order * SLICE + SLICE] = value


def denominators(member, everything, groups):
    return pl.pallas_call(
        denominator_kernel,
        in_specs=[SMEM, pl.BlockSpec()],
        out_shape=(
            jax.ShapeDtypeStruct((1, 4 * SLICE), jnp.float32),
            jax.ShapeDtypeStruct((1, 2 * SLICE), jnp.float32),
            jax.ShapeDtypeStruct((2, SLICE), jnp.float32),
            jax.ShapeDtypeStruct((groups, 1, 2 * SLICE), jnp.float32),
        ),
        compiler_params=params(),
        name="denominators",
    )(member, everything)


def backward_kernel(
    bands, first, partner_ref, row_ref, own_ref, everyone_ref, pos_ref, e0_in, e1_in, *refs
):
    if first:
        c0_in, c1_in, c_ref, refs = refs[0], refs[1], refs[2], refs[3:]
    else:
        c_ref, refs = refs[0], refs[1:]
    out_refs, (run_ref, e_buf, e_sem, c_sem) = refs[:-4], refs[-4:]
    own_pieces = e0_in.shape[0]
    copies = []
    for step, (start, many) in enumerate(STEPS):
        group = []
        for k, (source, low, high) in enumerate(
            ((0, 0, own_pieces), (1, own_pieces, own_pieces + e1_in.shape[0]))
        ):
            begin, end = max(start, low), min(start + many, high)
            if begin >= end:
                continue
            here, there = pl.ds(begin, end - begin), pl.ds(begin - low, end - begin)
            at = 0
            for which, (order, row, size) in enumerate(bands):
                group.append(
                    pltpu.make_async_copy(
                        (e0_in, e1_in)[source].at[there, order, pl.ds(row, size)],
                        e_buf.at[here, pl.ds(at, size)],
                        e_sem.at[step, k, which],
                    )
                )
                at += size
            if first:
                src = (c0_in, c1_in)[source].at[there]
                group.append(pltpu.make_async_copy(src, c_ref.at[here], c_sem.at[step, k]))
        copies.append(group)
        for copy in group:
            copy.start()

    columns, places = [], []
    for order, row, size in bands:
        column = as_column(row_ref[:, order * SLICE : order * SLICE + SLICE])
        columns.append(column[row : row + size])
        places.append(lax.broadcasted_iota(jnp.int32, (size, 128), 0) + (order * SLICE + row))
    row_inv = 1.0 / jnp.concatenate(columns, axis=0)
    row_ids = jnp.concatenate(places, axis=0)
    wide = 2 * SLICE
    col_inv = [1.0 / own_ref[...]] + [1.0 / everyone_ref[partner_ref[k]] for k in range(2)]
    for step, (start, many) in enumerate(STEPS):
        for copy in copies[step]:
            copy.wait()
        his, los = [], []
        for at in range(start * PIECE, (start + many) * PIECE, 128):
            inv = col_inv[at // wide][:, at % wide : at % wide + 128]
            weight = e_buf[at // PIECE, :, at % PIECE : at % PIECE + 128] * (row_inv + inv)
            if at < wide:
                weight = weight - jnp.where(row_ids == pos_ref[:, at : at + 128], 2.0, 0.0)
            hi, lo = split(weight)
            his.append(hi)
            los.append(lo)
        cols = c_ref[start : start + many].reshape(many * PIECE, 2 * WIDTH)
        c_hi, c_lo = cols[:, :WIDTH], cols[:, WIDTH:]
        part = jnp.dot(
            jnp.concatenate(his + his + los, axis=1),
            jnp.concatenate([c_hi, c_lo, c_hi], axis=0),
            preferred_element_type=jnp.float32,
        )
        if step == 0:
            run_ref[...] = part
        elif step + 1 < len(STEPS):
            run_ref[...] += part
        else:
            part = run_ref[...] + part
            size = part.shape[0] // len(out_refs)
            for which, ref in enumerate(out_refs):
                ref[...] = part[which * size : which * size + size]


def backward(bands, pieces, partners, row_den, own_den, everyone, pos, e0, e1, *cols):
    first = len(cols) == 2
    count = 9 * PIECE
    col_shape = [jax.ShapeDtypeStruct((9, PIECE, 2 * WIDTH), jnp.bfloat16)]
    return pl.pallas_call(
        functools.partial(backward_kernel, bands, first),
        in_specs=[SMEM] + [pl.BlockSpec()] * 4 + [HBM] * 2 + ([HBM] * 2 if first else [pl.BlockSpec()]),
        out_shape=col_shape * first + [jax.ShapeDtypeStruct((SLICE // pieces, WIDTH), jnp.float32)] * pieces,
        scratch_shapes=[
            pltpu.VMEM((SLICE, WIDTH), jnp.float32),
            pltpu.VMEM((9, SLICE, PIECE), jnp.float32),
            pltpu.SemaphoreType.DMA((len(STEPS), 2, len(bands))),
            pltpu.SemaphoreType.DMA((len(STEPS), 2)),
        ],
        cost_estimate=pl.CostEstimate(
            flops=6 * SLICE * count * WIDTH, bytes_accessed=4 * SLICE * count, transcendentals=0
        ),
        compiler_params=params(VMEM_BACKWARD),
        name="backward_%d_%d" % bands[0][:2],
    )(partners, row_den, own_den, everyone, pos, in_hbm(e0), in_hbm(e1), *(map(in_hbm, cols) if first else cols))


def add_kernel(a_ref, b_ref, c_ref, d_ref, ab_ref, cd_ref):
    ab_ref[...] = a_ref[...] + b_ref[...]
    cd_ref[...] = c_ref[...] + d_ref[...]


def add_pairs(a, b, c, d):
    out = jax.ShapeDtypeStruct(a.shape, jnp.float32)
    return pl.pallas_call(add_kernel, out_shape=(out, out), compiler_params=params(), name="add_pairs")(
        a, b, c, d
    )


def finish_kernel(emb_ref, run_ref, low0, low1, high0, high1, line_ref, loss_ref, grad_ref):
    values = emb_ref[...]
    radius = radius_of(values)
    unit = values / radius
    low, high = low0[...] + low1[...], high0[...] + high1[...]
    slope = (run_ref[...] + jnp.concatenate([low, high], axis=0)) / LOGIT_DIVISOR
    grad_ref[...] = (slope - unit * jnp.sum(unit * slope, axis=-1, keepdims=True)) / radius
    loss_ref[...] = (jnp.log(line_ref[0:1]) - line_ref[1:2]).reshape(loss_ref.shape)


def finish(embeddings, run, lows, highs, line):
    rows, width = embeddings.shape
    return pl.pallas_call(
        finish_kernel,
        out_shape=(
            jax.ShapeDtypeStruct((rows,), jnp.float32),
            jax.ShapeDtypeStruct((rows, width), jnp.float32),
        ),
        compiler_params=params(),
        name="finish",
    )(embeddings, run, *lows, *highs, line)


def local(embeddings, positive, pairing):
    rows, width = embeddings.shape
    members = lax.axis_size("mem")
    groups = lax.axis_size("grp")
    block = rows * members
    rounds = pairing.shape[0]
    group = lax.axis_index("grp")
    member = lax.axis_index("mem")
    half = rows // 2

    def shift(value, by):
        return lax.ppermute(value, "mem", [(m, (m + by) % members) for m in range(members)])

    def swap(value):
        return lax.ppermute(value, "mem", [(m, m ^ 1) for m in range(members)])

    left, right = shift(embeddings, 2), shift(embeddings, -2)
    far = (shift(left[:half], 2), shift(right[half:], -2))
    per = rows * width // (groups * 128)
    tiles = embeddings.reshape(rows // 8, 8, width // 128, 128).transpose(0, 2, 1, 3)
    pieces = lax.all_to_all(tiles.reshape(groups, per, 128), "grp", 0, 0, tiled=True)
    ready = prepare("prepare", left, right, embeddings)
    picked, ready, mine, same = lax.optimization_barrier((pick(pairing, pieces), ready, embeddings, positive))
    got = lax.all_to_all(picked, "grp", 0, 0, tiled=True)
    sib, pos_sib = swap(mine), swap(same)

    both = jnp.concatenate([positive, pos_sib]) - group * block
    owner = both // rows
    turn = (owner // 2 - member // 2) % (members // 2)
    order = jnp.where(turn == 0, SELF, jnp.where(turn == 3, 0, jnp.where(turn == 1, 1, 3)))
    pos = jnp.where(owner % 2 == member % 2, order * rows + both % rows, -1).reshape(1, 2 * rows)

    ready_far = prepare("prepare_far", *far)
    c_own, e_own, line = own_scores(ready, ready_far, embeddings, sib, pos)
    got, line = lax.optimization_barrier((got, line))
    e_part, c_part, line = forward(ready, ready_far, line, got, swap(got), members)

    everything = lax.all_to_all(line, "mem", 0, 0, tiled=True)
    row_den, own_den, line, spread = denominators(jnp.reshape(member, (1,)), everything, groups)
    everyone = lax.all_to_all(spread, "grp", 0, 0, tiled=True)

    shared = (pairing[:, group], row_den, own_den, everyone, pos, e_own, e_part)
    cols, far_low, far_high = backward(((3, 0, rows),), 2, *shared, c_own, c_part)
    shared += (cols,)
    far_low, far_high = shift(far_low, 2), shift(far_high, -2)
    left_low, right_high = backward(((0, 0, half), (1, half, half)), 2, *shared)
    high0, low1 = shift(right_high, 2), shift(left_low, -2)
    left_high, right_low = backward(((0, half, half), (1, 0, half)), 2, *shared)
    right_low, left_high = add_pairs(right_low, far_low, left_high, far_high)
    low0, high1 = shift(right_low, 2), shift(left_high, -2)
    (run,) = backward(((SELF, 0, rows),), 1, *shared)
    return finish(embeddings, run, (low0, low1), (high0, high1), line)


def solution(mesh):
    placed = (P(("grp", "mem"), None), P(("grp", "mem")), P())
    return jax.shard_map(
        local,
        mesh=mesh,
        in_specs=placed,
        out_specs=(P(("grp", "mem")), P(("grp", "mem"), None)),
        check_vma=False,
    )
```

```python
import functools

import jax
import jax.numpy as jnp
from jax import lax
from jax.experimental import pallas as pl
from jax.experimental.pallas import tpu as pltpu
from jax.sharding import PartitionSpec as P

LOGIT_DIVISOR = 0.1
EPSILON = 1e-06
SLICE = 384
WIDTH = 256
SELF = 2
PIECE = 256
STEPS = ((0, 3), (3, 3), (6, 3))
VMEM = 16 * 1024 * 1024
VMEM_LARGE = 44 * 1024 * 1024
VMEM_BACKWARD = 28 * 1024 * 1024
HBM = pl.BlockSpec(memory_space=pltpu.HBM)
SMEM = pl.BlockSpec(memory_space=pltpu.SMEM)


def split(values):
    hi = values.astype(jnp.bfloat16)
    lo = (values - hi.astype(jnp.float32)).astype(jnp.bfloat16)
    return hi, lo


def rows_of(tiles):
    pairs = tiles.reshape(tiles.shape[0] // 2, 2, 8, 128)
    rows = tiles.shape[0] * 4
    return jnp.concatenate([pairs[:, 0].reshape(rows, 128), pairs[:, 1].reshape(rows, 128)], axis=1)


def radius_of(values):
    return jnp.sqrt(jnp.sum(values * values, axis=-1, keepdims=True) + EPSILON)


def as_column(line):
    return jnp.broadcast_to(line, (128, line.shape[1])).T


def in_hbm(value):
    return pltpu.with_memory_space_constraint(value, pltpu.HBM)


def params(limit=VMEM):
    return pltpu.CompilerParams(vmem_limit_bytes=limit)


def pick_kernel(pairing_ref, pieces_ref, out_ref):
    size = pieces_ref.shape[1]
    for which in range(out_ref.shape[1] // size):
        for group in range(out_ref.shape[0]):
            out_ref[group, which * size : which * size + size] = pieces_ref[pairing_ref[which, group]]


def pick(pairing, pieces):
    rounds, groups = pairing.shape
    return pl.pallas_call(
        pick_kernel,
        in_specs=[SMEM, pl.BlockSpec()],
        out_shape=jax.ShapeDtypeStruct((groups, rounds * pieces.shape[1], 128), jnp.float32),
        compiler_params=params(),
        name="pick",
    )(pairing, pieces)


def scaled_rows(refs, out_ref, at=0):
    for ref in refs:
        values = ref[...]
        hi, lo = split(values * (1.0 / (radius_of(values) * LOGIT_DIVISOR)))
        out_ref[at : at + hi.shape[0]] = jnp.concatenate([hi, lo, hi], axis=1)
        at += hi.shape[0]


def unit_parts(values):
    hi, lo = split(values * (1.0 / radius_of(values)))
    return jnp.concatenate([hi, lo], axis=1)


def product(left, cols):
    hi, lo = cols[:, :WIDTH], cols[:, WIDTH:]
    return lax.dot_general(
        left,
        jnp.concatenate([hi, hi, lo], axis=1),
        (((1,), (1,)), ((), ())),
        preferred_element_type=jnp.float32,
    )


def exponentials(scores, first_row, pos_ref, store):
    height = scores.shape[0]
    total = jnp.zeros((height, 128), jnp.float32)
    match = jnp.zeros((height, 128), jnp.float32)
    if first_row is not None:
        row_ids = lax.broadcasted_iota(jnp.int32, (height, 128), 0) + first_row
        lane_ids = lax.broadcasted_iota(jnp.int32, (height, 128), 1)
    for k in range(0, scores.shape[1], 128):
        score = scores[:, k : k + 128]
        e = jnp.exp(score)
        if first_row is not None:
            match = match + jnp.where(row_ids == pos_ref[:, k : k + 128], score, 0.0)
            if first_row <= SELF * SLICE < first_row + height and k < SLICE:
                e = jnp.where(row_ids - SELF * SLICE == lane_ids + k, 0.0, e)
        total = total + e
        store(k, e)
    return total, match


def as_line(total):
    return jnp.sum(total.T, axis=0, keepdims=True)


def put_columns(c_buf, at, parts):
    done = 0
    while done < parts.shape[0]:
        inside = (at + done) % PIECE
        size = min(PIECE - inside, parts.shape[0] - done)
        c_buf[(at + done) // PIECE, inside : inside + size] = parts[done : done + size]
        done += size


def own_kernel(
    ready, ready_far, mine, sib, pos_ref, c_out, e_out, line_ref, left_ref, c_buf, e_buf, in_sem, c_sem, e_sem
):
    at = ready.shape[0]
    ready_copies = [
        pltpu.make_async_copy(ready, left_ref.at[pl.ds(0, at)], in_sem.at[0]),
        pltpu.make_async_copy(ready_far, left_ref.at[pl.ds(at, ready_far.shape[0])], in_sem.at[1]),
    ]
    for copy in ready_copies:
        copy.start()
    for which, ref in enumerate((mine, sib)):
        put_columns(c_buf, which * SLICE, unit_parts(ref[...]))
    cols = c_buf[...].reshape(2 * SLICE, 2 * WIDTH)
    copies = [pltpu.make_async_copy(c_buf, c_out, c_sem)]
    copies[0].start()
    for copy in ready_copies:
        copy.wait()

    coming = product(left_ref[:SLICE], cols)
    totals, matches = [], []
    for order in range(4):
        scores = coming
        if order < 3:
            at = (order + 1) * SLICE
            coming = product(left_ref[at : at + SLICE], cols)

        def store(k, e):
            e_buf[k // PIECE, order, :, k % PIECE : k % PIECE + 128] = e

        total, match = exponentials(scores, order * SLICE, pos_ref, store)
        totals.append(as_line(total))
        matches.append(as_line(match))
        copies.append(pltpu.make_async_copy(e_buf.at[:, order], e_out.at[:, order], e_sem.at[order]))
        copies[-1].start()
    line_ref[0:1] = jnp.concatenate(totals, axis=1)
    line_ref[1:2] = jnp.concatenate(matches, axis=1)
    for copy in copies:
        copy.wait()


def own_scores(ready, ready_far, mine, sib, pos):
    rows, wide = 4 * SLICE, 2 * SLICE
    shapes = [((3, PIECE, 2 * WIDTH), jnp.bfloat16), ((3, 4, SLICE, PIECE), jnp.float32)]
    return pl.pallas_call(
        own_kernel,
        in_specs=[HBM] * 2 + [pl.BlockSpec()] * 3,
        out_specs=[HBM] * 2 + [pl.BlockSpec()],
        out_shape=[pltpu.HBM(*shape) for shape in shapes] + [jax.ShapeDtypeStruct((2, rows), jnp.float32)],
        scratch_shapes=[
            pltpu.VMEM((rows, 3 * WIDTH), jnp.bfloat16),
            pltpu.VMEM(*shapes[0]),
            pltpu.VMEM(*shapes[1]),
            pltpu.SemaphoreType.DMA((2,)),
            pltpu.SemaphoreType.DMA,
            pltpu.SemaphoreType.DMA((4,)),
        ],
        cost_estimate=pl.CostEstimate(
            flops=6 * rows * wide * WIDTH, bytes_accessed=4 * rows * wide, transcendentals=rows * wide
        ),
        compiler_params=params(VMEM_LARGE),
        name="own_scores",
    )(in_hbm(ready), in_hbm(ready_far), mine, sib, pos)


def prepare_kernel(*refs):
    pieces, (out_ref, buf, sem) = refs[:-3], refs[-3:]
    scaled_rows(pieces, buf)
    copy = pltpu.make_async_copy(buf, out_ref, sem)
    copy.start()
    copy.wait()


def prepare(name, *pieces):
    rows = sum(piece.shape[0] for piece in pieces)
    shape = ((rows, 3 * WIDTH), jnp.bfloat16)
    return pl.pallas_call(
        prepare_kernel,
        out_specs=HBM,
        out_shape=pltpu.HBM(*shape),
        scratch_shapes=[pltpu.VMEM(*shape), pltpu.SemaphoreType.DMA],
        cost_estimate=pl.CostEstimate(flops=20 * 10**9, bytes_accessed=8 * rows * WIDTH, transcendentals=0),
        compiler_params=params(),
        name=name,
    )(*pieces)


def forward_kernel(
    ready, ready_far, line_in, got, got_sib, e_out, c_out, line_ref,
    left_ref, c_buf, e_buf, tot_ref, in_sem, c_sem, e_sem,
):
    orders, wide = e_buf.shape[1], 2 * SLICE
    many = wide // PIECE
    chunks = e_buf.shape[0] // many
    at = ready.shape[0]
    ready_copies = [
        pltpu.make_async_copy(ready, left_ref.at[pl.ds(0, at)], in_sem.at[0]),
        pltpu.make_async_copy(ready_far, left_ref.at[pl.ds(at, ready_far.shape[0])], in_sem.at[1]),
    ]
    for copy in ready_copies:
        copy.start()
    half = got.shape[1] // 2
    tiles = got.shape[0] * half // 8
    copies = []

    def columns(chunk):
        for which, ref in enumerate((got, got_sib)):
            piece = rows_of(ref[:, chunk * half : chunk * half + half].reshape(tiles, 8, 128))
            put_columns(c_buf, chunk * wide + which * SLICE, unit_parts(piece))
        view = (pl.ds(chunk * many, many),)
        copies.append(pltpu.make_async_copy(c_buf.at[view], c_out.at[view], c_sem.at[chunk]))
        copies[-1].start()

    def scores_of(chunk, band):
        cols = c_buf[chunk * many : chunk * many + many].reshape(wide, 2 * WIDTH)
        return product(left_ref[band * wide : band * wide + wide], cols)

    columns(0)
    for copy in ready_copies:
        copy.wait()
    items = [(chunk, band) for chunk in range(chunks) for band in range(orders // 2)]
    coming = scores_of(*items[0])
    for turn, (chunk, band) in enumerate(items):
        scores = coming
        if turn + 1 < len(items):
            if items[turn + 1][0] != chunk:
                columns(items[turn + 1][0])
            coming = scores_of(*items[turn + 1])

        def store(k, e):
            lane = k % PIECE
            e = e.reshape(2, SLICE, 128)
            e_buf[chunk * many + k // PIECE, 2 * band : 2 * band + 2, :, lane : lane + 128] = e

        total, _ = exponentials(scores, None, None, store)
        if chunk == 0:
            tot_ref[band * wide : band * wide + wide] = total
        else:
            tot_ref[band * wide : band * wide + wide] += total
        view = (pl.ds(chunk * many, many), pl.ds(2 * band, 2))
        copies.append(pltpu.make_async_copy(e_buf.at[view], e_out.at[view], e_sem.at[turn]))
        copies[-1].start()

    total = as_line(tot_ref[...]) + line_in[0:1]
    for member in range(line_ref.shape[0]):
        line_ref[member, 0:1] = total
        line_ref[member, 1:2] = line_in[1:2]
    for copy in copies:
        copy.wait()


def forward(ready, ready_far, line, got, got_sib, members):
    rows, wide = 4 * SLICE, 2 * SLICE
    e_shape, c_shape = ((6, 4, SLICE, PIECE), jnp.float32), ((6, PIECE, 2 * WIDTH), jnp.bfloat16)
    return pl.pallas_call(
        forward_kernel,
        in_specs=[HBM] * 2 + [pl.BlockSpec()] * 3,
        out_specs=[HBM] * 2 + [pl.BlockSpec()],
        out_shape=(
            pltpu.HBM(*e_shape),
            pltpu.HBM(*c_shape),
            jax.ShapeDtypeStruct((members, 2, rows), jnp.float32),
        ),
        scratch_shapes=[
            pltpu.VMEM((rows, 3 * WIDTH), jnp.bfloat16),
            pltpu.VMEM(*c_shape),
            pltpu.VMEM(*e_shape),
            pltpu.VMEM((rows, 128), jnp.float32),
            pltpu.SemaphoreType.DMA((2,)),
            pltpu.SemaphoreType.DMA((2,)),
            pltpu.SemaphoreType.DMA((4,)),
        ],
        cost_estimate=pl.CostEstimate(
            flops=12 * rows * wide * WIDTH, bytes_accessed=8 * rows * wide, transcendentals=2 * rows * wide
        ),
        compiler_params=params(VMEM_LARGE),
        name="forward",
    )(in_hbm(ready), in_hbm(ready_far), line, got, got_sib)


def denominator_kernel(member_ref, all_ref, row_ref, own_ref, line_ref, spread_ref):
    member = member_ref[0]
    members = all_ref.shape[0]

    def summed(owner, kind):
        value = 0.0
        for by, order in ((0, SELF), (2, 0), (members - 2, 1), (4, 3)):
            held = all_ref[lax.rem(owner + by, members)]
            value = value + held[kind : kind + 1, order * SLICE : order * SLICE + SLICE]
        return value

    mate = member + 1 - 2 * lax.rem(member, 2)
    own = summed(member, 0)
    line_ref[0:1] = own
    line_ref[1:2] = summed(member, 1)
    both = jnp.concatenate([own, summed(mate, 0)], axis=1)
    own_ref[...] = both
    spread_ref[...] = jnp.broadcast_to(both.reshape(1, 1, 2 * SLICE), spread_ref.shape)
    for order, by in enumerate((members - 2, 2, 0, 4)):
        value = own if by == 0 else summed(lax.rem(member + by, members), 0)
        row_ref[:, order * SLICE : order * SLICE + SLICE] = value


def denominators(member, everything, groups):
    return pl.pallas_call(
        denominator_kernel,
        in_specs=[SMEM, pl.BlockSpec()],
        out_shape=(
            jax.ShapeDtypeStruct((1, 4 * SLICE), jnp.float32),
            jax.ShapeDtypeStruct((1, 2 * SLICE), jnp.float32),
            jax.ShapeDtypeStruct((2, SLICE), jnp.float32),
            jax.ShapeDtypeStruct((groups, 1, 2 * SLICE), jnp.float32),
        ),
        compiler_params=params(),
        name="denominators",
    )(member, everything)


def backward_kernel(
    bands, first, partner_ref, row_ref, own_ref, everyone_ref, pos_ref, e0_in, e1_in, *refs
):
    if first:
        c0_in, c1_in, c_ref, refs = refs[0], refs[1], refs[2], refs[3:]
    else:
        c_ref, refs = refs[0], refs[1:]
    out_refs, (run_ref, e_buf, e_sem, c_sem) = refs[:-4], refs[-4:]
    own_pieces = e0_in.shape[0]
    copies = []
    for step, (start, many) in enumerate(STEPS):
        group = []
        for k, (source, low, high) in enumerate(
            ((0, 0, own_pieces), (1, own_pieces, own_pieces + e1_in.shape[0]))
        ):
            begin, end = max(start, low), min(start + many, high)
            if begin >= end:
                continue
            here, there = pl.ds(begin, end - begin), pl.ds(begin - low, end - begin)
            at = 0
            for which, (order, row, size) in enumerate(bands):
                group.append(
                    pltpu.make_async_copy(
                        (e0_in, e1_in)[source].at[there, order, pl.ds(row, size)],
                        e_buf.at[here, pl.ds(at, size)],
                        e_sem.at[step, k, which],
                    )
                )
                at += size
            if first:
                src = (c0_in, c1_in)[source].at[there]
                group.append(pltpu.make_async_copy(src, c_ref.at[here], c_sem.at[step, k]))
        copies.append(group)
        for copy in group:
            copy.start()

    columns, places = [], []
    for order, row, size in bands:
        column = as_column(row_ref[:, order * SLICE : order * SLICE + SLICE])
        columns.append(column[row : row + size])
        places.append(lax.broadcasted_iota(jnp.int32, (size, 128), 0) + (order * SLICE + row))
    row_inv = 1.0 / jnp.concatenate(columns, axis=0)
    row_ids = jnp.concatenate(places, axis=0)
    wide = 2 * SLICE
    col_inv = [1.0 / own_ref[...]] + [1.0 / everyone_ref[partner_ref[k]] for k in range(2)]
    for step, (start, many) in enumerate(STEPS):
        for copy in copies[step]:
            copy.wait()
        his, los = [], []
        for at in range(start * PIECE, (start + many) * PIECE, 128):
            inv = col_inv[at // wide][:, at % wide : at % wide + 128]
            weight = e_buf[at // PIECE, :, at % PIECE : at % PIECE + 128] * (row_inv + inv)
            if at < wide:
                weight = weight - jnp.where(row_ids == pos_ref[:, at : at + 128], 2.0, 0.0)
            hi, lo = split(weight)
            his.append(hi)
            los.append(lo)
        cols = c_ref[start : start + many].reshape(many * PIECE, 2 * WIDTH)
        c_hi, c_lo = cols[:, :WIDTH], cols[:, WIDTH:]
        part = jnp.dot(
            jnp.concatenate(his + his + los, axis=1),
            jnp.concatenate([c_hi, c_lo, c_hi], axis=0),
            preferred_element_type=jnp.float32,
        )
        if step == 0:
            run_ref[...] = part
        elif step + 1 < len(STEPS):
            run_ref[...] += part
        else:
            part = run_ref[...] + part
            size = part.shape[0] // len(out_refs)
            for which, ref in enumerate(out_refs):
                ref[...] = part[which * size : which * size + size]


def backward(bands, pieces, partners, row_den, own_den, everyone, pos, e0, e1, *cols):
    first = len(cols) == 2
    count = 9 * PIECE
    col_shape = [jax.ShapeDtypeStruct((9, PIECE, 2 * WIDTH), jnp.bfloat16)]
    return pl.pallas_call(
        functools.partial(backward_kernel, bands, first),
        in_specs=[SMEM] + [pl.BlockSpec()] * 4 + [HBM] * 2 + ([HBM] * 2 if first else [pl.BlockSpec()]),
        out_shape=col_shape * first + [jax.ShapeDtypeStruct((SLICE // pieces, WIDTH), jnp.float32)] * pieces,
        scratch_shapes=[
            pltpu.VMEM((SLICE, WIDTH), jnp.float32),
            pltpu.VMEM((9, SLICE, PIECE), jnp.float32),
            pltpu.SemaphoreType.DMA((len(STEPS), 2, len(bands))),
            pltpu.SemaphoreType.DMA((len(STEPS), 2)),
        ],
        cost_estimate=pl.CostEstimate(
            flops=6 * SLICE * count * WIDTH, bytes_accessed=4 * SLICE * count, transcendentals=0
        ),
        compiler_params=params(VMEM_BACKWARD),
        name="backward_%d_%d" % bands[0][:2],
    )(partners, row_den, own_den, everyone, pos, in_hbm(e0), in_hbm(e1), *(map(in_hbm, cols) if first else cols))


def add_kernel(a_ref, b_ref, c_ref, d_ref, ab_ref, cd_ref):
    ab_ref[...] = a_ref[...] + b_ref[...]
    cd_ref[...] = c_ref[...] + d_ref[...]


def add_pairs(a, b, c, d):
    out = jax.ShapeDtypeStruct(a.shape, jnp.float32)
    return pl.pallas_call(add_kernel, out_shape=(out, out), compiler_params=params(), name="add_pairs")(
        a, b, c, d
    )


def finish_kernel(emb_ref, run_ref, low0, low1, high0, high1, line_ref, loss_ref, grad_ref):
    values = emb_ref[...]
    radius = radius_of(values)
    unit = values / radius
    low, high = low0[...] + low1[...], high0[...] + high1[...]
    slope = (run_ref[...] + jnp.concatenate([low, high], axis=0)) / LOGIT_DIVISOR
    grad_ref[...] = (slope - unit * jnp.sum(unit * slope, axis=-1, keepdims=True)) / radius
    loss_ref[...] = (jnp.log(line_ref[0:1]) - line_ref[1:2]).reshape(loss_ref.shape)


def finish(embeddings, run, lows, highs, line):
    rows, width = embeddings.shape
    return pl.pallas_call(
        finish_kernel,
        out_shape=(
            jax.ShapeDtypeStruct((rows,), jnp.float32),
            jax.ShapeDtypeStruct((rows, width), jnp.float32),
        ),
        compiler_params=params(),
        name="finish",
    )(embeddings, run, *lows, *highs, line)


def local(embeddings, positive, pairing):
    rows, width = embeddings.shape
    members = lax.axis_size("mem")
    groups = lax.axis_size("grp")
    block = rows * members
    rounds = pairing.shape[0]
    group = lax.axis_index("grp")
    member = lax.axis_index("mem")
    half = rows // 2

    def shift(value, by):
        return lax.ppermute(value, "mem", [(m, (m + by) % members) for m in range(members)])

    def swap(value):
        return lax.ppermute(value, "mem", [(m, m ^ 1) for m in range(members)])

    left, right = shift(embeddings, 2), shift(embeddings, -2)
    far = (shift(left[:half], 2), shift(right[half:], -2))
    per = rows * width // (groups * 128)
    tiles = embeddings.reshape(rows // 8, 8, width // 128, 128).transpose(0, 2, 1, 3)
    pieces = lax.all_to_all(tiles.reshape(groups, per, 128), "grp", 0, 0, tiled=True)
    ready = prepare("prepare", left, right)
    picked, ready = lax.optimization_barrier((pick(pairing, pieces), ready))
    got = lax.all_to_all(picked, "grp", 0, 0, tiled=True)
    sib, pos_sib = swap(embeddings), swap(positive)

    both = jnp.concatenate([positive, pos_sib]) - group * block
    owner = both // rows
    turn = (owner // 2 - member // 2) % (members // 2)
    order = jnp.where(turn == 0, SELF, jnp.where(turn == 3, 0, jnp.where(turn == 1, 1, 3)))
    pos = jnp.where(owner % 2 == member % 2, order * rows + both % rows, -1).reshape(1, 2 * rows)

    ready_far = prepare("prepare_far", embeddings, *far)
    c_own, e_own, line = own_scores(ready, ready_far, embeddings, sib, pos)
    got, line = lax.optimization_barrier((got, line))
    e_part, c_part, line = forward(ready, ready_far, line, got, swap(got), members)

    everything = lax.all_to_all(line, "mem", 0, 0, tiled=True)
    row_den, own_den, line, spread = denominators(jnp.reshape(member, (1,)), everything, groups)
    everyone = lax.all_to_all(spread, "grp", 0, 0, tiled=True)

    shared = (pairing[:, group], row_den, own_den, everyone, pos, e_own, e_part)
    cols, far_low, far_high = backward(((3, 0, rows),), 2, *shared, c_own, c_part)
    shared += (cols,)
    far_low, far_high = shift(far_low, 2), shift(far_high, -2)
    left_low, right_high = backward(((0, 0, half), (1, half, half)), 2, *shared)
    high0, low1 = shift(right_high, 2), shift(left_low, -2)
    left_high, right_low = backward(((0, half, half), (1, 0, half)), 2, *shared)
    right_low, left_high = add_pairs(right_low, far_low, left_high, far_high)
    low0, high1 = shift(right_low, 2), shift(left_high, -2)
    (run,) = backward(((SELF, 0, rows),), 1, *shared)
    return finish(embeddings, run, (low0, low1), (high0, high1), line)


def solution(mesh):
    placed = (P(("grp", "mem"), None), P(("grp", "mem")), P())
    return jax.shard_map(
        local,
        mesh=mesh,
        in_specs=placed,
        out_specs=(P(("grp", "mem")), P(("grp", "mem"), None)),
        check_vma=False,
    )
```

```python
import functools

import jax
import jax.numpy as jnp
from jax import lax
from jax.experimental import pallas as pl
from jax.experimental.pallas import tpu as pltpu
from jax.sharding import PartitionSpec as P

LOGIT_DIVISOR = 0.1
EPSILON = 1e-06
SLICE = 384
WIDTH = 256
SELF = 2
PIECE = 256
STEPS = ((0, 3), (3, 3), (6, 3))
VMEM = 16 * 1024 * 1024
VMEM_LARGE = 44 * 1024 * 1024
VMEM_BACKWARD = 28 * 1024 * 1024
HBM = pl.BlockSpec(memory_space=pltpu.HBM)
SMEM = pl.BlockSpec(memory_space=pltpu.SMEM)


def split(values):
    hi = values.astype(jnp.bfloat16)
    lo = (values - hi.astype(jnp.float32)).astype(jnp.bfloat16)
    return hi, lo


def rows_of(tiles):
    pairs = tiles.reshape(tiles.shape[0] // 2, 2, 8, 128)
    rows = tiles.shape[0] * 4
    return jnp.concatenate([pairs[:, 0].reshape(rows, 128), pairs[:, 1].reshape(rows, 128)], axis=1)


def radius_of(values):
    return jnp.sqrt(jnp.sum(values * values, axis=-1, keepdims=True) + EPSILON)


def as_column(line):
    return jnp.broadcast_to(line, (128, line.shape[1])).T


def in_hbm(value):
    return pltpu.with_memory_space_constraint(value, pltpu.HBM)


def params(limit=VMEM):
    return pltpu.CompilerParams(vmem_limit_bytes=limit)


def pick_kernel(place_ref, same_ref, other_ref, out_ref):
    size = same_ref.shape[1]
    for which in range(out_ref.shape[1] // size):
        for column in range(out_ref.shape[0]):
            place = place_ref[which, column]
            near = jnp.full((size, 128), place_ref[which + 2, column]) == 1
            piece = jnp.where(near, same_ref[place], other_ref[place])
            out_ref[column, which * size : which * size + size] = piece


def pick(places, same, other):
    columns, size, _ = same.shape
    rounds = places.shape[0] // 2
    return pl.pallas_call(
        pick_kernel,
        in_specs=[SMEM] + [pl.BlockSpec()] * 2,
        out_shape=jax.ShapeDtypeStruct((columns, rounds * size, 128), jnp.float32),
        compiler_params=params(),
        name="pick",
    )(places, same, other)


def scaled_rows(refs, out_ref, at=0):
    for ref in refs:
        values = ref[...]
        hi, lo = split(values * (1.0 / (radius_of(values) * LOGIT_DIVISOR)))
        out_ref[at : at + hi.shape[0]] = jnp.concatenate([hi, lo, hi], axis=1)
        at += hi.shape[0]


def unit_parts(values):
    hi, lo = split(values * (1.0 / radius_of(values)))
    return jnp.concatenate([hi, lo], axis=1)


def product(left, cols):
    hi, lo = cols[:, :WIDTH], cols[:, WIDTH:]
    return lax.dot_general(
        left,
        jnp.concatenate([hi, hi, lo], axis=1),
        (((1,), (1,)), ((), ())),
        preferred_element_type=jnp.float32,
    )


def exponentials(scores, first_row, pos_ref, store):
    height = scores.shape[0]
    total = jnp.zeros((height, 128), jnp.float32)
    match = jnp.zeros((height, 128), jnp.float32)
    if first_row is not None:
        row_ids = lax.broadcasted_iota(jnp.int32, (height, 128), 0) + first_row
        lane_ids = lax.broadcasted_iota(jnp.int32, (height, 128), 1)
    for k in range(0, scores.shape[1], 128):
        score = scores[:, k : k + 128]
        e = jnp.exp(score)
        if first_row is not None:
            match = match + jnp.where(row_ids == pos_ref[:, k : k + 128], score, 0.0)
            if first_row <= SELF * SLICE < first_row + height and k < SLICE:
                e = jnp.where(row_ids - SELF * SLICE == lane_ids + k, 0.0, e)
        total = total + e
        store(k, e)
    return total, match


def as_line(total):
    return jnp.sum(total.T, axis=0, keepdims=True)


def put_columns(c_buf, at, parts):
    done = 0
    while done < parts.shape[0]:
        inside = (at + done) % PIECE
        size = min(PIECE - inside, parts.shape[0] - done)
        c_buf[(at + done) // PIECE, inside : inside + size] = parts[done : done + size]
        done += size


def own_kernel(
    ready, ready_far, mine, sib, pos_ref, c_out, e_out, line_ref, left_ref, c_buf, e_buf, in_sem, c_sem, e_sem
):
    at = ready.shape[0]
    ready_copies = [
        pltpu.make_async_copy(ready, left_ref.at[pl.ds(0, at)], in_sem.at[0]),
        pltpu.make_async_copy(ready_far, left_ref.at[pl.ds(at, ready_far.shape[0])], in_sem.at[1]),
    ]
    for copy in ready_copies:
        copy.start()
    for which, ref in enumerate((mine, sib)):
        put_columns(c_buf, which * SLICE, unit_parts(ref[...]))
    cols = c_buf[...].reshape(2 * SLICE, 2 * WIDTH)
    copies = [pltpu.make_async_copy(c_buf, c_out, c_sem)]
    copies[0].start()
    for copy in ready_copies:
        copy.wait()

    coming = product(left_ref[:SLICE], cols)
    totals, matches = [], []
    for order in range(4):
        scores = coming
        if order < 3:
            at = (order + 1) * SLICE
            coming = product(left_ref[at : at + SLICE], cols)

        def store(k, e):
            e_buf[k // PIECE, order, :, k % PIECE : k % PIECE + 128] = e

        total, match = exponentials(scores, order * SLICE, pos_ref, store)
        totals.append(as_line(total))
        matches.append(as_line(match))
        copies.append(pltpu.make_async_copy(e_buf.at[:, order], e_out.at[:, order], e_sem.at[order]))
        copies[-1].start()
    line_ref[0:1] = jnp.concatenate(totals, axis=1)
    line_ref[1:2] = jnp.concatenate(matches, axis=1)
    for copy in copies:
        copy.wait()


def own_scores(ready, ready_far, mine, sib, pos):
    rows, wide = 4 * SLICE, 2 * SLICE
    shapes = [((3, PIECE, 2 * WIDTH), jnp.bfloat16), ((3, 4, SLICE, PIECE), jnp.float32)]
    return pl.pallas_call(
        own_kernel,
        in_specs=[HBM] * 2 + [pl.BlockSpec()] * 3,
        out_specs=[HBM] * 2 + [pl.BlockSpec()],
        out_shape=[pltpu.HBM(*shape) for shape in shapes] + [jax.ShapeDtypeStruct((2, rows), jnp.float32)],
        scratch_shapes=[
            pltpu.VMEM((rows, 3 * WIDTH), jnp.bfloat16),
            pltpu.VMEM(*shapes[0]),
            pltpu.VMEM(*shapes[1]),
            pltpu.SemaphoreType.DMA((2,)),
            pltpu.SemaphoreType.DMA,
            pltpu.SemaphoreType.DMA((4,)),
        ],
        cost_estimate=pl.CostEstimate(
            flops=6 * rows * wide * WIDTH, bytes_accessed=4 * rows * wide, transcendentals=rows * wide
        ),
        compiler_params=params(VMEM_LARGE),
        name="own_scores",
    )(in_hbm(ready), in_hbm(ready_far), mine, sib, pos)


def prepare_kernel(*refs):
    pieces, (out_ref, buf, sem) = refs[:-3], refs[-3:]
    scaled_rows(pieces, buf)
    copy = pltpu.make_async_copy(buf, out_ref, sem)
    copy.start()
    copy.wait()


def prepare(name, *pieces):
    rows = sum(piece.shape[0] for piece in pieces)
    shape = ((rows, 3 * WIDTH), jnp.bfloat16)
    return pl.pallas_call(
        prepare_kernel,
        out_specs=HBM,
        out_shape=pltpu.HBM(*shape),
        scratch_shapes=[pltpu.VMEM(*shape), pltpu.SemaphoreType.DMA],
        cost_estimate=pl.CostEstimate(flops=20 * 10**9, bytes_accessed=8 * rows * WIDTH, transcendentals=0),
        compiler_params=params(),
        name=name,
    )(*pieces)


def forward_kernel(
    ready, ready_far, line_in, got, got_sib, e_out, c_out, line_ref,
    left_ref, c_buf, e_buf, tot_ref, in_sem, c_sem, e_sem,
):
    orders, wide = e_buf.shape[1], 2 * SLICE
    many = wide // PIECE
    chunks = e_buf.shape[0] // many
    at = ready.shape[0]
    ready_copies = [
        pltpu.make_async_copy(ready, left_ref.at[pl.ds(0, at)], in_sem.at[0]),
        pltpu.make_async_copy(ready_far, left_ref.at[pl.ds(at, ready_far.shape[0])], in_sem.at[1]),
    ]
    for copy in ready_copies:
        copy.start()
    half = got.shape[1] // 2
    tiles = got.shape[0] * half // 8
    copies = []

    def columns(chunk):
        for which, ref in enumerate((got, got_sib)):
            piece = rows_of(ref[:, chunk * half : chunk * half + half].reshape(tiles, 8, 128))
            put_columns(c_buf, chunk * wide + which * SLICE, unit_parts(piece))
        view = (pl.ds(chunk * many, many),)
        copies.append(pltpu.make_async_copy(c_buf.at[view], c_out.at[view], c_sem.at[chunk]))
        copies[-1].start()

    def scores_of(chunk, band):
        cols = c_buf[chunk * many : chunk * many + many].reshape(wide, 2 * WIDTH)
        return product(left_ref[band * wide : band * wide + wide], cols)

    columns(0)
    for copy in ready_copies:
        copy.wait()
    items = [(chunk, band) for chunk in range(chunks) for band in range(orders // 2)]
    coming = scores_of(*items[0])
    for turn, (chunk, band) in enumerate(items):
        scores = coming
        if turn + 1 < len(items):
            if items[turn + 1][0] != chunk:
                columns(items[turn + 1][0])
            coming = scores_of(*items[turn + 1])

        def store(k, e):
            lane = k % PIECE
            e = e.reshape(2, SLICE, 128)
            e_buf[chunk * many + k // PIECE, 2 * band : 2 * band + 2, :, lane : lane + 128] = e

        total, _ = exponentials(scores, None, None, store)
        if chunk == 0:
            tot_ref[band * wide : band * wide + wide] = total
        else:
            tot_ref[band * wide : band * wide + wide] += total
        view = (pl.ds(chunk * many, many), pl.ds(2 * band, 2))
        copies.append(pltpu.make_async_copy(e_buf.at[view], e_out.at[view], e_sem.at[turn]))
        copies[-1].start()

    total = as_line(tot_ref[...]) + line_in[0:1]
    for member in range(line_ref.shape[0]):
        line_ref[member, 0:1] = total
        line_ref[member, 1:2] = line_in[1:2]
    for copy in copies:
        copy.wait()


def forward(ready, ready_far, line, got, got_sib, members):
    rows, wide = 4 * SLICE, 2 * SLICE
    e_shape, c_shape = ((6, 4, SLICE, PIECE), jnp.float32), ((6, PIECE, 2 * WIDTH), jnp.bfloat16)
    return pl.pallas_call(
        forward_kernel,
        in_specs=[HBM] * 2 + [pl.BlockSpec()] * 3,
        out_specs=[HBM] * 2 + [pl.BlockSpec()],
        out_shape=(
            pltpu.HBM(*e_shape),
            pltpu.HBM(*c_shape),
            jax.ShapeDtypeStruct((members, 2, rows), jnp.float32),
        ),
        scratch_shapes=[
            pltpu.VMEM((rows, 3 * WIDTH), jnp.bfloat16),
            pltpu.VMEM(*c_shape),
            pltpu.VMEM(*e_shape),
            pltpu.VMEM((rows, 128), jnp.float32),
            pltpu.SemaphoreType.DMA((2,)),
            pltpu.SemaphoreType.DMA((2,)),
            pltpu.SemaphoreType.DMA((4,)),
        ],
        cost_estimate=pl.CostEstimate(
            flops=12 * rows * wide * WIDTH, bytes_accessed=8 * rows * wide, transcendentals=2 * rows * wide
        ),
        compiler_params=params(VMEM_LARGE),
        name="forward",
    )(in_hbm(ready), in_hbm(ready_far), line, got, got_sib)


def denominator_kernel(member_ref, all_ref, row_ref, own_ref, line_ref, spread_ref):
    member = member_ref[0]
    members = all_ref.shape[0]

    def summed(owner, kind):
        value = 0.0
        for by, order in ((0, SELF), (2, 0), (members - 2, 1), (4, 3)):
            held = all_ref[lax.rem(owner + by, members)]
            value = value + held[kind : kind + 1, order * SLICE : order * SLICE + SLICE]
        return value

    mate = member + 1 - 2 * lax.rem(member, 2)
    own = summed(member, 0)
    line_ref[0:1] = own
    line_ref[1:2] = summed(member, 1)
    both = jnp.concatenate([own, summed(mate, 0)], axis=1)
    own_ref[...] = both
    spread_ref[...] = jnp.broadcast_to(both.reshape(1, 1, 2 * SLICE), spread_ref.shape)
    for order, by in enumerate((members - 2, 2, 0, 4)):
        value = own if by == 0 else summed(lax.rem(member + by, members), 0)
        row_ref[:, order * SLICE : order * SLICE + SLICE] = value


def denominators(member, everything, groups):
    return pl.pallas_call(
        denominator_kernel,
        in_specs=[SMEM, pl.BlockSpec()],
        out_shape=(
            jax.ShapeDtypeStruct((1, 4 * SLICE), jnp.float32),
            jax.ShapeDtypeStruct((1, 2 * SLICE), jnp.float32),
            jax.ShapeDtypeStruct((2, SLICE), jnp.float32),
            jax.ShapeDtypeStruct((groups, 1, 2 * SLICE), jnp.float32),
        ),
        compiler_params=params(),
        name="denominators",
    )(member, everything)


def backward_kernel(
    bands, first, partner_ref, row_ref, own_ref, same_ref, other_ref, pos_ref, e0_in, e1_in, *refs
):
    if first:
        c0_in, c1_in, c_ref, refs = refs[0], refs[1], refs[2], refs[3:]
    else:
        c_ref, refs = refs[0], refs[1:]
    out_refs, (run_ref, e_buf, e_sem, c_sem) = refs[:-4], refs[-4:]
    own_pieces = e0_in.shape[0]
    copies = []
    for step, (start, many) in enumerate(STEPS):
        group = []
        for k, (source, low, high) in enumerate(
            ((0, 0, own_pieces), (1, own_pieces, own_pieces + e1_in.shape[0]))
        ):
            begin, end = max(start, low), min(start + many, high)
            if begin >= end:
                continue
            here, there = pl.ds(begin, end - begin), pl.ds(begin - low, end - begin)
            at = 0
            for which, (order, row, size) in enumerate(bands):
                group.append(
                    pltpu.make_async_copy(
                        (e0_in, e1_in)[source].at[there, order, pl.ds(row, size)],
                        e_buf.at[here, pl.ds(at, size)],
                        e_sem.at[step, k, which],
                    )
                )
                at += size
            if first:
                src = (c0_in, c1_in)[source].at[there]
                group.append(pltpu.make_async_copy(src, c_ref.at[here], c_sem.at[step, k]))
        copies.append(group)
        for copy in group:
            copy.start()

    columns, places = [], []
    for order, row, size in bands:
        column = as_column(row_ref[:, order * SLICE : order * SLICE + SLICE])
        columns.append(column[row : row + size])
        places.append(lax.broadcasted_iota(jnp.int32, (size, 128), 0) + (order * SLICE + row))
    row_inv = 1.0 / jnp.concatenate(columns, axis=0)
    row_ids = jnp.concatenate(places, axis=0)
    wide = 2 * SLICE
    col_inv = [1.0 / own_ref[...]]
    for k in range(2):
        place = partner_ref[k]
        near = jnp.full((1, wide), partner_ref[k + 2]) == 1
        col_inv.append(1.0 / jnp.where(near, same_ref[place], other_ref[place]))
    for step, (start, many) in enumerate(STEPS):
        for copy in copies[step]:
            copy.wait()
        his, los = [], []
        for at in range(start * PIECE, (start + many) * PIECE, 128):
            inv = col_inv[at // wide][:, at % wide : at % wide + 128]
            weight = e_buf[at // PIECE, :, at % PIECE : at % PIECE + 128] * (row_inv + inv)
            if at < wide:
                weight = weight - jnp.where(row_ids == pos_ref[:, at : at + 128], 2.0, 0.0)
            hi, lo = split(weight)
            his.append(hi)
            los.append(lo)
        cols = c_ref[start : start + many].reshape(many * PIECE, 2 * WIDTH)
        c_hi, c_lo = cols[:, :WIDTH], cols[:, WIDTH:]
        part = jnp.dot(
            jnp.concatenate(his + his + los, axis=1),
            jnp.concatenate([c_hi, c_lo, c_hi], axis=0),
            preferred_element_type=jnp.float32,
        )
        if step == 0:
            run_ref[...] = part
        elif step + 1 < len(STEPS):
            run_ref[...] += part
        else:
            part = run_ref[...] + part
            size = part.shape[0] // len(out_refs)
            for which, ref in enumerate(out_refs):
                ref[...] = part[which * size : which * size + size]


def backward(bands, pieces, partners, row_den, own_den, same, other, pos, e0, e1, *cols):
    first = len(cols) == 2
    count = 9 * PIECE
    col_shape = [jax.ShapeDtypeStruct((9, PIECE, 2 * WIDTH), jnp.bfloat16)]
    return pl.pallas_call(
        functools.partial(backward_kernel, bands, first),
        in_specs=[SMEM] + [pl.BlockSpec()] * 5 + [HBM] * 2 + ([HBM] * 2 if first else [pl.BlockSpec()]),
        out_shape=col_shape * first + [jax.ShapeDtypeStruct((SLICE // pieces, WIDTH), jnp.float32)] * pieces,
        scratch_shapes=[
            pltpu.VMEM((SLICE, WIDTH), jnp.float32),
            pltpu.VMEM((9, SLICE, PIECE), jnp.float32),
            pltpu.SemaphoreType.DMA((len(STEPS), 2, len(bands))),
            pltpu.SemaphoreType.DMA((len(STEPS), 2)),
        ],
        cost_estimate=pl.CostEstimate(
            flops=6 * SLICE * count * WIDTH, bytes_accessed=4 * SLICE * count, transcendentals=0
        ),
        compiler_params=params(VMEM_BACKWARD),
        name="backward_%d_%d" % bands[0][:2],
    )(partners, row_den, own_den, same, other, pos, in_hbm(e0), in_hbm(e1), *(map(in_hbm, cols) if first else cols))


def add_kernel(a_ref, b_ref, c_ref, d_ref, ab_ref, cd_ref):
    ab_ref[...] = a_ref[...] + b_ref[...]
    cd_ref[...] = c_ref[...] + d_ref[...]


def add_pairs(a, b, c, d):
    out = jax.ShapeDtypeStruct(a.shape, jnp.float32)
    return pl.pallas_call(add_kernel, out_shape=(out, out), compiler_params=params(), name="add_pairs")(
        a, b, c, d
    )


def finish_kernel(emb_ref, run_ref, low0, low1, high0, high1, line_ref, loss_ref, grad_ref):
    values = emb_ref[...]
    radius = radius_of(values)
    unit = values / radius
    low, high = low0[...] + low1[...], high0[...] + high1[...]
    slope = (run_ref[...] + jnp.concatenate([low, high], axis=0)) / LOGIT_DIVISOR
    grad_ref[...] = (slope - unit * jnp.sum(unit * slope, axis=-1, keepdims=True)) / radius
    loss_ref[...] = (jnp.log(line_ref[0:1]) - line_ref[1:2]).reshape(loss_ref.shape)


def finish(embeddings, run, lows, highs, line):
    rows, width = embeddings.shape
    return pl.pallas_call(
        finish_kernel,
        out_shape=(
            jax.ShapeDtypeStruct((rows,), jnp.float32),
            jax.ShapeDtypeStruct((rows, width), jnp.float32),
        ),
        compiler_params=params(),
        name="finish",
    )(embeddings, run, *lows, *highs, line)


def local(embeddings, positive, pairing):
    rows, width = embeddings.shape
    members = lax.axis_size("mem")
    groups = lax.axis_size("grp")
    block = rows * members
    rounds = pairing.shape[0]
    group = lax.axis_index("grp")
    member = lax.axis_index("mem")
    half = rows // 2

    def shift(value, by):
        return lax.ppermute(value, "mem", [(m, (m + by) % members) for m in range(members)])

    def swap(value):
        return lax.ppermute(value, "mem", [(m, m ^ 1) for m in range(members)])

    layers = [list(range(layer, groups, 2)) for layer in range(2)]
    columns = groups // 2

    def across(value):
        return lax.all_to_all(value, "grp", 0, 0, tiled=True, axis_index_groups=layers)

    def flip(value):
        return lax.ppermute(value, "grp", [(g, g ^ 1) for g in range(groups)])

    layer = group % 2
    mates = jnp.where(layer == 0, pairing[:, 0::2], pairing[:, 1::2])
    places = jnp.concatenate([mates // 2, (mates % 2 == layer).astype(jnp.int32)])
    partners = lax.dynamic_index_in_dim(places, group // 2, 1, keepdims=False)

    left, right = shift(embeddings, 2), shift(embeddings, -2)
    far = (shift(left[:half], 2), shift(right[half:], -2))
    per = rows * width // (columns * 128)
    tiles = embeddings.reshape(rows // 8, 8, width // 128, 128).transpose(0, 2, 1, 3)
    pieces = across(tiles.reshape(columns, per, 128))
    ready = prepare("prepare", left, right)
    picked, ready = lax.optimization_barrier((pick(places, pieces, flip(pieces)), ready))
    got = across(picked)
    sib, pos_sib = swap(embeddings), swap(positive)

    both = jnp.concatenate([positive, pos_sib]) - group * block
    owner = both // rows
    turn = (owner // 2 - member // 2) % (members // 2)
    order = jnp.where(turn == 0, SELF, jnp.where(turn == 3, 0, jnp.where(turn == 1, 1, 3)))
    pos = jnp.where(owner % 2 == member % 2, order * rows + both % rows, -1).reshape(1, 2 * rows)

    ready_far = prepare("prepare_far", embeddings, *far)
    c_own, e_own, line = own_scores(ready, ready_far, embeddings, sib, pos)
    got, line = lax.optimization_barrier((got, line))
    e_part, c_part, line = forward(ready, ready_far, line, got, swap(got), members)

    everything = lax.all_to_all(line, "mem", 0, 0, tiled=True)
    row_den, own_den, line, spread = denominators(jnp.reshape(member, (1,)), everything, columns)
    same = across(spread)

    shared = (partners, row_den, own_den, same, flip(same), pos, e_own, e_part)
    cols, far_low, far_high = backward(((3, 0, rows),), 2, *shared, c_own, c_part)
    shared += (cols,)
    far_low, far_high = shift(far_low, 2), shift(far_high, -2)
    left_low, right_high = backward(((0, 0, half), (1, half, half)), 2, *shared)
    high0, low1 = shift(right_high, 2), shift(left_low, -2)
    left_high, right_low = backward(((0, half, half), (1, 0, half)), 2, *shared)
    right_low, left_high = add_pairs(right_low, far_low, left_high, far_high)
    low0, high1 = shift(right_low, 2), shift(left_high, -2)
    (run,) = backward(((SELF, 0, rows),), 1, *shared)
    return finish(embeddings, run, (low0, low1), (high0, high1), line)


def solution(mesh):
    placed = (P(("grp", "mem"), None), P(("grp", "mem")), P())
    return jax.shard_map(
        local,
        mesh=mesh,
        in_specs=placed,
        out_specs=(P(("grp", "mem")), P(("grp", "mem"), None)),
        check_vma=False,
    )
```

```python
import functools

import jax
import jax.numpy as jnp
from jax import lax
from jax.experimental import pallas as pl
from jax.experimental.pallas import tpu as pltpu
from jax.sharding import PartitionSpec as P

LOGIT_DIVISOR = 0.1
EPSILON = 1e-06
SLICE = 384
WIDTH = 256
SELF = 2
PIECE = 256
STEPS = ((0, 3), (3, 3), (6, 3))
VMEM = 16 * 1024 * 1024
VMEM_LARGE = 44 * 1024 * 1024
VMEM_BACKWARD = 28 * 1024 * 1024
HBM = pl.BlockSpec(memory_space=pltpu.HBM)
SMEM = pl.BlockSpec(memory_space=pltpu.SMEM)


def split(values):
    hi = values.astype(jnp.bfloat16)
    lo = (values - hi.astype(jnp.float32)).astype(jnp.bfloat16)
    return hi, lo


def rows_of(tiles):
    pairs = tiles.reshape(tiles.shape[0] // 2, 2, 8, 128)
    rows = tiles.shape[0] * 4
    return jnp.concatenate([pairs[:, 0].reshape(rows, 128), pairs[:, 1].reshape(rows, 128)], axis=1)


def radius_of(values):
    return jnp.sqrt(jnp.sum(values * values, axis=-1, keepdims=True) + EPSILON)


def as_column(line):
    return jnp.broadcast_to(line, (128, line.shape[1])).T


def in_hbm(value):
    return pltpu.with_memory_space_constraint(value, pltpu.HBM)


def params(limit=VMEM):
    return pltpu.CompilerParams(vmem_limit_bytes=limit)


def pick_kernel(pairing_ref, pieces_ref, out_ref):
    size = pieces_ref.shape[1]
    for which in range(out_ref.shape[1] // size):
        for group in range(out_ref.shape[0]):
            out_ref[group, which * size : which * size + size] = pieces_ref[pairing_ref[which, group]]


def pick(pairing, pieces):
    rounds, groups = pairing.shape
    return pl.pallas_call(
        pick_kernel,
        in_specs=[SMEM, pl.BlockSpec()],
        out_shape=jax.ShapeDtypeStruct((groups, rounds * pieces.shape[1], 128), jnp.float32),
        compiler_params=params(),
        name="pick",
    )(pairing, pieces)


def scaled_rows(refs, out_ref, at=0):
    for ref in refs:
        values = ref[...]
        hi, lo = split(values * (1.0 / (radius_of(values) * LOGIT_DIVISOR)))
        out_ref[at : at + hi.shape[0]] = jnp.concatenate([hi, lo, hi], axis=1)
        at += hi.shape[0]


def unit_parts(values):
    hi, lo = split(values * (1.0 / radius_of(values)))
    return jnp.concatenate([hi, lo], axis=1)


def product(left, cols):
    hi, lo = cols[:, :WIDTH], cols[:, WIDTH:]
    return lax.dot_general(
        left,
        jnp.concatenate([hi, hi, lo], axis=1),
        (((1,), (1,)), ((), ())),
        preferred_element_type=jnp.float32,
    )


def exponentials(scores, first_row, pos_ref, store):
    height = scores.shape[0]
    total = jnp.zeros((height, 128), jnp.float32)
    match = jnp.zeros((height, 128), jnp.float32)
    if first_row is not None:
        row_ids = lax.broadcasted_iota(jnp.int32, (height, 128), 0) + first_row
        lane_ids = lax.broadcasted_iota(jnp.int32, (height, 128), 1)
    for k in range(0, scores.shape[1], 128):
        score = scores[:, k : k + 128]
        e = jnp.exp(score)
        if first_row is not None:
            match = match + jnp.where(row_ids == pos_ref[:, k : k + 128], score, 0.0)
            if first_row <= SELF * SLICE < first_row + height and k < SLICE:
                e = jnp.where(row_ids - SELF * SLICE == lane_ids + k, 0.0, e)
        total = total + e
        store(k, e)
    return total, match


def as_line(total):
    return jnp.sum(total.T, axis=0, keepdims=True)


def put_columns(c_buf, at, parts):
    done = 0
    while done < parts.shape[0]:
        inside = (at + done) % PIECE
        size = min(PIECE - inside, parts.shape[0] - done)
        c_buf[(at + done) // PIECE, inside : inside + size] = parts[done : done + size]
        done += size


def own_kernel(
    ready, ready_far, mine, sib, pos_ref, c_out, e_out, line_ref, left_ref, c_buf, e_buf, in_sem, c_sem, e_sem
):
    at = ready.shape[0]
    ready_copies = [
        pltpu.make_async_copy(ready, left_ref.at[pl.ds(0, at)], in_sem.at[0]),
        pltpu.make_async_copy(ready_far, left_ref.at[pl.ds(at, ready_far.shape[0])], in_sem.at[1]),
    ]
    for copy in ready_copies:
        copy.start()
    for which, ref in enumerate((mine, sib)):
        put_columns(c_buf, which * SLICE, unit_parts(ref[...]))
    cols = c_buf[...].reshape(2 * SLICE, 2 * WIDTH)
    copies = [pltpu.make_async_copy(c_buf, c_out, c_sem)]
    copies[0].start()
    for copy in ready_copies:
        copy.wait()

    coming = product(left_ref[:SLICE], cols)
    totals, matches = [], []
    for order in range(4):
        scores = coming
        if order < 3:
            at = (order + 1) * SLICE
            coming = product(left_ref[at : at + SLICE], cols)

        def store(k, e):
            e_buf[k // PIECE, order, :, k % PIECE : k % PIECE + 128] = e

        total, match = exponentials(scores, order * SLICE, pos_ref, store)
        totals.append(as_line(total))
        matches.append(as_line(match))
        copies.append(pltpu.make_async_copy(e_buf.at[:, order], e_out.at[:, order], e_sem.at[order]))
        copies[-1].start()
    line_ref[0:1] = jnp.concatenate(totals, axis=1)
    line_ref[1:2] = jnp.concatenate(matches, axis=1)
    for copy in copies:
        copy.wait()


def own_scores(ready, ready_far, mine, sib, pos):
    rows, wide = 4 * SLICE, 2 * SLICE
    shapes = [((3, PIECE, 2 * WIDTH), jnp.bfloat16), ((3, 4, SLICE, PIECE), jnp.float32)]
    return pl.pallas_call(
        own_kernel,
        in_specs=[HBM] * 2 + [pl.BlockSpec()] * 3,
        out_specs=[HBM] * 2 + [pl.BlockSpec()],
        out_shape=[pltpu.HBM(*shape) for shape in shapes] + [jax.ShapeDtypeStruct((2, rows), jnp.float32)],
        scratch_shapes=[
            pltpu.VMEM((rows, 3 * WIDTH), jnp.bfloat16),
            pltpu.VMEM(*shapes[0]),
            pltpu.VMEM(*shapes[1]),
            pltpu.SemaphoreType.DMA((2,)),
            pltpu.SemaphoreType.DMA,
            pltpu.SemaphoreType.DMA((4,)),
        ],
        cost_estimate=pl.CostEstimate(
            flops=6 * rows * wide * WIDTH, bytes_accessed=4 * rows * wide, transcendentals=rows * wide
        ),
        compiler_params=params(VMEM_LARGE),
        name="own_scores",
    )(in_hbm(ready), in_hbm(ready_far), mine, sib, pos)


def prepare_kernel(*refs):
    pieces, (out_ref, buf, sem) = refs[:-3], refs[-3:]
    scaled_rows(pieces, buf)
    copy = pltpu.make_async_copy(buf, out_ref, sem)
    copy.start()
    copy.wait()


def prepare(name, *pieces):
    rows = sum(piece.shape[0] for piece in pieces)
    shape = ((rows, 3 * WIDTH), jnp.bfloat16)
    return pl.pallas_call(
        prepare_kernel,
        out_specs=HBM,
        out_shape=pltpu.HBM(*shape),
        scratch_shapes=[pltpu.VMEM(*shape), pltpu.SemaphoreType.DMA],
        cost_estimate=pl.CostEstimate(flops=20 * 10**9, bytes_accessed=8 * rows * WIDTH, transcendentals=0),
        compiler_params=params(),
        name=name,
    )(*pieces)


def forward_kernel(
    ready, ready_far, line_in, got, got_sib, e_out, c_out, line_ref,
    left_ref, c_buf, e_buf, tot_ref, in_sem, c_sem, e_sem,
):
    orders, wide = e_buf.shape[1], 2 * SLICE
    many = wide // PIECE
    chunks = e_buf.shape[0] // many
    at = ready.shape[0]
    ready_copies = [
        pltpu.make_async_copy(ready, left_ref.at[pl.ds(0, at)], in_sem.at[0]),
        pltpu.make_async_copy(ready_far, left_ref.at[pl.ds(at, ready_far.shape[0])], in_sem.at[1]),
    ]
    for copy in ready_copies:
        copy.start()
    half = got.shape[1] // 2
    tiles = got.shape[0] * half // 8
    copies = []

    def columns(chunk):
        for which, ref in enumerate((got, got_sib)):
            piece = rows_of(ref[:, chunk * half : chunk * half + half].reshape(tiles, 8, 128))
            put_columns(c_buf, chunk * wide + which * SLICE, unit_parts(piece))
        view = (pl.ds(chunk * many, many),)
        copies.append(pltpu.make_async_copy(c_buf.at[view], c_out.at[view], c_sem.at[chunk]))
        copies[-1].start()

    def scores_of(chunk, band):
        cols = c_buf[chunk * many : chunk * many + many].reshape(wide, 2 * WIDTH)
        return product(left_ref[band * wide : band * wide + wide], cols)

    columns(0)
    ready_copies[0].wait()
    items = [(chunk, band) for chunk in range(chunks) for band in range(orders // 2)]
    coming = scores_of(*items[0])
    ready_copies[1].wait()
    for turn, (chunk, band) in enumerate(items):
        scores = coming
        if turn + 1 < len(items):
            if items[turn + 1][0] != chunk:
                columns(items[turn + 1][0])
            coming = scores_of(*items[turn + 1])

        def store(k, e):
            lane = k % PIECE
            e = e.reshape(2, SLICE, 128)
            e_buf[chunk * many + k // PIECE, 2 * band : 2 * band + 2, :, lane : lane + 128] = e

        total, _ = exponentials(scores, None, None, store)
        if chunk == 0:
            tot_ref[band * wide : band * wide + wide] = total
        else:
            tot_ref[band * wide : band * wide + wide] += total
        view = (pl.ds(chunk * many, many), pl.ds(2 * band, 2))
        copies.append(pltpu.make_async_copy(e_buf.at[view], e_out.at[view], e_sem.at[turn]))
        copies[-1].start()

    total = as_line(tot_ref[...]) + line_in[0:1]
    for member in range(line_ref.shape[0]):
        line_ref[member, 0:1] = total
        line_ref[member, 1:2] = line_in[1:2]
    for copy in copies:
        copy.wait()


def forward(ready, ready_far, line, got, got_sib, members):
    rows, wide = 4 * SLICE, 2 * SLICE
    e_shape, c_shape = ((6, 4, SLICE, PIECE), jnp.float32), ((6, PIECE, 2 * WIDTH), jnp.bfloat16)
    return pl.pallas_call(
        forward_kernel,
        in_specs=[HBM] * 2 + [pl.BlockSpec()] * 3,
        out_specs=[HBM] * 2 + [pl.BlockSpec()],
        out_shape=(
            pltpu.HBM(*e_shape),
            pltpu.HBM(*c_shape),
            jax.ShapeDtypeStruct((members, 2, rows), jnp.float32),
        ),
        scratch_shapes=[
            pltpu.VMEM((rows, 3 * WIDTH), jnp.bfloat16),
            pltpu.VMEM(*c_shape),
            pltpu.VMEM(*e_shape),
            pltpu.VMEM((rows, 128), jnp.float32),
            pltpu.SemaphoreType.DMA((2,)),
            pltpu.SemaphoreType.DMA((2,)),
            pltpu.SemaphoreType.DMA((4,)),
        ],
        cost_estimate=pl.CostEstimate(
            flops=12 * rows * wide * WIDTH, bytes_accessed=8 * rows * wide, transcendentals=2 * rows * wide
        ),
        compiler_params=params(VMEM_LARGE),
        name="forward",
    )(in_hbm(ready), in_hbm(ready_far), line, got, got_sib)


def denominator_kernel(member_ref, all_ref, row_ref, own_ref, line_ref, spread_ref):
    member = member_ref[0]
    members = all_ref.shape[0]

    def summed(owner, kind):
        value = 0.0
        for by, order in ((0, SELF), (2, 0), (members - 2, 1), (4, 3)):
            held = all_ref[lax.rem(owner + by, members)]
            value = value + held[kind : kind + 1, order * SLICE : order * SLICE + SLICE]
        return value

    mate = member + 1 - 2 * lax.rem(member, 2)
    own = summed(member, 0)
    line_ref[0:1] = own
    line_ref[1:2] = summed(member, 1)
    both = jnp.concatenate([own, summed(mate, 0)], axis=1)
    own_ref[...] = both
    spread_ref[...] = jnp.broadcast_to(both.reshape(1, 1, 2 * SLICE), spread_ref.shape)
    for order, by in enumerate((members - 2, 2, 0, 4)):
        value = own if by == 0 else summed(lax.rem(member + by, members), 0)
        row_ref[:, order * SLICE : order * SLICE + SLICE] = value


def denominators(member, everything, groups):
    return pl.pallas_call(
        denominator_kernel,
        in_specs=[SMEM, pl.BlockSpec()],
        out_shape=(
            jax.ShapeDtypeStruct((1, 4 * SLICE), jnp.float32),
            jax.ShapeDtypeStruct((1, 2 * SLICE), jnp.float32),
            jax.ShapeDtypeStruct((2, SLICE), jnp.float32),
            jax.ShapeDtypeStruct((groups, 1, 2 * SLICE), jnp.float32),
        ),
        compiler_params=params(),
        name="denominators",
    )(member, everything)


def backward_kernel(
    bands, first, partner_ref, row_ref, own_ref, everyone_ref, pos_ref, e0_in, e1_in, *refs
):
    if first:
        c0_in, c1_in, c_ref, refs = refs[0], refs[1], refs[2], refs[3:]
    else:
        c_ref, refs = refs[0], refs[1:]
    out_refs, (run_ref, e_buf, e_sem, c_sem) = refs[:-4], refs[-4:]
    own_pieces = e0_in.shape[0]
    copies = []
    for step, (start, many) in enumerate(STEPS):
        group = []
        for k, (source, low, high) in enumerate(
            ((0, 0, own_pieces), (1, own_pieces, own_pieces + e1_in.shape[0]))
        ):
            begin, end = max(start, low), min(start + many, high)
            if begin >= end:
                continue
            here, there = pl.ds(begin, end - begin), pl.ds(begin - low, end - begin)
            at = 0
            for which, (order, row, size) in enumerate(bands):
                group.append(
                    pltpu.make_async_copy(
                        (e0_in, e1_in)[source].at[there, order, pl.ds(row, size)],
                        e_buf.at[here, pl.ds(at, size)],
                        e_sem.at[step, k, which],
                    )
                )
                at += size
            if first:
                src = (c0_in, c1_in)[source].at[there]
                group.append(pltpu.make_async_copy(src, c_ref.at[here], c_sem.at[step, k]))
        copies.append(group)
        for copy in group:
            copy.start()

    columns, places = [], []
    for order, row, size in bands:
        column = as_column(row_ref[:, order * SLICE : order * SLICE + SLICE])
        columns.append(column[row : row + size])
        places.append(lax.broadcasted_iota(jnp.int32, (size, 128), 0) + (order * SLICE + row))
    row_inv = 1.0 / jnp.concatenate(columns, axis=0)
    row_ids = jnp.concatenate(places, axis=0)
    wide = 2 * SLICE
    col_inv = [1.0 / own_ref[...]] + [1.0 / everyone_ref[partner_ref[k]] for k in range(2)]
    for step, (start, many) in enumerate(STEPS):
        for copy in copies[step]:
            copy.wait()
        his, los = [], []
        for at in range(start * PIECE, (start + many) * PIECE, 128):
            inv = col_inv[at // wide][:, at % wide : at % wide + 128]
            weight = e_buf[at // PIECE, :, at % PIECE : at % PIECE + 128] * (row_inv + inv)
            if at < wide:
                weight = weight - jnp.where(row_ids == pos_ref[:, at : at + 128], 2.0, 0.0)
            hi, lo = split(weight)
            his.append(hi)
            los.append(lo)
        cols = c_ref[start : start + many].reshape(many * PIECE, 2 * WIDTH)
        c_hi, c_lo = cols[:, :WIDTH], cols[:, WIDTH:]
        part = jnp.dot(
            jnp.concatenate(his + his + los, axis=1),
            jnp.concatenate([c_hi, c_lo, c_hi], axis=0),
            preferred_element_type=jnp.float32,
        )
        if step == 0:
            run_ref[...] = part
        elif step + 1 < len(STEPS):
            run_ref[...] += part
        else:
            part = run_ref[...] + part
            size = part.shape[0] // len(out_refs)
            for which, ref in enumerate(out_refs):
                ref[...] = part[which * size : which * size + size]


def backward(bands, pieces, partners, row_den, own_den, everyone, pos, e0, e1, *cols):
    first = len(cols) == 2
    count = 9 * PIECE
    col_shape = [jax.ShapeDtypeStruct((9, PIECE, 2 * WIDTH), jnp.bfloat16)]
    return pl.pallas_call(
        functools.partial(backward_kernel, bands, first),
        in_specs=[SMEM] + [pl.BlockSpec()] * 4 + [HBM] * 2 + ([HBM] * 2 if first else [pl.BlockSpec()]),
        out_shape=col_shape * first + [jax.ShapeDtypeStruct((SLICE // pieces, WIDTH), jnp.float32)] * pieces,
        scratch_shapes=[
            pltpu.VMEM((SLICE, WIDTH), jnp.float32),
            pltpu.VMEM((9, SLICE, PIECE), jnp.float32),
            pltpu.SemaphoreType.DMA((len(STEPS), 2, len(bands))),
            pltpu.SemaphoreType.DMA((len(STEPS), 2)),
        ],
        cost_estimate=pl.CostEstimate(
            flops=6 * SLICE * count * WIDTH, bytes_accessed=4 * SLICE * count, transcendentals=0
        ),
        compiler_params=params(VMEM_BACKWARD),
        name="backward_%d_%d" % bands[0][:2],
    )(partners, row_den, own_den, everyone, pos, in_hbm(e0), in_hbm(e1), *(map(in_hbm, cols) if first else cols))


def add_kernel(a_ref, b_ref, c_ref, d_ref, ab_ref, cd_ref):
    ab_ref[...] = a_ref[...] + b_ref[...]
    cd_ref[...] = c_ref[...] + d_ref[...]


def add_pairs(a, b, c, d):
    out = jax.ShapeDtypeStruct(a.shape, jnp.float32)
    return pl.pallas_call(add_kernel, out_shape=(out, out), compiler_params=params(), name="add_pairs")(
        a, b, c, d
    )


def finish_kernel(emb_ref, run_ref, low0, low1, high0, high1, line_ref, loss_ref, grad_ref):
    values = emb_ref[...]
    radius = radius_of(values)
    unit = values / radius
    low, high = low0[...] + low1[...], high0[...] + high1[...]
    slope = (run_ref[...] + jnp.concatenate([low, high], axis=0)) / LOGIT_DIVISOR
    grad_ref[...] = (slope - unit * jnp.sum(unit * slope, axis=-1, keepdims=True)) / radius
    loss_ref[...] = (jnp.log(line_ref[0:1]) - line_ref[1:2]).reshape(loss_ref.shape)


def finish(embeddings, run, lows, highs, line):
    rows, width = embeddings.shape
    return pl.pallas_call(
        finish_kernel,
        out_shape=(
            jax.ShapeDtypeStruct((rows,), jnp.float32),
            jax.ShapeDtypeStruct((rows, width), jnp.float32),
        ),
        compiler_params=params(),
        name="finish",
    )(embeddings, run, *lows, *highs, line)


def local(embeddings, positive, pairing):
    rows, width = embeddings.shape
    members = lax.axis_size("mem")
    groups = lax.axis_size("grp")
    block = rows * members
    rounds = pairing.shape[0]
    group = lax.axis_index("grp")
    member = lax.axis_index("mem")
    half = rows // 2

    def shift(value, by):
        return lax.ppermute(value, "mem", [(m, (m + by) % members) for m in range(members)])

    def swap(value):
        return lax.ppermute(value, "mem", [(m, m ^ 1) for m in range(members)])

    left, right = shift(embeddings, 2), shift(embeddings, -2)
    far = (shift(left[:half], 2), shift(right[half:], -2))
    per = rows * width // (groups * 128)
    tiles = embeddings.reshape(rows // 8, 8, width // 128, 128).transpose(0, 2, 1, 3)
    pieces = lax.all_to_all(tiles.reshape(groups, per, 128), "grp", 0, 0, tiled=True)
    ready = prepare("prepare", left, right)
    picked, ready = lax.optimization_barrier((pick(pairing, pieces), ready))
    got = lax.all_to_all(picked, "grp", 0, 0, tiled=True)
    sib, pos_sib = swap(embeddings), swap(positive)

    both = jnp.concatenate([positive, pos_sib]) - group * block
    owner = both // rows
    turn = (owner // 2 - member // 2) % (members // 2)
    order = jnp.where(turn == 0, SELF, jnp.where(turn == 3, 0, jnp.where(turn == 1, 1, 3)))
    pos = jnp.where(owner % 2 == member % 2, order * rows + both % rows, -1).reshape(1, 2 * rows)

    ready_far = prepare("prepare_far", embeddings, *far)
    c_own, e_own, line = own_scores(ready, ready_far, embeddings, sib, pos)
    got, line, partners = lax.optimization_barrier((got, line, pairing[:, group]))
    e_part, c_part, line = forward(ready, ready_far, line, got, swap(got), members)

    everything = lax.all_to_all(line, "mem", 0, 0, tiled=True)
    row_den, own_den, line, spread = denominators(jnp.reshape(member, (1,)), everything, groups)
    everyone = lax.all_to_all(spread, "grp", 0, 0, tiled=True)

    shared = (partners, row_den, own_den, everyone, pos, e_own, e_part)
    cols, far_low, far_high = backward(((3, 0, rows),), 2, *shared, c_own, c_part)
    shared += (cols,)
    far_low, far_high = shift(far_low, 2), shift(far_high, -2)
    left_low, right_high = backward(((0, 0, half), (1, half, half)), 2, *shared)
    high0, low1 = shift(right_high, 2), shift(left_low, -2)
    left_high, right_low = backward(((0, half, half), (1, 0, half)), 2, *shared)
    right_low, left_high = add_pairs(right_low, far_low, left_high, far_high)
    low0, high1 = shift(right_low, 2), shift(left_high, -2)
    (run,) = backward(((SELF, 0, rows),), 1, *shared)
    return finish(embeddings, run, (low0, low1), (high0, high1), line)


def solution(mesh):
    placed = (P(("grp", "mem"), None), P(("grp", "mem")), P())
    return jax.shard_map(
        local,
        mesh=mesh,
        in_specs=placed,
        out_specs=(P(("grp", "mem")), P(("grp", "mem"), None)),
        check_vma=False,
    )
```

```python
import functools

import jax
import jax.numpy as jnp
from jax import lax
from jax.experimental import pallas as pl
from jax.experimental.pallas import tpu as pltpu
from jax.sharding import PartitionSpec as P

LOGIT_DIVISOR = 0.1
EPSILON = 1e-06
SLICE = 384
WIDTH = 256
SELF = 2
PIECE = 256
STEPS = ((0, 3), (3, 3), (6, 3))
VMEM = 16 * 1024 * 1024
VMEM_LARGE = 44 * 1024 * 1024
VMEM_BACKWARD = 28 * 1024 * 1024
HBM = pl.BlockSpec(memory_space=pltpu.HBM)
SMEM = pl.BlockSpec(memory_space=pltpu.SMEM)


def split(values):
    hi = values.astype(jnp.bfloat16)
    lo = (values - hi.astype(jnp.float32)).astype(jnp.bfloat16)
    return hi, lo


def rows_of(tiles):
    pairs = tiles.reshape(tiles.shape[0] // 2, 2, 8, 128)
    rows = tiles.shape[0] * 4
    return jnp.concatenate([pairs[:, 0].reshape(rows, 128), pairs[:, 1].reshape(rows, 128)], axis=1)


def radius_of(values):
    return jnp.sqrt(jnp.sum(values * values, axis=-1, keepdims=True) + EPSILON)


def as_column(line):
    return jnp.broadcast_to(line, (128, line.shape[1])).T


def in_hbm(value):
    return pltpu.with_memory_space_constraint(value, pltpu.HBM)


def params(limit=VMEM):
    return pltpu.CompilerParams(vmem_limit_bytes=limit)


def pick_kernel(pairing_ref, pieces_ref, out_ref):
    size = pieces_ref.shape[1]
    for which in range(out_ref.shape[1] // size):
        for group in range(out_ref.shape[0]):
            out_ref[group, which * size : which * size + size] = pieces_ref[pairing_ref[which, group]]


def pick(pairing, pieces):
    rounds, groups = pairing.shape
    return pl.pallas_call(
        pick_kernel,
        in_specs=[SMEM, pl.BlockSpec()],
        out_shape=jax.ShapeDtypeStruct((groups, rounds * pieces.shape[1], 128), jnp.float32),
        compiler_params=params(),
        name="pick",
    )(pairing, pieces)


def scaled_rows(refs, out_ref, at=0):
    for ref in refs:
        values = ref[...]
        hi, lo = split(values * (1.0 / (radius_of(values) * LOGIT_DIVISOR)))
        out_ref[at : at + hi.shape[0]] = jnp.concatenate([hi, lo, hi], axis=1)
        at += hi.shape[0]


def unit_parts(values):
    hi, lo = split(values * (1.0 / radius_of(values)))
    return jnp.concatenate([hi, lo], axis=1)


def product(left, cols):
    hi, lo = cols[:, :WIDTH], cols[:, WIDTH:]
    return lax.dot_general(
        left,
        jnp.concatenate([hi, hi, lo], axis=1),
        (((1,), (1,)), ((), ())),
        preferred_element_type=jnp.float32,
    )


def exponentials(scores, first_row, pos_ref, store):
    height = scores.shape[0]
    total = jnp.zeros((height, 128), jnp.float32)
    match = jnp.zeros((height, 128), jnp.float32)
    if first_row is not None:
        row_ids = lax.broadcasted_iota(jnp.int32, (height, 128), 0) + first_row
        lane_ids = lax.broadcasted_iota(jnp.int32, (height, 128), 1)
    for k in range(0, scores.shape[1], 128):
        score = scores[:, k : k + 128]
        e = jnp.exp(score)
        if first_row is not None:
            match = match + jnp.where(row_ids == pos_ref[:, k : k + 128], score, 0.0)
            if first_row <= SELF * SLICE < first_row + height and k < SLICE:
                e = jnp.where(row_ids - SELF * SLICE == lane_ids + k, 0.0, e)
        total = total + e
        store(k, e)
    return total, match


def as_line(total):
    return jnp.sum(total.T, axis=0, keepdims=True)


def put_columns(c_buf, at, parts):
    done = 0
    while done < parts.shape[0]:
        inside = (at + done) % PIECE
        size = min(PIECE - inside, parts.shape[0] - done)
        c_buf[(at + done) // PIECE, inside : inside + size] = parts[done : done + size]
        done += size


def own_kernel(
    ready, ready_far, mine, sib, pos_ref, c_out, e_out, line_ref, left_ref, c_buf, e_buf, in_sem, c_sem, e_sem
):
    at = ready.shape[0]
    ready_copies = [
        pltpu.make_async_copy(ready, left_ref.at[pl.ds(0, at)], in_sem.at[0]),
        pltpu.make_async_copy(ready_far, left_ref.at[pl.ds(at, ready_far.shape[0])], in_sem.at[1]),
    ]
    for copy in ready_copies:
        copy.start()
    for which, ref in enumerate((mine, sib)):
        put_columns(c_buf, which * SLICE, unit_parts(ref[...]))
    cols = c_buf[...].reshape(2 * SLICE, 2 * WIDTH)
    copies = [pltpu.make_async_copy(c_buf, c_out, c_sem)]
    copies[0].start()
    for copy in ready_copies:
        copy.wait()

    totals, matches = [], []
    for band in range(2):
        scores = product(left_ref[band * 2 * SLICE : (band + 1) * 2 * SLICE], cols)

        def store(k, e):
            e_buf[k // PIECE, 2 * band : 2 * band + 2, :, k % PIECE : k % PIECE + 128] = e.reshape(2, SLICE, 128)

        total, match = exponentials(scores, band * 2 * SLICE, pos_ref, store)
        totals.append(as_line(total))
        matches.append(as_line(match))
        view = (slice(None), pl.ds(2 * band, 2))
        copies.append(pltpu.make_async_copy(e_buf.at[view], e_out.at[view], e_sem.at[band]))
        copies[-1].start()
    line_ref[0:1] = jnp.concatenate(totals, axis=1)
    line_ref[1:2] = jnp.concatenate(matches, axis=1)
    for copy in copies:
        copy.wait()


def own_scores(ready, ready_far, mine, sib, pos):
    rows, wide = 4 * SLICE, 2 * SLICE
    shapes = [((3, PIECE, 2 * WIDTH), jnp.bfloat16), ((3, 4, SLICE, PIECE), jnp.float32)]
    return pl.pallas_call(
        own_kernel,
        in_specs=[HBM] * 2 + [pl.BlockSpec()] * 3,
        out_specs=[HBM] * 2 + [pl.BlockSpec()],
        out_shape=[pltpu.HBM(*shape) for shape in shapes] + [jax.ShapeDtypeStruct((2, rows), jnp.float32)],
        scratch_shapes=[
            pltpu.VMEM((rows, 3 * WIDTH), jnp.bfloat16),
            pltpu.VMEM(*shapes[0]),
            pltpu.VMEM(*shapes[1]),
            pltpu.SemaphoreType.DMA((2,)),
            pltpu.SemaphoreType.DMA,
            pltpu.SemaphoreType.DMA((2,)),
        ],
        cost_estimate=pl.CostEstimate(
            flops=6 * rows * wide * WIDTH, bytes_accessed=4 * rows * wide, transcendentals=rows * wide
        ),
        compiler_params=params(VMEM_LARGE),
        name="own_scores",
    )(in_hbm(ready), in_hbm(ready_far), mine, sib, pos)


def prepare_kernel(*refs):
    pieces, (out_ref, buf, sem) = refs[:-3], refs[-3:]
    scaled_rows(pieces, buf)
    copy = pltpu.make_async_copy(buf, out_ref, sem)
    copy.start()
    copy.wait()


def prepare(name, *pieces):
    rows = sum(piece.shape[0] for piece in pieces)
    shape = ((rows, 3 * WIDTH), jnp.bfloat16)
    return pl.pallas_call(
        prepare_kernel,
        out_specs=HBM,
        out_shape=pltpu.HBM(*shape),
        scratch_shapes=[pltpu.VMEM(*shape), pltpu.SemaphoreType.DMA],
        cost_estimate=pl.CostEstimate(flops=20 * 10**9, bytes_accessed=8 * rows * WIDTH, transcendentals=0),
        compiler_params=params(),
        name=name,
    )(*pieces)


def forward_kernel(
    ready, ready_far, line_in, got, got_sib, e_out, c_out, line_ref,
    left_ref, c_buf, e_buf, tot_ref, in_sem, c_sem, e_sem,
):
    orders, wide = e_buf.shape[1], 2 * SLICE
    many = wide // PIECE
    chunks = e_buf.shape[0] // many
    at = ready.shape[0]
    ready_copies = [
        pltpu.make_async_copy(ready, left_ref.at[pl.ds(0, at)], in_sem.at[0]),
        pltpu.make_async_copy(ready_far, left_ref.at[pl.ds(at, ready_far.shape[0])], in_sem.at[1]),
    ]
    for copy in ready_copies:
        copy.start()
    half = got.shape[1] // 2
    tiles = got.shape[0] * half // 8
    copies = []

    def columns(chunk):
        for which, ref in enumerate((got, got_sib)):
            piece = rows_of(ref[:, chunk * half : chunk * half + half].reshape(tiles, 8, 128))
            put_columns(c_buf, chunk * wide + which * SLICE, unit_parts(piece))
        view = (pl.ds(chunk * many, many),)
        copies.append(pltpu.make_async_copy(c_buf.at[view], c_out.at[view], c_sem.at[chunk]))
        copies[-1].start()

    def scores_of(chunk, band):
        cols = c_buf[chunk * many : chunk * many + many].reshape(wide, 2 * WIDTH)
        return product(left_ref[band * wide : band * wide + wide], cols)

    columns(0)
    for copy in ready_copies:
        copy.wait()
    items = [(chunk, band) for chunk in range(chunks) for band in range(orders // 2)]
    for turn, (chunk, band) in enumerate(items):
        if turn > 0 and band == 0:
            columns(chunk)
        scores = scores_of(chunk, band)

        def store(k, e):
            lane = k % PIECE
            e = e.reshape(2, SLICE, 128)
            e_buf[chunk * many + k // PIECE, 2 * band : 2 * band + 2, :, lane : lane + 128] = e

        total, _ = exponentials(scores, None, None, store)
        if chunk == 0:
            tot_ref[band * wide : band * wide + wide] = total
        else:
            tot_ref[band * wide : band * wide + wide] += total
        view = (pl.ds(chunk * many, many), pl.ds(2 * band, 2))
        copies.append(pltpu.make_async_copy(e_buf.at[view], e_out.at[view], e_sem.at[turn]))
        copies[-1].start()

    total = as_line(tot_ref[...]) + line_in[0:1]
    for member in range(line_ref.shape[0]):
        line_ref[member, 0:1] = total
        line_ref[member, 1:2] = line_in[1:2]
    for copy in copies:
        copy.wait()


def forward(ready, ready_far, line, got, got_sib, members):
    rows, wide = 4 * SLICE, 2 * SLICE
    e_shape, c_shape = ((6, 4, SLICE, PIECE), jnp.float32), ((6, PIECE, 2 * WIDTH), jnp.bfloat16)
    return pl.pallas_call(
        forward_kernel,
        in_specs=[HBM] * 2 + [pl.BlockSpec()] * 3,
        out_specs=[HBM] * 2 + [pl.BlockSpec()],
        out_shape=(
            pltpu.HBM(*e_shape),
            pltpu.HBM(*c_shape),
            jax.ShapeDtypeStruct((members, 2, rows), jnp.float32),
        ),
        scratch_shapes=[
            pltpu.VMEM((rows, 3 * WIDTH), jnp.bfloat16),
            pltpu.VMEM(*c_shape),
            pltpu.VMEM(*e_shape),
            pltpu.VMEM((rows, 128), jnp.float32),
            pltpu.SemaphoreType.DMA((2,)),
            pltpu.SemaphoreType.DMA((2,)),
            pltpu.SemaphoreType.DMA((4,)),
        ],
        cost_estimate=pl.CostEstimate(
            flops=12 * rows * wide * WIDTH, bytes_accessed=8 * rows * wide, transcendentals=2 * rows * wide
        ),
        compiler_params=params(VMEM_LARGE),
        name="forward",
    )(in_hbm(ready), in_hbm(ready_far), line, got, got_sib)


def denominator_kernel(member_ref, all_ref, row_ref, own_ref, line_ref, spread_ref):
    member = member_ref[0]
    members = all_ref.shape[0]

    def summed(owner, kind):
        value = 0.0
        for by, order in ((0, SELF), (2, 0), (members - 2, 1), (4, 3)):
            held = all_ref[lax.rem(owner + by, members)]
            value = value + held[kind : kind + 1, order * SLICE : order * SLICE + SLICE]
        return value

    mate = member + 1 - 2 * lax.rem(member, 2)
    own = summed(member, 0)
    line_ref[0:1] = own
    line_ref[1:2] = summed(member, 1)
    both = jnp.concatenate([own, summed(mate, 0)], axis=1)
    own_ref[...] = both
    spread_ref[...] = jnp.broadcast_to(both.reshape(1, 1, 2 * SLICE), spread_ref.shape)
    for order, by in enumerate((members - 2, 2, 0, 4)):
        value = own if by == 0 else summed(lax.rem(member + by, members), 0)
        row_ref[:, order * SLICE : order * SLICE + SLICE] = value


def denominators(member, everything, groups):
    return pl.pallas_call(
        denominator_kernel,
        in_specs=[SMEM, pl.BlockSpec()],
        out_shape=(
            jax.ShapeDtypeStruct((1, 4 * SLICE), jnp.float32),
            jax.ShapeDtypeStruct((1, 2 * SLICE), jnp.float32),
            jax.ShapeDtypeStruct((2, SLICE), jnp.float32),
            jax.ShapeDtypeStruct((groups, 1, 2 * SLICE), jnp.float32),
        ),
        compiler_params=params(),
        name="denominators",
    )(member, everything)


def backward_kernel(
    bands, first, partner_ref, row_ref, own_ref, everyone_ref, pos_ref, e0_in, e1_in, *refs
):
    if first:
        c0_in, c1_in, c_ref, refs = refs[0], refs[1], refs[2], refs[3:]
    else:
        c_ref, refs = refs[0], refs[1:]
    out_refs, (run_ref, e_buf, e_sem, c_sem) = refs[:-4], refs[-4:]
    own_pieces = e0_in.shape[0]
    copies = []
    for step, (start, many) in enumerate(STEPS):
        group = []
        for k, (source, low, high) in enumerate(
            ((0, 0, own_pieces), (1, own_pieces, own_pieces + e1_in.shape[0]))
        ):
            begin, end = max(start, low), min(start + many, high)
            if begin >= end:
                continue
            here, there = pl.ds(begin, end - begin), pl.ds(begin - low, end - begin)
            at = 0
            for which, (order, row, size) in enumerate(bands):
                group.append(
                    pltpu.make_async_copy(
                        (e0_in, e1_in)[source].at[there, order, pl.ds(row, size)],
                        e_buf.at[here, pl.ds(at, size)],
                        e_sem.at[step, k, which],
                    )
                )
                at += size
            if first:
                src = (c0_in, c1_in)[source].at[there]
                group.append(pltpu.make_async_copy(src, c_ref.at[here], c_sem.at[step, k]))
        copies.append(group)
        for copy in group:
            copy.start()

    columns, places = [], []
    for order, row, size in bands:
        column = as_column(row_ref[:, order * SLICE : order * SLICE + SLICE])
        columns.append(column[row : row + size])
        places.append(lax.broadcasted_iota(jnp.int32, (size, 128), 0) + (order * SLICE + row))
    row_inv = 1.0 / jnp.concatenate(columns, axis=0)
    row_ids = jnp.concatenate(places, axis=0)
    wide = 2 * SLICE
    col_inv = [1.0 / own_ref[...]] + [1.0 / everyone_ref[partner_ref[k]] for k in range(2)]
    for step, (start, many) in enumerate(STEPS):
        for copy in copies[step]:
            copy.wait()
        his, los = [], []
        for at in range(start * PIECE, (start + many) * PIECE, 128):
            inv = col_inv[at // wide][:, at % wide : at % wide + 128]
            weight = e_buf[at // PIECE, :, at % PIECE : at % PIECE + 128] * (row_inv + inv)
            if at < wide:
                weight = weight - jnp.where(row_ids == pos_ref[:, at : at + 128], 2.0, 0.0)
            hi, lo = split(weight)
            his.append(hi)
            los.append(lo)
        cols = c_ref[start : start + many].reshape(many * PIECE, 2 * WIDTH)
        c_hi, c_lo = cols[:, :WIDTH], cols[:, WIDTH:]
        part = jnp.dot(
            jnp.concatenate(his + his + los, axis=1),
            jnp.concatenate([c_hi, c_lo, c_hi], axis=0),
            preferred_element_type=jnp.float32,
        )
        if step == 0:
            run_ref[...] = part
        elif step + 1 < len(STEPS):
            run_ref[...] += part
        else:
            part = run_ref[...] + part
            size = part.shape[0] // len(out_refs)
            for which, ref in enumerate(out_refs):
                ref[...] = part[which * size : which * size + size]


def backward(bands, pieces, partners, row_den, own_den, everyone, pos, e0, e1, *cols):
    first = len(cols) == 2
    count = 9 * PIECE
    col_shape = [jax.ShapeDtypeStruct((9, PIECE, 2 * WIDTH), jnp.bfloat16)]
    return pl.pallas_call(
        functools.partial(backward_kernel, bands, first),
        in_specs=[SMEM] + [pl.BlockSpec()] * 4 + [HBM] * 2 + ([HBM] * 2 if first else [pl.BlockSpec()]),
        out_shape=col_shape * first + [jax.ShapeDtypeStruct((SLICE // pieces, WIDTH), jnp.float32)] * pieces,
        scratch_shapes=[
            pltpu.VMEM((SLICE, WIDTH), jnp.float32),
            pltpu.VMEM((9, SLICE, PIECE), jnp.float32),
            pltpu.SemaphoreType.DMA((len(STEPS), 2, len(bands))),
            pltpu.SemaphoreType.DMA((len(STEPS), 2)),
        ],
        cost_estimate=pl.CostEstimate(
            flops=6 * SLICE * count * WIDTH, bytes_accessed=4 * SLICE * count, transcendentals=0
        ),
        compiler_params=params(VMEM_BACKWARD),
        name="backward_%d_%d" % bands[0][:2],
    )(partners, row_den, own_den, everyone, pos, in_hbm(e0), in_hbm(e1), *(map(in_hbm, cols) if first else cols))


def add_kernel(a_ref, b_ref, c_ref, d_ref, ab_ref, cd_ref):
    ab_ref[...] = a_ref[...] + b_ref[...]
    cd_ref[...] = c_ref[...] + d_ref[...]


def add_pairs(a, b, c, d):
    out = jax.ShapeDtypeStruct(a.shape, jnp.float32)
    return pl.pallas_call(add_kernel, out_shape=(out, out), compiler_params=params(), name="add_pairs")(
        a, b, c, d
    )


def finish_kernel(emb_ref, run_ref, low0, low1, high0, high1, line_ref, loss_ref, grad_ref):
    values = emb_ref[...]
    radius = radius_of(values)
    unit = values / radius
    low, high = low0[...] + low1[...], high0[...] + high1[...]
    slope = (run_ref[...] + jnp.concatenate([low, high], axis=0)) / LOGIT_DIVISOR
    grad_ref[...] = (slope - unit * jnp.sum(unit * slope, axis=-1, keepdims=True)) / radius
    loss_ref[...] = (jnp.log(line_ref[0:1]) - line_ref[1:2]).reshape(loss_ref.shape)


def finish(embeddings, run, lows, highs, line):
    rows, width = embeddings.shape
    return pl.pallas_call(
        finish_kernel,
        out_shape=(
            jax.ShapeDtypeStruct((rows,), jnp.float32),
            jax.ShapeDtypeStruct((rows, width), jnp.float32),
        ),
        compiler_params=params(),
        name="finish",
    )(embeddings, run, *lows, *highs, line)


def local(embeddings, positive, pairing):
    rows, width = embeddings.shape
    members = lax.axis_size("mem")
    groups = lax.axis_size("grp")
    block = rows * members
    rounds = pairing.shape[0]
    group = lax.axis_index("grp")
    member = lax.axis_index("mem")
    half = rows // 2

    def shift(value, by):
        return lax.ppermute(value, "mem", [(m, (m + by) % members) for m in range(members)])

    def swap(value):
        return lax.ppermute(value, "mem", [(m, m ^ 1) for m in range(members)])

    left, right = shift(embeddings, 2), shift(embeddings, -2)
    far = (shift(left[:half], 2), shift(right[half:], -2))
    per = rows * width // (groups * 128)
    tiles = embeddings.reshape(rows // 8, 8, width // 128, 128).transpose(0, 2, 1, 3)
    pieces = lax.all_to_all(tiles.reshape(groups, per, 128), "grp", 0, 0, tiled=True)
    ready = prepare("prepare", left, right)
    picked, ready = lax.optimization_barrier((pick(pairing, pieces), ready))
    got = lax.all_to_all(picked, "grp", 0, 0, tiled=True)
    sib, pos_sib = swap(embeddings), swap(positive)

    both = jnp.concatenate([positive, pos_sib]) - group * block
    owner = both // rows
    turn = (owner // 2 - member // 2) % (members // 2)
    order = jnp.where(turn == 0, SELF, jnp.where(turn == 3, 0, jnp.where(turn == 1, 1, 3)))
    pos = jnp.where(owner % 2 == member % 2, order * rows + both % rows, -1).reshape(1, 2 * rows)

    ready_far = prepare("prepare_far", embeddings, *far)
    c_own, e_own, line = own_scores(ready, ready_far, embeddings, sib, pos)
    got, line, partners = lax.optimization_barrier((got, line, pairing[:, group]))
    e_part, c_part, line = forward(ready, ready_far, line, got, swap(got), members)

    everything = lax.all_to_all(line, "mem", 0, 0, tiled=True)
    row_den, own_den, line, spread = denominators(jnp.reshape(member, (1,)), everything, groups)
    everyone = lax.all_to_all(spread, "grp", 0, 0, tiled=True)

    shared = (partners, row_den, own_den, everyone, pos, e_own, e_part)
    cols, far_low, far_high = backward(((3, 0, rows),), 2, *shared, c_own, c_part)
    shared += (cols,)
    far_low, far_high = shift(far_low, 2), shift(far_high, -2)
    left_low, right_high = backward(((0, 0, half), (1, half, half)), 2, *shared)
    high0, low1 = shift(right_high, 2), shift(left_low, -2)
    left_high, right_low = backward(((0, half, half), (1, 0, half)), 2, *shared)
    right_low, left_high = add_pairs(right_low, far_low, left_high, far_high)
    low0, high1 = shift(right_low, 2), shift(left_high, -2)
    (run,) = backward(((SELF, 0, rows),), 1, *shared)
    return finish(embeddings, run, (low0, low1), (high0, high1), line)


def solution(mesh):
    placed = (P(("grp", "mem"), None), P(("grp", "mem")), P())
    return jax.shard_map(
        local,
        mesh=mesh,
        in_specs=placed,
        out_specs=(P(("grp", "mem")), P(("grp", "mem"), None)),
        check_vma=False,
    )
```

```python
import functools

import jax
import jax.numpy as jnp
from jax import lax
from jax.experimental import pallas as pl
from jax.experimental.pallas import tpu as pltpu
from jax.sharding import PartitionSpec as P

LOGIT_DIVISOR = 0.1
EPSILON = 1e-06
SLICE = 384
WIDTH = 256
SELF = 2
PIECE = 256
STEPS = ((0, 3), (3, 3), (6, 3))
VMEM = 16 * 1024 * 1024
VMEM_LARGE = 44 * 1024 * 1024
VMEM_BACKWARD = 28 * 1024 * 1024
HBM = pl.BlockSpec(memory_space=pltpu.HBM)
SMEM = pl.BlockSpec(memory_space=pltpu.SMEM)


def split(values):
    hi = values.astype(jnp.bfloat16)
    lo = (values - hi.astype(jnp.float32)).astype(jnp.bfloat16)
    return hi, lo


def rows_of(tiles):
    pairs = tiles.reshape(tiles.shape[0] // 2, 2, 8, 128)
    rows = tiles.shape[0] * 4
    return jnp.concatenate([pairs[:, 0].reshape(rows, 128), pairs[:, 1].reshape(rows, 128)], axis=1)


def radius_of(values):
    return jnp.sqrt(jnp.sum(values * values, axis=-1, keepdims=True) + EPSILON)


def as_column(line):
    return jnp.broadcast_to(line, (128, line.shape[1])).T


def in_hbm(value):
    return pltpu.with_memory_space_constraint(value, pltpu.HBM)


def params(limit=VMEM):
    return pltpu.CompilerParams(vmem_limit_bytes=limit)


def pick_kernel(pairing_ref, pieces_ref, out_ref, buf, sems):
    size = pieces_ref.shape[1]
    part = buf.shape[0] // sems.shape[0]
    copies = []
    for begin in range(0, buf.shape[0], part):
        for group in range(begin, begin + part):
            for which in range(buf.shape[1] // size):
                buf[group, which * size : which * size + size] = pieces_ref[pairing_ref[which, group]]
        view = (pl.ds(begin, part),)
        copies.append(pltpu.make_async_copy(buf.at[view], out_ref.at[view], sems.at[begin // part]))
        copies[-1].start()
    for copy in copies:
        copy.wait()


def pick(pairing, pieces):
    rounds, groups = pairing.shape
    shape = ((groups, rounds * pieces.shape[1], 128), jnp.float32)
    return pl.pallas_call(
        pick_kernel,
        in_specs=[SMEM, pl.BlockSpec()],
        out_specs=HBM,
        out_shape=pltpu.HBM(*shape),
        scratch_shapes=[pltpu.VMEM(*shape), pltpu.SemaphoreType.DMA((4,))],
        compiler_params=params(),
        name="pick",
    )(pairing, pieces)


def scaled_rows(refs, out_ref, at=0):
    for ref in refs:
        values = ref[...]
        hi, lo = split(values * (1.0 / (radius_of(values) * LOGIT_DIVISOR)))
        out_ref[at : at + hi.shape[0]] = jnp.concatenate([hi, lo, hi], axis=1)
        at += hi.shape[0]


def unit_parts(values):
    hi, lo = split(values * (1.0 / radius_of(values)))
    return jnp.concatenate([hi, lo], axis=1)


def product(left, cols):
    hi, lo = cols[:, :WIDTH], cols[:, WIDTH:]
    return lax.dot_general(
        left,
        jnp.concatenate([hi, hi, lo], axis=1),
        (((1,), (1,)), ((), ())),
        preferred_element_type=jnp.float32,
    )


def exponentials(scores, first_row, pos_ref, store):
    height = scores.shape[0]
    total = jnp.zeros((height, 128), jnp.float32)
    match = jnp.zeros((height, 128), jnp.float32)
    if first_row is not None:
        row_ids = lax.broadcasted_iota(jnp.int32, (height, 128), 0) + first_row
        lane_ids = lax.broadcasted_iota(jnp.int32, (height, 128), 1)
    for k in range(0, scores.shape[1], 128):
        score = scores[:, k : k + 128]
        e = jnp.exp(score)
        if first_row is not None:
            match = match + jnp.where(row_ids == pos_ref[:, k : k + 128], score, 0.0)
            if first_row <= SELF * SLICE < first_row + height and k < SLICE:
                e = jnp.where(row_ids - SELF * SLICE == lane_ids + k, 0.0, e)
        total = total + e
        store(k, e)
    return total, match


def as_line(total):
    return jnp.sum(total.T, axis=0, keepdims=True)


def put_columns(c_buf, at, parts):
    done = 0
    while done < parts.shape[0]:
        inside = (at + done) % PIECE
        size = min(PIECE - inside, parts.shape[0] - done)
        c_buf[(at + done) // PIECE, inside : inside + size] = parts[done : done + size]
        done += size


def own_kernel(
    ready, ready_far, mine, sib, pos_ref, c_out, e_out, line_ref, left_ref, c_buf, e_buf, in_sem, c_sem, e_sem
):
    at = ready.shape[0]
    ready_copies = [
        pltpu.make_async_copy(ready, left_ref.at[pl.ds(0, at)], in_sem.at[0]),
        pltpu.make_async_copy(ready_far, left_ref.at[pl.ds(at, ready_far.shape[0])], in_sem.at[1]),
    ]
    for copy in ready_copies:
        copy.start()
    for which, ref in enumerate((mine, sib)):
        put_columns(c_buf, which * SLICE, unit_parts(ref[...]))
    cols = c_buf[...].reshape(2 * SLICE, 2 * WIDTH)
    copies = [pltpu.make_async_copy(c_buf, c_out, c_sem)]
    copies[0].start()
    for copy in ready_copies:
        copy.wait()

    totals, matches = [], []
    for band in range(2):
        scores = product(left_ref[band * 2 * SLICE : (band + 1) * 2 * SLICE], cols)

        def store(k, e):
            e_buf[k // PIECE, 2 * band : 2 * band + 2, :, k % PIECE : k % PIECE + 128] = e.reshape(2, SLICE, 128)

        total, match = exponentials(scores, band * 2 * SLICE, pos_ref, store)
        totals.append(as_line(total))
        matches.append(as_line(match))
        view = (slice(None), pl.ds(2 * band, 2))
        copies.append(pltpu.make_async_copy(e_buf.at[view], e_out.at[view], e_sem.at[band]))
        copies[-1].start()
    line_ref[0:1] = jnp.concatenate(totals, axis=1)
    line_ref[1:2] = jnp.concatenate(matches, axis=1)
    for copy in copies:
        copy.wait()


def own_scores(ready, ready_far, mine, sib, pos):
    rows, wide = 4 * SLICE, 2 * SLICE
    shapes = [((3, PIECE, 2 * WIDTH), jnp.bfloat16), ((3, 4, SLICE, PIECE), jnp.float32)]
    return pl.pallas_call(
        own_kernel,
        in_specs=[HBM] * 2 + [pl.BlockSpec()] * 3,
        out_specs=[HBM] * 2 + [pl.BlockSpec()],
        out_shape=[pltpu.HBM(*shape) for shape in shapes] + [jax.ShapeDtypeStruct((2, rows), jnp.float32)],
        scratch_shapes=[
            pltpu.VMEM((rows, 3 * WIDTH), jnp.bfloat16),
            pltpu.VMEM(*shapes[0]),
            pltpu.VMEM(*shapes[1]),
            pltpu.SemaphoreType.DMA((2,)),
            pltpu.SemaphoreType.DMA,
            pltpu.SemaphoreType.DMA((2,)),
        ],
        cost_estimate=pl.CostEstimate(
            flops=6 * rows * wide * WIDTH, bytes_accessed=4 * rows * wide, transcendentals=rows * wide
        ),
        compiler_params=params(VMEM_LARGE),
        name="own_scores",
    )(in_hbm(ready), in_hbm(ready_far), mine, sib, pos)


def prepare_kernel(*refs):
    pieces, (out_ref, buf, sem) = refs[:-3], refs[-3:]
    scaled_rows(pieces, buf)
    copy = pltpu.make_async_copy(buf, out_ref, sem)
    copy.start()
    copy.wait()


def prepare(name, *pieces):
    rows = sum(piece.shape[0] for piece in pieces)
    shape = ((rows, 3 * WIDTH), jnp.bfloat16)
    return pl.pallas_call(
        prepare_kernel,
        out_specs=HBM,
        out_shape=pltpu.HBM(*shape),
        scratch_shapes=[pltpu.VMEM(*shape), pltpu.SemaphoreType.DMA],
        cost_estimate=pl.CostEstimate(flops=20 * 10**9, bytes_accessed=8 * rows * WIDTH, transcendentals=0),
        compiler_params=params(),
        name=name,
    )(*pieces)


def forward_kernel(
    ready, ready_far, line_in, got, got_sib, e_out, c_out, line_ref,
    left_ref, c_buf, e_buf, tot_ref, in_sem, c_sem, e_sem,
):
    orders, wide = e_buf.shape[1], 2 * SLICE
    many = wide // PIECE
    chunks = e_buf.shape[0] // many
    at = ready.shape[0]
    ready_copies = [
        pltpu.make_async_copy(ready, left_ref.at[pl.ds(0, at)], in_sem.at[0]),
        pltpu.make_async_copy(ready_far, left_ref.at[pl.ds(at, ready_far.shape[0])], in_sem.at[1]),
    ]
    for copy in ready_copies:
        copy.start()
    half = got.shape[1] // 2
    tiles = got.shape[0] * half // 8
    copies = []

    def columns(chunk):
        for which, ref in enumerate((got, got_sib)):
            piece = rows_of(ref[:, chunk * half : chunk * half + half].reshape(tiles, 8, 128))
            put_columns(c_buf, chunk * wide + which * SLICE, unit_parts(piece))
        view = (pl.ds(chunk * many, many),)
        copies.append(pltpu.make_async_copy(c_buf.at[view], c_out.at[view], c_sem.at[chunk]))
        copies[-1].start()

    def scores_of(chunk, band):
        cols = c_buf[chunk * many : chunk * many + many].reshape(wide, 2 * WIDTH)
        return product(left_ref[band * wide : band * wide + wide], cols)

    columns(0)
    for copy in ready_copies:
        copy.wait()
    items = [(chunk, band) for chunk in range(chunks) for band in range(orders // 2)]
    for turn, (chunk, band) in enumerate(items):
        if turn > 0 and band == 0:
            columns(chunk)
        scores = scores_of(chunk, band)

        def store(k, e):
            lane = k % PIECE
            e = e.reshape(2, SLICE, 128)
            e_buf[chunk * many + k // PIECE, 2 * band : 2 * band + 2, :, lane : lane + 128] = e

        total, _ = exponentials(scores, None, None, store)
        if chunk == 0:
            tot_ref[band * wide : band * wide + wide] = total
        else:
            tot_ref[band * wide : band * wide + wide] += total
        for k in range(many):
            view = (chunk * many + k, pl.ds(2 * band, 2))
            copies.append(pltpu.make_async_copy(e_buf.at[view], e_out.at[view], e_sem.at[turn, k]))
            copies[-1].start()

    total = as_line(tot_ref[...]) + line_in[0:1]
    for member in range(line_ref.shape[0]):
        line_ref[member, 0:1] = total
        line_ref[member, 1:2] = line_in[1:2]
    for copy in copies:
        copy.wait()


def forward(ready, ready_far, line, got, got_sib, members):
    rows, wide = 4 * SLICE, 2 * SLICE
    e_shape, c_shape = ((6, 4, SLICE, PIECE), jnp.float32), ((6, PIECE, 2 * WIDTH), jnp.bfloat16)
    return pl.pallas_call(
        forward_kernel,
        in_specs=[HBM] * 2 + [pl.BlockSpec()] * 3,
        out_specs=[HBM] * 2 + [pl.BlockSpec()],
        out_shape=(
            pltpu.HBM(*e_shape),
            pltpu.HBM(*c_shape),
            jax.ShapeDtypeStruct((members, 2, rows), jnp.float32),
        ),
        scratch_shapes=[
            pltpu.VMEM((rows, 3 * WIDTH), jnp.bfloat16),
            pltpu.VMEM(*c_shape),
            pltpu.VMEM(*e_shape),
            pltpu.VMEM((rows, 128), jnp.float32),
            pltpu.SemaphoreType.DMA((2,)),
            pltpu.SemaphoreType.DMA((2,)),
            pltpu.SemaphoreType.DMA((4, 3)),
        ],
        cost_estimate=pl.CostEstimate(
            flops=12 * rows * wide * WIDTH, bytes_accessed=8 * rows * wide, transcendentals=2 * rows * wide
        ),
        compiler_params=params(VMEM_LARGE),
        name="forward",
    )(in_hbm(ready), in_hbm(ready_far), line, got, got_sib)


def denominator_kernel(member_ref, all_ref, row_ref, own_ref, line_ref, spread_ref):
    member = member_ref[0]
    members = all_ref.shape[0]

    def summed(owner, kind):
        value = 0.0
        for by, order in ((0, SELF), (2, 0), (members - 2, 1), (4, 3)):
            held = all_ref[lax.rem(owner + by, members)]
            value = value + held[kind : kind + 1, order * SLICE : order * SLICE + SLICE]
        return value

    mate = member + 1 - 2 * lax.rem(member, 2)
    own = summed(member, 0)
    line_ref[0:1] = own
    line_ref[1:2] = summed(member, 1)
    both = jnp.concatenate([own, summed(mate, 0)], axis=1)
    own_ref[...] = both
    spread_ref[...] = jnp.broadcast_to(both.reshape(1, 1, 2 * SLICE), spread_ref.shape)
    for order, by in enumerate((members - 2, 2, 0, 4)):
        value = own if by == 0 else summed(lax.rem(member + by, members), 0)
        row_ref[:, order * SLICE : order * SLICE + SLICE] = value


def denominators(member, everything, groups):
    return pl.pallas_call(
        denominator_kernel,
        in_specs=[SMEM, pl.BlockSpec()],
        out_shape=(
            jax.ShapeDtypeStruct((1, 4 * SLICE), jnp.float32),
            jax.ShapeDtypeStruct((1, 2 * SLICE), jnp.float32),
            jax.ShapeDtypeStruct((2, SLICE), jnp.float32),
            jax.ShapeDtypeStruct((groups, 1, 2 * SLICE), jnp.float32),
        ),
        compiler_params=params(),
        name="denominators",
    )(member, everything)


def backward_kernel(
    bands, first, partner_ref, row_ref, own_ref, everyone_ref, pos_ref, e0_in, e1_in, *refs
):
    if first:
        c0_in, c1_in, c_ref, refs = refs[0], refs[1], refs[2], refs[3:]
    else:
        c_ref, refs = refs[0], refs[1:]
    out_refs, (run_ref, e_buf, e_sem, c_sem) = refs[:-4], refs[-4:]
    own_pieces = e0_in.shape[0]
    copies = []
    for step, (start, many) in enumerate(STEPS):
        group = []
        for k in range(many):
            piece = start + k
            if piece < own_pieces:
                e_src, place = e0_in, piece
            else:
                e_src, place = e1_in, piece - own_pieces
            at = 0
            for which, (order, row, size) in enumerate(bands):
                group.append(
                    pltpu.make_async_copy(
                        e_src.at[place, order, pl.ds(row, size)],
                        e_buf.at[piece, pl.ds(at, size)],
                        e_sem.at[step, k, which],
                    )
                )
                at += size
            if first:
                c_src = c0_in if piece < own_pieces else c1_in
                group.append(pltpu.make_async_copy(c_src.at[place], c_ref.at[piece], c_sem.at[step, k]))
        copies.append(group)
        for copy in group:
            copy.start()

    columns, places = [], []
    for order, row, size in bands:
        column = as_column(row_ref[:, order * SLICE : order * SLICE + SLICE])
        columns.append(column[row : row + size])
        places.append(lax.broadcasted_iota(jnp.int32, (size, 128), 0) + (order * SLICE + row))
    row_inv = 1.0 / jnp.concatenate(columns, axis=0)
    row_ids = jnp.concatenate(places, axis=0)
    wide = 2 * SLICE
    col_inv = [1.0 / own_ref[...]] + [1.0 / everyone_ref[partner_ref[k]] for k in range(2)]
    for step, (start, many) in enumerate(STEPS):
        for copy in copies[step]:
            copy.wait()
        his, los = [], []
        for at in range(start * PIECE, (start + many) * PIECE, 128):
            inv = col_inv[at // wide][:, at % wide : at % wide + 128]
            weight = e_buf[at // PIECE, :, at % PIECE : at % PIECE + 128] * (row_inv + inv)
            if at < wide:
                weight = weight - jnp.where(row_ids == pos_ref[:, at : at + 128], 2.0, 0.0)
            hi, lo = split(weight)
            his.append(hi)
            los.append(lo)
        cols = c_ref[start : start + many].reshape(many * PIECE, 2 * WIDTH)
        c_hi, c_lo = cols[:, :WIDTH], cols[:, WIDTH:]
        part = jnp.dot(
            jnp.concatenate(his + his + los, axis=1),
            jnp.concatenate([c_hi, c_lo, c_hi], axis=0),
            preferred_element_type=jnp.float32,
        )
        if step == 0:
            run_ref[...] = part
        elif step + 1 < len(STEPS):
            run_ref[...] += part
        else:
            part = run_ref[...] + part
            size = part.shape[0] // len(out_refs)
            for which, ref in enumerate(out_refs):
                ref[...] = part[which * size : which * size + size]


def backward(bands, pieces, partners, row_den, own_den, everyone, pos, e0, e1, *cols):
    first = len(cols) == 2
    count = 9 * PIECE
    col_shape = [jax.ShapeDtypeStruct((9, PIECE, 2 * WIDTH), jnp.bfloat16)]
    return pl.pallas_call(
        functools.partial(backward_kernel, bands, first),
        in_specs=[SMEM] + [pl.BlockSpec()] * 4 + [HBM] * 2 + ([HBM] * 2 if first else [pl.BlockSpec()]),
        out_shape=col_shape * first + [jax.ShapeDtypeStruct((SLICE // pieces, WIDTH), jnp.float32)] * pieces,
        scratch_shapes=[
            pltpu.VMEM((SLICE, WIDTH), jnp.float32),
            pltpu.VMEM((9, SLICE, PIECE), jnp.float32),
            pltpu.SemaphoreType.DMA((len(STEPS), 3, len(bands))),
            pltpu.SemaphoreType.DMA((len(STEPS), 3)),
        ],
        cost_estimate=pl.CostEstimate(
            flops=6 * SLICE * count * WIDTH, bytes_accessed=4 * SLICE * count, transcendentals=0
        ),
        compiler_params=params(VMEM_BACKWARD),
        name="backward_%d_%d" % bands[0][:2],
    )(partners, row_den, own_den, everyone, pos, in_hbm(e0), in_hbm(e1), *(map(in_hbm, cols) if first else cols))


def add_kernel(a_ref, b_ref, c_ref, d_ref, ab_ref, cd_ref):
    ab_ref[...] = a_ref[...] + b_ref[...]
    cd_ref[...] = c_ref[...] + d_ref[...]


def add_pairs(a, b, c, d):
    out = jax.ShapeDtypeStruct(a.shape, jnp.float32)
    return pl.pallas_call(add_kernel, out_shape=(out, out), compiler_params=params(), name="add_pairs")(
        a, b, c, d
    )


def finish_kernel(emb_ref, run_ref, low0, low1, high0, high1, line_ref, loss_ref, grad_ref):
    values = emb_ref[...]
    radius = radius_of(values)
    unit = values / radius
    low, high = low0[...] + low1[...], high0[...] + high1[...]
    slope = (run_ref[...] + jnp.concatenate([low, high], axis=0)) / LOGIT_DIVISOR
    grad_ref[...] = (slope - unit * jnp.sum(unit * slope, axis=-1, keepdims=True)) / radius
    loss_ref[...] = (jnp.log(line_ref[0:1]) - line_ref[1:2]).reshape(loss_ref.shape)


def finish(embeddings, run, lows, highs, line):
    rows, width = embeddings.shape
    return pl.pallas_call(
        finish_kernel,
        out_shape=(
            jax.ShapeDtypeStruct((rows,), jnp.float32),
            jax.ShapeDtypeStruct((rows, width), jnp.float32),
        ),
        compiler_params=params(),
        name="finish",
    )(embeddings, run, *lows, *highs, line)


def local(embeddings, positive, pairing):
    rows, width = embeddings.shape
    members = lax.axis_size("mem")
    groups = lax.axis_size("grp")
    block = rows * members
    rounds = pairing.shape[0]
    group = lax.axis_index("grp")
    member = lax.axis_index("mem")
    half = rows // 2

    def shift(value, by):
        return lax.ppermute(value, "mem", [(m, (m + by) % members) for m in range(members)])

    def swap(value):
        return lax.ppermute(value, "mem", [(m, m ^ 1) for m in range(members)])

    left, right = shift(embeddings, 2), shift(embeddings, -2)
    far = (shift(left[:half], 2), shift(right[half:], -2))
    per = rows * width // (groups * 128)
    tiles = embeddings.reshape(rows // 8, 8, width // 128, 128).transpose(0, 2, 1, 3)
    pieces = lax.all_to_all(tiles.reshape(groups, per, 128), "grp", 0, 0, tiled=True)
    ready = prepare("prepare", left, right)
    picked, ready = lax.optimization_barrier((pick(pairing, pieces), ready))
    got = lax.all_to_all(picked, "grp", 0, 0, tiled=True)
    sib, pos_sib = swap(embeddings), swap(positive)

    both = jnp.concatenate([positive, pos_sib]) - group * block
    owner = both // rows
    turn = (owner // 2 - member // 2) % (members // 2)
    order = jnp.where(turn == 0, SELF, jnp.where(turn == 3, 0, jnp.where(turn == 1, 1, 3)))
    pos = jnp.where(owner % 2 == member % 2, order * rows + both % rows, -1).reshape(1, 2 * rows)

    ready_far = prepare("prepare_far", embeddings, *far)
    c_own, e_own, line = own_scores(ready, ready_far, embeddings, sib, pos)
    got, line, partners = lax.optimization_barrier((got, line, pairing[:, group]))
    e_part, c_part, line = forward(ready, ready_far, line, got, swap(got), members)

    everything = lax.all_to_all(line, "mem", 0, 0, tiled=True)
    row_den, own_den, line, spread = denominators(jnp.reshape(member, (1,)), everything, groups)
    everyone = lax.all_to_all(spread, "grp", 0, 0, tiled=True)

    shared = (partners, row_den, own_den, everyone, pos, e_own, e_part)
    cols, far_low, far_high = backward(((3, 0, rows),), 2, *shared, c_own, c_part)
    shared += (cols,)
    far_low, far_high = shift(far_low, 2), shift(far_high, -2)
    left_low, right_high = backward(((0, 0, half), (1, half, half)), 2, *shared)
    high0, low1 = shift(right_high, 2), shift(left_low, -2)
    left_high, right_low = backward(((0, half, half), (1, 0, half)), 2, *shared)
    right_low, left_high = add_pairs(right_low, far_low, left_high, far_high)
    low0, high1 = shift(right_low, 2), shift(left_high, -2)
    (run,) = backward(((SELF, 0, rows),), 1, *shared)
    return finish(embeddings, run, (low0, low1), (high0, high1), line)


def solution(mesh):
    placed = (P(("grp", "mem"), None), P(("grp", "mem")), P())
    return jax.shard_map(
        local,
        mesh=mesh,
        in_specs=placed,
        out_specs=(P(("grp", "mem")), P(("grp", "mem"), None)),
        check_vma=False,
    )
```

```python
import functools

import jax
import jax.numpy as jnp
from jax import lax
from jax.experimental import pallas as pl
from jax.experimental.pallas import tpu as pltpu
from jax.sharding import PartitionSpec as P

LOGIT_DIVISOR = 0.1
EPSILON = 1e-06
SLICE = 384
WIDTH = 256
SELF = 2
PIECE = 256
STEPS = ((0, 4), (4, 5))
VMEM = 16 * 1024 * 1024
VMEM_LARGE = 44 * 1024 * 1024
VMEM_BACKWARD = 28 * 1024 * 1024
HBM = pl.BlockSpec(memory_space=pltpu.HBM)
SMEM = pl.BlockSpec(memory_space=pltpu.SMEM)


def split(values):
    hi = values.astype(jnp.bfloat16)
    lo = (values - hi.astype(jnp.float32)).astype(jnp.bfloat16)
    return hi, lo


def rows_of(tiles):
    pairs = tiles.reshape(tiles.shape[0] // 2, 2, 8, 128)
    rows = tiles.shape[0] * 4
    return jnp.concatenate([pairs[:, 0].reshape(rows, 128), pairs[:, 1].reshape(rows, 128)], axis=1)


def radius_of(values):
    return jnp.sqrt(jnp.sum(values * values, axis=-1, keepdims=True) + EPSILON)


def as_column(line):
    return jnp.broadcast_to(line, (128, line.shape[1])).T


def in_hbm(value):
    return pltpu.with_memory_space_constraint(value, pltpu.HBM)


def params(limit=VMEM):
    return pltpu.CompilerParams(vmem_limit_bytes=limit)


def pick_kernel(pairing_ref, pieces_ref, out_ref):
    size = pieces_ref.shape[1]
    for which in range(out_ref.shape[1] // size):
        for group in range(out_ref.shape[0]):
            out_ref[group, which * size : which * size + size] = pieces_ref[pairing_ref[which, group]]


def pick(pairing, pieces):
    rounds, groups = pairing.shape
    return pl.pallas_call(
        pick_kernel,
        in_specs=[SMEM, pl.BlockSpec()],
        out_shape=jax.ShapeDtypeStruct((groups, rounds * pieces.shape[1], 128), jnp.float32),
        compiler_params=params(),
        name="pick",
    )(pairing, pieces)


def scaled_rows(refs, out_ref, at=0):
    for ref in refs:
        values = ref[...]
        hi, lo = split(values * (1.0 / (radius_of(values) * LOGIT_DIVISOR)))
        out_ref[at : at + hi.shape[0]] = jnp.concatenate([hi, lo, hi], axis=1)
        at += hi.shape[0]


def unit_parts(values):
    hi, lo = split(values * (1.0 / radius_of(values)))
    return jnp.concatenate([hi, lo], axis=1)


def product(left, cols):
    hi, lo = cols[:, :WIDTH], cols[:, WIDTH:]
    return lax.dot_general(
        left,
        jnp.concatenate([hi, hi, lo], axis=1),
        (((1,), (1,)), ((), ())),
        preferred_element_type=jnp.float32,
    )


def exponentials(scores, first_row, pos_ref, store):
    height = scores.shape[0]
    total = jnp.zeros((height, 128), jnp.float32)
    match = jnp.zeros((height, 128), jnp.float32)
    if first_row is not None:
        row_ids = lax.broadcasted_iota(jnp.int32, (height, 128), 0) + first_row
        lane_ids = lax.broadcasted_iota(jnp.int32, (height, 128), 1)
    for k in range(0, scores.shape[1], 128):
        score = scores[:, k : k + 128]
        e = jnp.exp(score)
        if first_row is not None:
            match = match + jnp.where(row_ids == pos_ref[:, k : k + 128], score, 0.0)
            if first_row <= SELF * SLICE < first_row + height and k < SLICE:
                e = jnp.where(row_ids - SELF * SLICE == lane_ids + k, 0.0, e)
        total = total + e
        store(k, e)
    return total, match


def as_line(total):
    return jnp.sum(total.T, axis=0, keepdims=True)


def put_columns(c_buf, at, parts):
    done = 0
    while done < parts.shape[0]:
        inside = (at + done) % PIECE
        size = min(PIECE - inside, parts.shape[0] - done)
        c_buf[(at + done) // PIECE, inside : inside + size] = parts[done : done + size]
        done += size


def own_kernel(
    ready, ready_far, mine, sib, pos_ref, c_out, e_out, line_ref, left_ref, c_buf, e_buf, in_sem, c_sem, e_sem
):
    at = ready.shape[0]
    ready_copies = [
        pltpu.make_async_copy(ready, left_ref.at[pl.ds(0, at)], in_sem.at[0]),
        pltpu.make_async_copy(ready_far, left_ref.at[pl.ds(at, ready_far.shape[0])], in_sem.at[1]),
    ]
    for copy in ready_copies:
        copy.start()
    for which, ref in enumerate((mine, sib)):
        put_columns(c_buf, which * SLICE, unit_parts(ref[...]))
    cols = c_buf[...].reshape(2 * SLICE, 2 * WIDTH)
    copies = [pltpu.make_async_copy(c_buf, c_out, c_sem)]
    copies[0].start()
    for copy in ready_copies:
        copy.wait()

    totals, matches = [], []
    for band in range(2):
        scores = product(left_ref[band * 2 * SLICE : (band + 1) * 2 * SLICE], cols)

        def store(k, e):
            e_buf[k // PIECE, 2 * band : 2 * band + 2, :, k % PIECE : k % PIECE + 128] = e.reshape(2, SLICE, 128)

        total, match = exponentials(scores, band * 2 * SLICE, pos_ref, store)
        totals.append(as_line(total))
        matches.append(as_line(match))
        view = (slice(None), pl.ds(2 * band, 2))
        copies.append(pltpu.make_async_copy(e_buf.at[view], e_out.at[view], e_sem.at[band]))
        copies[-1].start()
    line_ref[0:1] = jnp.concatenate(totals, axis=1)
    line_ref[1:2] = jnp.concatenate(matches, axis=1)
    for copy in copies:
        copy.wait()


def own_scores(ready, ready_far, mine, sib, pos):
    rows, wide = 4 * SLICE, 2 * SLICE
    shapes = [((3, PIECE, 2 * WIDTH), jnp.bfloat16), ((3, 4, SLICE, PIECE), jnp.float32)]
    return pl.pallas_call(
        own_kernel,
        in_specs=[HBM] * 2 + [pl.BlockSpec()] * 3,
        out_specs=[HBM] * 2 + [pl.BlockSpec()],
        out_shape=[pltpu.HBM(*shape) for shape in shapes] + [jax.ShapeDtypeStruct((2, rows), jnp.float32)],
        scratch_shapes=[
            pltpu.VMEM((rows, 3 * WIDTH), jnp.bfloat16),
            pltpu.VMEM(*shapes[0]),
            pltpu.VMEM(*shapes[1]),
            pltpu.SemaphoreType.DMA((2,)),
            pltpu.SemaphoreType.DMA,
            pltpu.SemaphoreType.DMA((2,)),
        ],
        cost_estimate=pl.CostEstimate(
            flops=6 * rows * wide * WIDTH, bytes_accessed=4 * rows * wide, transcendentals=rows * wide
        ),
        compiler_params=params(VMEM_LARGE),
        name="own_scores",
    )(in_hbm(ready), in_hbm(ready_far), mine, sib, pos)


def prepare_kernel(*refs):
    pieces, (out_ref, buf, sem) = refs[:-3], refs[-3:]
    scaled_rows(pieces, buf)
    copy = pltpu.make_async_copy(buf, out_ref, sem)
    copy.start()
    copy.wait()


def prepare(name, *pieces):
    rows = sum(piece.shape[0] for piece in pieces)
    shape = ((rows, 3 * WIDTH), jnp.bfloat16)
    return pl.pallas_call(
        prepare_kernel,
        out_specs=HBM,
        out_shape=pltpu.HBM(*shape),
        scratch_shapes=[pltpu.VMEM(*shape), pltpu.SemaphoreType.DMA],
        cost_estimate=pl.CostEstimate(flops=20 * 10**9, bytes_accessed=8 * rows * WIDTH, transcendentals=0),
        compiler_params=params(),
        name=name,
    )(*pieces)


def forward_kernel(
    ready, ready_far, line_in, got, got_sib, e_out, c_out, line_ref,
    left_ref, c_buf, e_buf, tot_ref, in_sem, c_sem, e_sem,
):
    orders, wide = e_buf.shape[1], 2 * SLICE
    many = wide // PIECE
    chunks = e_buf.shape[0] // many
    at = ready.shape[0]
    ready_copies = [
        pltpu.make_async_copy(ready, left_ref.at[pl.ds(0, at)], in_sem.at[0]),
        pltpu.make_async_copy(ready_far, left_ref.at[pl.ds(at, ready_far.shape[0])], in_sem.at[1]),
    ]
    for copy in ready_copies:
        copy.start()
    half = got.shape[1] // 2
    tiles = got.shape[0] * half // 8
    copies = []

    def columns(chunk):
        for which, ref in enumerate((got, got_sib)):
            piece = rows_of(ref[:, chunk * half : chunk * half + half].reshape(tiles, 8, 128))
            put_columns(c_buf, chunk * wide + which * SLICE, unit_parts(piece))
        view = (pl.ds(chunk * many, many),)
        copies.append(pltpu.make_async_copy(c_buf.at[view], c_out.at[view], c_sem.at[chunk]))
        copies[-1].start()

    def scores_of(chunk, band):
        cols = c_buf[chunk * many : chunk * many + many].reshape(wide, 2 * WIDTH)
        return product(left_ref[band * wide : band * wide + wide], cols)

    columns(0)
    for copy in ready_copies:
        copy.wait()
    items = [(chunk, band) for chunk in range(chunks) for band in range(orders // 2)]
    for turn, (chunk, band) in enumerate(items):
        if turn > 0 and band == 0:
            columns(chunk)
        scores = scores_of(chunk, band)

        def store(k, e):
            lane = k % PIECE
            e = e.reshape(2, SLICE, 128)
            e_buf[chunk * many + k // PIECE, 2 * band : 2 * band + 2, :, lane : lane + 128] = e

        total, _ = exponentials(scores, None, None, store)
        if chunk == 0:
            tot_ref[band * wide : band * wide + wide] = total
        else:
            tot_ref[band * wide : band * wide + wide] += total
        view = (pl.ds(chunk * many, many), pl.ds(2 * band, 2))
        copies.append(pltpu.make_async_copy(e_buf.at[view], e_out.at[view], e_sem.at[turn]))
        copies[-1].start()

    total = as_line(tot_ref[...]) + line_in[0:1]
    for member in range(line_ref.shape[0]):
        line_ref[member, 0:1] = total
        line_ref[member, 1:2] = line_in[1:2]
    for copy in copies:
        copy.wait()


def forward(ready, ready_far, line, got, got_sib, members):
    rows, wide = 4 * SLICE, 2 * SLICE
    e_shape, c_shape = ((6, 4, SLICE, PIECE), jnp.float32), ((6, PIECE, 2 * WIDTH), jnp.bfloat16)
    return pl.pallas_call(
        forward_kernel,
        in_specs=[HBM] * 2 + [pl.BlockSpec()] * 3,
        out_specs=[HBM] * 2 + [pl.BlockSpec()],
        out_shape=(
            pltpu.HBM(*e_shape),
            pltpu.HBM(*c_shape),
            jax.ShapeDtypeStruct((members, 2, rows), jnp.float32),
        ),
        scratch_shapes=[
            pltpu.VMEM((rows, 3 * WIDTH), jnp.bfloat16),
            pltpu.VMEM(*c_shape),
            pltpu.VMEM(*e_shape),
            pltpu.VMEM((rows, 128), jnp.float32),
            pltpu.SemaphoreType.DMA((2,)),
            pltpu.SemaphoreType.DMA((2,)),
            pltpu.SemaphoreType.DMA((4,)),
        ],
        cost_estimate=pl.CostEstimate(
            flops=12 * rows * wide * WIDTH, bytes_accessed=8 * rows * wide, transcendentals=2 * rows * wide
        ),
        compiler_params=params(VMEM_LARGE),
        name="forward",
    )(in_hbm(ready), in_hbm(ready_far), line, got, got_sib)


def denominator_kernel(member_ref, all_ref, row_ref, own_ref, line_ref, spread_ref):
    member = member_ref[0]
    members = all_ref.shape[0]

    def summed(owner, kind):
        value = 0.0
        for by, order in ((0, SELF), (2, 0), (members - 2, 1), (4, 3)):
            held = all_ref[lax.rem(owner + by, members)]
            value = value + held[kind : kind + 1, order * SLICE : order * SLICE + SLICE]
        return value

    mate = member + 1 - 2 * lax.rem(member, 2)
    own = summed(member, 0)
    line_ref[0:1] = own
    line_ref[1:2] = summed(member, 1)
    both = jnp.concatenate([own, summed(mate, 0)], axis=1)
    own_ref[...] = both
    spread_ref[...] = jnp.broadcast_to(both.reshape(1, 1, 2 * SLICE), spread_ref.shape)
    for order, by in enumerate((members - 2, 2, 0, 4)):
        value = own if by == 0 else summed(lax.rem(member + by, members), 0)
        row_ref[:, order * SLICE : order * SLICE + SLICE] = value


def denominators(member, everything, groups):
    return pl.pallas_call(
        denominator_kernel,
        in_specs=[SMEM, pl.BlockSpec()],
        out_shape=(
            jax.ShapeDtypeStruct((1, 4 * SLICE), jnp.float32),
            jax.ShapeDtypeStruct((1, 2 * SLICE), jnp.float32),
            jax.ShapeDtypeStruct((2, SLICE), jnp.float32),
            jax.ShapeDtypeStruct((groups, 1, 2 * SLICE), jnp.float32),
        ),
        compiler_params=params(),
        name="denominators",
    )(member, everything)


def backward_kernel(
    bands, first, partner_ref, row_ref, own_ref, everyone_ref, pos_ref, e0_in, e1_in, *refs
):
    if first:
        c0_in, c1_in, c_ref, refs = refs[0], refs[1], refs[2], refs[3:]
    else:
        c_ref, refs = refs[0], refs[1:]
    out_refs, (run_ref, e_buf, e_sem, c_sem) = refs[:-4], refs[-4:]
    own_pieces = e0_in.shape[0]
    copies = []
    for step, (start, many) in enumerate(STEPS):
        group = []
        for k, (source, low, high) in enumerate(
            ((0, 0, own_pieces), (1, own_pieces, own_pieces + e1_in.shape[0]))
        ):
            begin, end = max(start, low), min(start + many, high)
            if begin >= end:
                continue
            here, there = pl.ds(begin, end - begin), pl.ds(begin - low, end - begin)
            at = 0
            for which, (order, row, size) in enumerate(bands):
                group.append(
                    pltpu.make_async_copy(
                        (e0_in, e1_in)[source].at[there, order, pl.ds(row, size)],
                        e_buf.at[here, pl.ds(at, size)],
                        e_sem.at[step, k, which],
                    )
                )
                at += size
            if first:
                src = (c0_in, c1_in)[source].at[there]
                group.append(pltpu.make_async_copy(src, c_ref.at[here], c_sem.at[step, k]))
        copies.append(group)
        for copy in group:
            copy.start()

    columns, places = [], []
    for order, row, size in bands:
        column = as_column(row_ref[:, order * SLICE : order * SLICE + SLICE])
        columns.append(column[row : row + size])
        places.append(lax.broadcasted_iota(jnp.int32, (size, 128), 0) + (order * SLICE + row))
    row_inv = 1.0 / jnp.concatenate(columns, axis=0)
    row_ids = jnp.concatenate(places, axis=0)
    wide = 2 * SLICE
    col_inv = [1.0 / own_ref[...]] + [1.0 / everyone_ref[partner_ref[k]] for k in range(2)]
    for step, (start, many) in enumerate(STEPS):
        for copy in copies[step]:
            copy.wait()
        his, los = [], []
        for at in range(start * PIECE, (start + many) * PIECE, 128):
            inv = col_inv[at // wide][:, at % wide : at % wide + 128]
            weight = e_buf[at // PIECE, :, at % PIECE : at % PIECE + 128] * (row_inv + inv)
            if at < wide:
                weight = weight - jnp.where(row_ids == pos_ref[:, at : at + 128], 2.0, 0.0)
            hi, lo = split(weight)
            his.append(hi)
            los.append(lo)
        cols = c_ref[start : start + many].reshape(many * PIECE, 2 * WIDTH)
        c_hi, c_lo = cols[:, :WIDTH], cols[:, WIDTH:]
        part = jnp.dot(
            jnp.concatenate(his + his + los, axis=1),
            jnp.concatenate([c_hi, c_lo, c_hi], axis=0),
            preferred_element_type=jnp.float32,
        )
        if step == 0:
            run_ref[...] = part
        elif step + 1 < len(STEPS):
            run_ref[...] += part
        else:
            part = run_ref[...] + part
            size = part.shape[0] // len(out_refs)
            for which, ref in enumerate(out_refs):
                ref[...] = part[which * size : which * size + size]


def backward(bands, pieces, partners, row_den, own_den, everyone, pos, e0, e1, *cols):
    first = len(cols) == 2
    count = 9 * PIECE
    col_shape = [jax.ShapeDtypeStruct((9, PIECE, 2 * WIDTH), jnp.bfloat16)]
    return pl.pallas_call(
        functools.partial(backward_kernel, bands, first),
        in_specs=[SMEM] + [pl.BlockSpec()] * 4 + [HBM] * 2 + ([HBM] * 2 if first else [pl.BlockSpec()]),
        out_shape=col_shape * first + [jax.ShapeDtypeStruct((SLICE // pieces, WIDTH), jnp.float32)] * pieces,
        scratch_shapes=[
            pltpu.VMEM((SLICE, WIDTH), jnp.float32),
            pltpu.VMEM((9, SLICE, PIECE), jnp.float32),
            pltpu.SemaphoreType.DMA((len(STEPS), 2, len(bands))),
            pltpu.SemaphoreType.DMA((len(STEPS), 2)),
        ],
        cost_estimate=pl.CostEstimate(
            flops=6 * SLICE * count * WIDTH, bytes_accessed=4 * SLICE * count, transcendentals=0
        ),
        compiler_params=params(VMEM_BACKWARD),
        name="backward_%d_%d" % bands[0][:2],
    )(partners, row_den, own_den, everyone, pos, in_hbm(e0), in_hbm(e1), *(map(in_hbm, cols) if first else cols))


def add_kernel(a_ref, b_ref, c_ref, d_ref, ab_ref, cd_ref):
    ab_ref[...] = a_ref[...] + b_ref[...]
    cd_ref[...] = c_ref[...] + d_ref[...]


def add_pairs(a, b, c, d):
    out = jax.ShapeDtypeStruct(a.shape, jnp.float32)
    return pl.pallas_call(add_kernel, out_shape=(out, out), compiler_params=params(), name="add_pairs")(
        a, b, c, d
    )


def finish_kernel(emb_ref, run_ref, low0, low1, high0, high1, line_ref, loss_ref, grad_ref):
    values = emb_ref[...]
    radius = radius_of(values)
    unit = values / radius
    low, high = low0[...] + low1[...], high0[...] + high1[...]
    slope = (run_ref[...] + jnp.concatenate([low, high], axis=0)) / LOGIT_DIVISOR
    grad_ref[...] = (slope - unit * jnp.sum(unit * slope, axis=-1, keepdims=True)) / radius
    loss_ref[...] = (jnp.log(line_ref[0:1]) - line_ref[1:2]).reshape(loss_ref.shape)


def finish(embeddings, run, lows, highs, line):
    rows, width = embeddings.shape
    return pl.pallas_call(
        finish_kernel,
        out_shape=(
            jax.ShapeDtypeStruct((rows,), jnp.float32),
            jax.ShapeDtypeStruct((rows, width), jnp.float32),
        ),
        compiler_params=params(),
        name="finish",
    )(embeddings, run, *lows, *highs, line)


def local(embeddings, positive, pairing):
    rows, width = embeddings.shape
    members = lax.axis_size("mem")
    groups = lax.axis_size("grp")
    block = rows * members
    rounds = pairing.shape[0]
    group = lax.axis_index("grp")
    member = lax.axis_index("mem")
    half = rows // 2

    def shift(value, by):
        return lax.ppermute(value, "mem", [(m, (m + by) % members) for m in range(members)])

    def swap(value):
        return lax.ppermute(value, "mem", [(m, m ^ 1) for m in range(members)])

    left, right = shift(embeddings, 2), shift(embeddings, -2)
    far = (shift(left[:half], 2), shift(right[half:], -2))
    per = rows * width // (groups * 128)
    tiles = embeddings.reshape(rows // 8, 8, width // 128, 128).transpose(0, 2, 1, 3)
    pieces = lax.all_to_all(tiles.reshape(groups, per, 128), "grp", 0, 0, tiled=True)
    ready = prepare("prepare", left, right)
    picked, ready = lax.optimization_barrier((pick(pairing, pieces), ready))
    got = lax.all_to_all(picked, "grp", 0, 0, tiled=True)
    sib, pos_sib = swap(embeddings), swap(positive)

    both = jnp.concatenate([positive, pos_sib]) - group * block
    owner = both // rows
    turn = (owner // 2 - member // 2) % (members // 2)
    order = jnp.where(turn == 0, SELF, jnp.where(turn == 3, 0, jnp.where(turn == 1, 1, 3)))
    pos = jnp.where(owner % 2 == member % 2, order * rows + both % rows, -1).reshape(1, 2 * rows)

    ready_far = prepare("prepare_far", embeddings, *far)
    c_own, e_own, line = own_scores(ready, ready_far, embeddings, sib, pos)
    got, line, partners = lax.optimization_barrier((got, line, pairing[:, group]))
    e_part, c_part, line = forward(ready, ready_far, line, got, swap(got), members)

    everything = lax.all_to_all(line, "mem", 0, 0, tiled=True)
    row_den, own_den, line, spread = denominators(jnp.reshape(member, (1,)), everything, groups)
    everyone = lax.all_to_all(spread, "grp", 0, 0, tiled=True)

    shared = (partners, row_den, own_den, everyone, pos, e_own, e_part)
    cols, far_low, far_high = backward(((3, 0, rows),), 2, *shared, c_own, c_part)
    shared += (cols,)
    far_low, far_high = shift(far_low, 2), shift(far_high, -2)
    left_low, right_high = backward(((0, 0, half), (1, half, half)), 2, *shared)
    high0, low1 = shift(right_high, 2), shift(left_low, -2)
    left_high, right_low = backward(((0, half, half), (1, 0, half)), 2, *shared)
    right_low, left_high = add_pairs(right_low, far_low, left_high, far_high)
    low0, high1 = shift(right_low, 2), shift(left_high, -2)
    (run,) = backward(((SELF, 0, rows),), 1, *shared)
    return finish(embeddings, run, (low0, low1), (high0, high1), line)


def solution(mesh):
    placed = (P(("grp", "mem"), None), P(("grp", "mem")), P())
    return jax.shard_map(
        local,
        mesh=mesh,
        in_specs=placed,
        out_specs=(P(("grp", "mem")), P(("grp", "mem"), None)),
        check_vma=False,
    )
```

```python
import functools

import jax
import jax.numpy as jnp
from jax import lax
from jax.experimental import pallas as pl
from jax.experimental.pallas import tpu as pltpu
from jax.sharding import PartitionSpec as P

LOGIT_DIVISOR = 0.1
EPSILON = 1e-06
SLICE = 384
WIDTH = 256
SELF = 2
PIECE = 256
STEPS = ((0, 3), (3, 3), (6, 3))
VMEM = 16 * 1024 * 1024
VMEM_LARGE = 44 * 1024 * 1024
VMEM_BACKWARD = 28 * 1024 * 1024
HBM = pl.BlockSpec(memory_space=pltpu.HBM)
SMEM = pl.BlockSpec(memory_space=pltpu.SMEM)


def split(values):
    hi = values.astype(jnp.bfloat16)
    lo = (values - hi.astype(jnp.float32)).astype(jnp.bfloat16)
    return hi, lo


def rows_of(tiles):
    pairs = tiles.reshape(tiles.shape[0] // 2, 2, 8, 128)
    rows = tiles.shape[0] * 4
    return jnp.concatenate([pairs[:, 0].reshape(rows, 128), pairs[:, 1].reshape(rows, 128)], axis=1)


def radius_of(values):
    return jnp.sqrt(jnp.sum(values * values, axis=-1, keepdims=True) + EPSILON)


def as_column(line):
    return jnp.broadcast_to(line, (128, line.shape[1])).T


def in_hbm(value):
    return pltpu.with_memory_space_constraint(value, pltpu.HBM)


def params(limit=VMEM):
    return pltpu.CompilerParams(vmem_limit_bytes=limit)


def pick_kernel(pairing_ref, pieces_ref, out_ref):
    size = pieces_ref.shape[1]
    for which in range(out_ref.shape[1] // size):
        for group in range(out_ref.shape[0]):
            out_ref[group, which * size : which * size + size] = pieces_ref[pairing_ref[which, group]]


def pick(pairing, pieces):
    rounds, groups = pairing.shape
    return pl.pallas_call(
        pick_kernel,
        in_specs=[SMEM, pl.BlockSpec()],
        out_shape=jax.ShapeDtypeStruct((groups, rounds * pieces.shape[1], 128), jnp.float32),
        compiler_params=params(),
        name="pick",
    )(pairing, pieces)


def scaled_rows(refs, out_ref, at=0):
    for ref in refs:
        values = ref[...]
        hi, lo = split(values * (1.0 / (radius_of(values) * LOGIT_DIVISOR)))
        out_ref[at : at + hi.shape[0]] = jnp.concatenate([hi, lo, hi], axis=1)
        at += hi.shape[0]


def unit_parts(values):
    hi, lo = split(values * (1.0 / radius_of(values)))
    return jnp.concatenate([hi, lo], axis=1)


def product(left, cols):
    hi, lo = cols[:, :WIDTH], cols[:, WIDTH:]
    return lax.dot_general(
        left,
        jnp.concatenate([hi, hi, lo], axis=1),
        (((1,), (1,)), ((), ())),
        preferred_element_type=jnp.float32,
    )


def exponentials(scores, first_row, pos_ref, store):
    height = scores.shape[0]
    total = jnp.zeros((height, 128), jnp.float32)
    match = jnp.zeros((height, 128), jnp.float32)
    if first_row is not None:
        row_ids = lax.broadcasted_iota(jnp.int32, (height, 128), 0) + first_row
        lane_ids = lax.broadcasted_iota(jnp.int32, (height, 128), 1)
    for k in range(0, scores.shape[1], 128):
        score = scores[:, k : k + 128]
        e = jnp.exp(score)
        if first_row is not None:
            match = match + jnp.where(row_ids == pos_ref[:, k : k + 128], score, 0.0)
            if first_row <= SELF * SLICE < first_row + height and k < SLICE:
                e = jnp.where(row_ids - SELF * SLICE == lane_ids + k, 0.0, e)
        total = total + e
        store(k, e)
    return total, match


def as_line(total):
    return jnp.sum(total.T, axis=0, keepdims=True)


def put_columns(c_buf, at, parts):
    done = 0
    while done < parts.shape[0]:
        inside = (at + done) % PIECE
        size = min(PIECE - inside, parts.shape[0] - done)
        c_buf[(at + done) // PIECE, inside : inside + size] = parts[done : done + size]
        done += size


def own_kernel(
    ready, ready_far, mine, sib, pos_ref, c_out, e_out, line_ref, left_ref, c_buf, e_buf, in_sem, c_sem, e_sem
):
    at = ready.shape[0]
    ready_copies = [
        pltpu.make_async_copy(ready, left_ref.at[pl.ds(0, at)], in_sem.at[0]),
        pltpu.make_async_copy(ready_far, left_ref.at[pl.ds(at, ready_far.shape[0])], in_sem.at[1]),
    ]
    for copy in ready_copies:
        copy.start()
    for which, ref in enumerate((mine, sib)):
        put_columns(c_buf, which * SLICE, unit_parts(ref[...]))
    cols = c_buf[...].reshape(2 * SLICE, 2 * WIDTH)
    copies = [pltpu.make_async_copy(c_buf, c_out, c_sem)]
    copies[0].start()
    for copy in ready_copies:
        copy.wait()

    totals, matches = [], []
    for band in range(2):
        scores = product(left_ref[band * 2 * SLICE : (band + 1) * 2 * SLICE], cols)

        def store(k, e):
            e_buf[k // PIECE, 2 * band : 2 * band + 2, :, k % PIECE : k % PIECE + 128] = e.reshape(2, SLICE, 128)

        total, match = exponentials(scores, band * 2 * SLICE, pos_ref, store)
        totals.append(as_line(total))
        matches.append(as_line(match))
        view = (slice(None), pl.ds(2 * band, 2))
        copies.append(pltpu.make_async_copy(e_buf.at[view], e_out.at[view], e_sem.at[band]))
        copies[-1].start()
    line_ref[0:1] = jnp.concatenate(totals, axis=1)
    line_ref[1:2] = jnp.concatenate(matches, axis=1)
    for copy in copies:
        copy.wait()


def own_scores(ready, ready_far, mine, sib, pos):
    rows, wide = 4 * SLICE, 2 * SLICE
    shapes = [((3, PIECE, 2 * WIDTH), jnp.bfloat16), ((3, 4, SLICE, PIECE), jnp.float32)]
    return pl.pallas_call(
        own_kernel,
        in_specs=[HBM] * 2 + [pl.BlockSpec()] * 3,
        out_specs=[HBM] * 2 + [pl.BlockSpec()],
        out_shape=[pltpu.HBM(*shape) for shape in shapes] + [jax.ShapeDtypeStruct((2, rows), jnp.float32)],
        scratch_shapes=[
            pltpu.VMEM((rows, 3 * WIDTH), jnp.bfloat16),
            pltpu.VMEM(*shapes[0]),
            pltpu.VMEM(*shapes[1]),
            pltpu.SemaphoreType.DMA((2,)),
            pltpu.SemaphoreType.DMA,
            pltpu.SemaphoreType.DMA((2,)),
        ],
        cost_estimate=pl.CostEstimate(
            flops=6 * rows * wide * WIDTH, bytes_accessed=4 * rows * wide, transcendentals=rows * wide
        ),
        compiler_params=params(VMEM_LARGE),
        name="own_scores",
    )(in_hbm(ready), in_hbm(ready_far), mine, sib, pos)


def prepare_kernel(*refs):
    pieces, (out_ref, buf, sem) = refs[:-3], refs[-3:]
    scaled_rows(pieces, buf)
    copy = pltpu.make_async_copy(buf, out_ref, sem)
    copy.start()
    copy.wait()


def prepare(name, *pieces):
    rows = sum(piece.shape[0] for piece in pieces)
    shape = ((rows, 3 * WIDTH), jnp.bfloat16)
    return pl.pallas_call(
        prepare_kernel,
        out_specs=HBM,
        out_shape=pltpu.HBM(*shape),
        scratch_shapes=[pltpu.VMEM(*shape), pltpu.SemaphoreType.DMA],
        cost_estimate=pl.CostEstimate(flops=20 * 10**9, bytes_accessed=8 * rows * WIDTH, transcendentals=0),
        compiler_params=params(),
        name=name,
    )(*pieces)


def forward_kernel(
    ready, ready_far, line_in, got, got_sib, e_out, c_out, line_ref,
    left_ref, c_buf, e_buf, tot_ref, in_sem, c_sem, e_sem,
):
    orders, wide = e_buf.shape[1], 2 * SLICE
    many = wide // PIECE
    chunks = e_buf.shape[0] // many
    at = ready.shape[0]
    ready_copies = [
        pltpu.make_async_copy(ready, left_ref.at[pl.ds(0, at)], in_sem.at[0]),
        pltpu.make_async_copy(ready_far, left_ref.at[pl.ds(at, ready_far.shape[0])], in_sem.at[1]),
    ]
    for copy in ready_copies:
        copy.start()
    half = got.shape[1] // 2
    tiles = got.shape[0] * half // 8
    copies = []

    def columns(chunk):
        for which, ref in enumerate((got, got_sib)):
            piece = rows_of(ref[:, chunk * half : chunk * half + half].reshape(tiles, 8, 128))
            put_columns(c_buf, chunk * wide + which * SLICE, unit_parts(piece))
        view = (pl.ds(chunk * many, many),)
        copies.append(pltpu.make_async_copy(c_buf.at[view], c_out.at[view], c_sem.at[chunk]))
        copies[-1].start()

    def scores_of(chunk, band):
        cols = c_buf[chunk * many : chunk * many + many].reshape(wide, 2 * WIDTH)
        return product(left_ref[band * wide : band * wide + wide], cols)

    columns(0)
    for copy in ready_copies:
        copy.wait()
    items = [(chunk, band) for chunk in range(chunks) for band in range(orders // 2)]
    for turn, (chunk, band) in enumerate(items):
        if turn > 0 and band == 0:
            columns(chunk)
        scores = scores_of(chunk, band)

        def store(k, e):
            lane = k % PIECE
            e = e.reshape(2, SLICE, 128)
            e_buf[chunk * many + k // PIECE, 2 * band : 2 * band + 2, :, lane : lane + 128] = e

        total, _ = exponentials(scores, None, None, store)
        if chunk == 0:
            tot_ref[band * wide : band * wide + wide] = total
        else:
            tot_ref[band * wide : band * wide + wide] += total
        view = (pl.ds(chunk * many, many), pl.ds(2 * band, 2))
        copies.append(pltpu.make_async_copy(e_buf.at[view], e_out.at[view], e_sem.at[turn]))
        copies[-1].start()

    total = as_line(tot_ref[...]) + line_in[0:1]
    for member in range(line_ref.shape[0]):
        line_ref[member, 0:1] = total
        line_ref[member, 1:2] = line_in[1:2]
    for copy in copies:
        copy.wait()


def forward(ready, ready_far, line, got, got_sib, members):
    rows, wide = 4 * SLICE, 2 * SLICE
    e_shape, c_shape = ((6, 4, SLICE, PIECE), jnp.float32), ((6, PIECE, 2 * WIDTH), jnp.bfloat16)
    return pl.pallas_call(
        forward_kernel,
        in_specs=[HBM] * 2 + [pl.BlockSpec()] * 3,
        out_specs=[HBM] * 2 + [pl.BlockSpec()],
        out_shape=(
            pltpu.HBM(*e_shape),
            pltpu.HBM(*c_shape),
            jax.ShapeDtypeStruct((members, 2, rows), jnp.float32),
        ),
        scratch_shapes=[
            pltpu.VMEM((rows, 3 * WIDTH), jnp.bfloat16),
            pltpu.VMEM(*c_shape),
            pltpu.VMEM(*e_shape),
            pltpu.VMEM((rows, 128), jnp.float32),
            pltpu.SemaphoreType.DMA((2,)),
            pltpu.SemaphoreType.DMA((2,)),
            pltpu.SemaphoreType.DMA((4,)),
        ],
        cost_estimate=pl.CostEstimate(
            flops=12 * rows * wide * WIDTH, bytes_accessed=8 * rows * wide, transcendentals=2 * rows * wide
        ),
        compiler_params=params(VMEM_LARGE),
        name="forward",
    )(in_hbm(ready), in_hbm(ready_far), line, got, got_sib)


def denominator_kernel(member_ref, all_ref, row_ref, own_ref, line_ref, spread_ref):
    member = member_ref[0]
    members = all_ref.shape[0]

    def summed(owner, kind):
        value = 0.0
        for by, order in ((0, SELF), (2, 0), (members - 2, 1), (4, 3)):
            held = all_ref[lax.rem(owner + by, members)]
            value = value + held[kind : kind + 1, order * SLICE : order * SLICE + SLICE]
        return value

    mate = member + 1 - 2 * lax.rem(member, 2)
    own = summed(member, 0)
    line_ref[0:1] = own
    line_ref[1:2] = summed(member, 1)
    both = jnp.concatenate([own, summed(mate, 0)], axis=1)
    own_ref[...] = both
    spread_ref[...] = jnp.broadcast_to(both.reshape(1, 1, 2 * SLICE), spread_ref.shape)
    for order, by in enumerate((members - 2, 2, 0, 4)):
        value = own if by == 0 else summed(lax.rem(member + by, members), 0)
        row_ref[:, order * SLICE : order * SLICE + SLICE] = value


def denominators(member, everything, groups):
    return pl.pallas_call(
        denominator_kernel,
        in_specs=[SMEM, pl.BlockSpec()],
        out_shape=(
            jax.ShapeDtypeStruct((1, 4 * SLICE), jnp.float32),
            jax.ShapeDtypeStruct((1, 2 * SLICE), jnp.float32),
            jax.ShapeDtypeStruct((2, SLICE), jnp.float32),
            jax.ShapeDtypeStruct((groups, 1, 2 * SLICE), jnp.float32),
        ),
        compiler_params=params(),
        name="denominators",
    )(member, everything)


def backward_kernel(
    bands, first, partner_ref, row_ref, own_ref, everyone_ref, pos_ref, e0_in, e1_in, *refs
):
    if first:
        c0_in, c1_in, c_ref, refs = refs[0], refs[1], refs[2], refs[3:]
    else:
        c_ref, refs = refs[0], refs[1:]
    out_refs, (run_ref, e_buf, e_sem, c_sem) = refs[:-4], refs[-4:]
    own_pieces = e0_in.shape[0]
    copies = []
    for step, (start, many) in enumerate(STEPS):
        group = []
        for k, (source, low, high) in enumerate(
            ((0, 0, own_pieces), (1, own_pieces, own_pieces + e1_in.shape[0]))
        ):
            begin, end = max(start, low), min(start + many, high)
            if begin >= end:
                continue
            here, there = pl.ds(begin, end - begin), pl.ds(begin - low, end - begin)
            at = 0
            for which, (order, row, size) in enumerate(bands):
                group.append(
                    pltpu.make_async_copy(
                        (e0_in, e1_in)[source].at[there, order, pl.ds(row, size)],
                        e_buf.at[here, pl.ds(at, size)],
                        e_sem.at[step, k, which],
                    )
                )
                at += size
            if first:
                src = (c0_in, c1_in)[source].at[there]
                group.append(pltpu.make_async_copy(src, c_ref.at[here], c_sem.at[step, k]))
        copies.append(group)
        for copy in group:
            copy.start()

    columns, places = [], []
    for order, row, size in bands:
        column = as_column(row_ref[:, order * SLICE : order * SLICE + SLICE])
        columns.append(column[row : row + size])
        places.append(lax.broadcasted_iota(jnp.int32, (size, 128), 0) + (order * SLICE + row))
    row_inv = 1.0 / jnp.concatenate(columns, axis=0)
    row_ids = jnp.concatenate(places, axis=0)
    wide = 2 * SLICE
    col_inv = [1.0 / own_ref[...]] + [1.0 / everyone_ref[partner_ref[k]] for k in range(2)]
    for step, (start, many) in enumerate(STEPS):
        for copy in copies[step]:
            copy.wait()
        his, los = [], []
        for at in range(start * PIECE, (start + many) * PIECE, 128):
            inv = col_inv[at // wide][:, at % wide : at % wide + 128]
            weight = e_buf[at // PIECE, :, at % PIECE : at % PIECE + 128] * (row_inv + inv)
            if at < wide:
                weight = weight - jnp.where(row_ids == pos_ref[:, at : at + 128], 2.0, 0.0)
            hi, lo = split(weight)
            his.append(hi)
            los.append(lo)
        cols = c_ref[start : start + many].reshape(many * PIECE, 2 * WIDTH)
        c_hi, c_lo = cols[:, :WIDTH], cols[:, WIDTH:]
        part = jnp.dot(
            jnp.concatenate(his + his + los, axis=1),
            jnp.concatenate([c_hi, c_lo, c_hi], axis=0),
            preferred_element_type=jnp.float32,
        )
        if step == 0:
            run_ref[...] = part
        elif step + 1 < len(STEPS):
            run_ref[...] += part
        else:
            part = run_ref[...] + part
            size = part.shape[0] // len(out_refs)
            for which, ref in enumerate(out_refs):
                ref[...] = part[which * size : which * size + size]


def backward(bands, pieces, partners, row_den, own_den, everyone, pos, e0, e1, *cols):
    first = len(cols) == 2
    count = 9 * PIECE
    height = sum(size for _, _, size in bands)
    col_shape = [jax.ShapeDtypeStruct((9, PIECE, 2 * WIDTH), jnp.bfloat16)]
    return pl.pallas_call(
        functools.partial(backward_kernel, bands, first),
        in_specs=[SMEM] + [pl.BlockSpec()] * 4 + [HBM] * 2 + ([HBM] * 2 if first else [pl.BlockSpec()]),
        out_shape=col_shape * first + [jax.ShapeDtypeStruct((height // pieces, WIDTH), jnp.float32)] * pieces,
        scratch_shapes=[
            pltpu.VMEM((height, WIDTH), jnp.float32),
            pltpu.VMEM((9, height, PIECE), jnp.float32),
            pltpu.SemaphoreType.DMA((len(STEPS), 2, len(bands))),
            pltpu.SemaphoreType.DMA((len(STEPS), 2)),
        ],
        cost_estimate=pl.CostEstimate(
            flops=6 * height * count * WIDTH, bytes_accessed=4 * height * count, transcendentals=0
        ),
        compiler_params=params(VMEM_BACKWARD),
        name="backward_%d_%d" % bands[0][:2],
    )(partners, row_den, own_den, everyone, pos, in_hbm(e0), in_hbm(e1), *(map(in_hbm, cols) if first else cols))


def add_kernel(a_ref, b_ref, c_ref, d_ref, ab_ref, cd_ref):
    ab_ref[...] = a_ref[...] + b_ref[...]
    cd_ref[...] = c_ref[...] + d_ref[...]


def add_pairs(a, b, c, d):
    out = jax.ShapeDtypeStruct(a.shape, jnp.float32)
    return pl.pallas_call(add_kernel, out_shape=(out, out), compiler_params=params(), name="add_pairs")(
        a, b, c, d
    )


def finish_kernel(emb_ref, run_ref, low0, low1, high0, high1, line_ref, loss_ref, grad_ref):
    values = emb_ref[...]
    radius = radius_of(values)
    unit = values / radius
    low, high = low0[...] + low1[...], high0[...] + high1[...]
    slope = (run_ref[...] + jnp.concatenate([low, high], axis=0)) / LOGIT_DIVISOR
    grad_ref[...] = (slope - unit * jnp.sum(unit * slope, axis=-1, keepdims=True)) / radius
    loss_ref[...] = (jnp.log(line_ref[0:1]) - line_ref[1:2]).reshape(loss_ref.shape)


def finish(embeddings, run, lows, highs, line):
    rows, width = embeddings.shape
    return pl.pallas_call(
        finish_kernel,
        out_shape=(
            jax.ShapeDtypeStruct((rows,), jnp.float32),
            jax.ShapeDtypeStruct((rows, width), jnp.float32),
        ),
        compiler_params=params(),
        name="finish",
    )(embeddings, run, *lows, *highs, line)


def local(embeddings, positive, pairing):
    rows, width = embeddings.shape
    members = lax.axis_size("mem")
    groups = lax.axis_size("grp")
    block = rows * members
    rounds = pairing.shape[0]
    group = lax.axis_index("grp")
    member = lax.axis_index("mem")
    half = rows // 2

    def shift(value, by):
        return lax.ppermute(value, "mem", [(m, (m + by) % members) for m in range(members)])

    def swap(value):
        return lax.ppermute(value, "mem", [(m, m ^ 1) for m in range(members)])

    left, right = shift(embeddings, 2), shift(embeddings, -2)
    far = (shift(left[:half], 2), shift(right[half:], -2))
    per = rows * width // (groups * 128)
    tiles = embeddings.reshape(rows // 8, 8, width // 128, 128).transpose(0, 2, 1, 3)
    pieces = lax.all_to_all(tiles.reshape(groups, per, 128), "grp", 0, 0, tiled=True)
    ready = prepare("prepare", left, right)
    picked, ready = lax.optimization_barrier((pick(pairing, pieces), ready))
    got = lax.all_to_all(picked, "grp", 0, 0, tiled=True)
    sib, pos_sib = swap(embeddings), swap(positive)

    both = jnp.concatenate([positive, pos_sib]) - group * block
    owner = both // rows
    turn = (owner // 2 - member // 2) % (members // 2)
    order = jnp.where(turn == 0, SELF, jnp.where(turn == 3, 0, jnp.where(turn == 1, 1, 3)))
    pos = jnp.where(owner % 2 == member % 2, order * rows + both % rows, -1).reshape(1, 2 * rows)

    ready_far = prepare("prepare_far", embeddings, *far)
    c_own, e_own, line = own_scores(ready, ready_far, embeddings, sib, pos)
    got, line, partners = lax.optimization_barrier((got, line, pairing[:, group]))
    e_part, c_part, line = forward(ready, ready_far, line, got, swap(got), members)

    everything = lax.all_to_all(line, "mem", 0, 0, tiled=True)
    row_den, own_den, line, spread = denominators(jnp.reshape(member, (1,)), everything, groups)
    everyone = lax.all_to_all(spread, "grp", 0, 0, tiled=True)

    shared = (partners, row_den, own_den, everyone, pos, e_own, e_part)
    cols, far_low, far_high = backward(((3, 0, rows),), 2, *shared, c_own, c_part)
    shared += (cols,)
    far_low, far_high = shift(far_low, 2), shift(far_high, -2)
    bands = ((0, 0, rows), (1, 0, rows))
    left_low, left_high, right_low, right_high = backward(bands, 4, *shared)
    high0, low1 = shift(right_high, 2), shift(left_low, -2)
    right_low, left_high = add_pairs(right_low, far_low, left_high, far_high)
    low0, high1 = shift(right_low, 2), shift(left_high, -2)
    (run,) = backward(((SELF, 0, rows),), 1, *shared)
    return finish(embeddings, run, (low0, low1), (high0, high1), line)


def solution(mesh):
    placed = (P(("grp", "mem"), None), P(("grp", "mem")), P())
    return jax.shard_map(
        local,
        mesh=mesh,
        in_specs=placed,
        out_specs=(P(("grp", "mem")), P(("grp", "mem"), None)),
        check_vma=False,
    )
```
